32 devices in a mesh: view: 4 (over y, x), strip: 8 (over z, core).
Axes of the slice: x: 2, y: 2, z: 4, core: 2. Of those that a mesh axis runs over, the one named last changes fastest.
Arguments:
- means: float32 [3, 16384], P(None, 'strip'), may hold values from -4 to 4
- inv_scales: float32 [2, 16384], P(None, 'strip'), may hold values from 0.15 to 0.6
- correlation: float32 [16384], P('strip'), may hold values from -0.6 to 0.6
- opacity: float32 [16384], P('strip'), may hold values from -7 to 4
- features: float32 [16384, 128], P('strip'), may hold values from -48 to 48
- cameras: float32 [4, 2, 4], P('view'), may hold values from -0.8 to 0.8
- owners: int32 [4, 8, 256, 1], P('view', 'strip'), may hold values from 0 to 7; in each aligned block of 256 rows (0 to 255, 256 to 511, ..., all dimensions but the last counted through in order) at most 64 rows name the same one
- slots: int32 [4, 8, 256], P('view', 'strip'), may hold values from 0 to 2047
- lengths: int32 [4, 8], P('view', 'strip'), may hold values from 1 to 256, 1280 in all within a row
- target: float32 [4, 128, 16, 128], P('view', 'strip'), may hold values from -6 to 6
- weights: float32 [3, 3, 128, 128], replicated, may hold values from -0.1875 to 0.1875
- bias: float32 [128], replicated, may hold values from -3 to 3
Outputs:
- geometry_grad: float32 [7, 16384], P(None, 'strip')
- feature_grad: float32 [16384, 128], P('strip')
- weight_grad: float32 [3, 3, 128, 128], replicated
- bias_grad: float32 [128], replicated
The draws below stay inside these ranges and needn't reach their ends.
Inputs may be any that keep to these rules, and one draw needn't show every extreme that they name: `owners`: in one device's entries (aligned blocks of 256 list entries in order of view, tile and position), no strip index is named more than 64 times; entries at or past a tile's length are padding but still name a primitive.
All inputs are finite; a program needn't handle non-finite values. No bound on the sum of `lengths` on one device may be relied on, other than what follows from the above.
Results may differ from the reference program's by a relative error of at most 0.0003.
Values sent between devices are 32-bit elements; how exact they have to be, the bound alone decides.
No kernel may reach another device: no remote copies, remote signals or barrier semaphores. Data moves between devices by JAX's collectives and lax.ppermute only.
A program may use at most 64 MiB of HBM per device.

```python
import math
import jax
import jax.numpy as jnp
import numpy as np
from jax import lax

CH = 128
CAP = 256
TILES_DEV = 1
P_DEV = 2048
VIEWS = 4
TILES = 8
PRIMS = 16384
IMG_ROWS = 128
IMG_COLS = 16
BUCKET = 64
N_STRIP = 8


def with_ends(array, key, low, high):
    longest = array.shape.index(max(array.shape))
    spots = []
    for shift in (0, 1):
        where = [jax.random.randint(jax.random.fold_in(key, axis), (), 0, length) for axis, length in enumerate(array.shape)]
        where[longest] = (where[longest] + shift) % array.shape[longest]
        spots.append(tuple(where))
    return array.at[spots[0]].set(low).at[spots[1]].set(high)


def block_scale(key, extent, cuts, smallest, high):
    def one(dim, parts):
        heights = jax.random.uniform(jax.random.fold_in(jax.random.fold_in(key, 6), dim), (parts,), jnp.float32, smallest / len(cuts), high / len(cuts))
        return jnp.repeat(jnp.exp(heights), extent[dim] // parts).reshape((-1,) + (1,) * (len(extent) - dim - 1))

    loudness = one(*cuts[0])
    for cut in cuts[1:]:
        loudness = loudness * one(*cut)
    return loudness


def length_profile(amount, total, most, skew):
    weights = [(1 << 20) // math.isqrt(standing ** skew) + 1 for standing in range(2, amount + 1)]
    rest, holding = total - most - (amount - 1), [1] * (amount - 1)
    while rest > 0:
        free = [i for i in range(amount - 1) if holding[i] < most]
        mass, remaining = sum([weights[i] for i in free]), rest
        for i in free:
            addition = min(most - holding[i], max(1, remaining * weights[i] // mass), rest)
            holding[i] = holding[i] + addition
            rest = rest - addition
    return np.array([most] + holding)


def ragged_sizes(stream_key, count, total, bound, slope):
    if count == 2:
        one = jax.random.randint(stream_key, (), max(1, total - bound), min(bound, total - 1) + 1)
        return jnp.stack([one, total - one])
    sizes = jnp.asarray(length_profile(count, total, bound, slope), jnp.int32)
    couples = (count - 1) // 2
    source_of, receiver = sizes[1:1 + 2 * couples:2], sizes[2:2 + 2 * couples:2]
    room = jnp.minimum(source_of - 1, bound - receiver)
    passed = jax.random.randint(jax.random.fold_in(stream_key, 1), (couples,), 0, 1 << 20) % (room + 1)
    sizes = sizes.at[1:1 + 2 * couples:2].set(source_of - passed).at[2:2 + 2 * couples:2].set(receiver + passed)
    return sizes[jax.random.permutation(jax.random.fold_in(stream_key, 2), count)]


def deal_out(key, own, number, rows, number_of, top, reach, lean):
    ranking = jax.random.permutation(key, number_of)
    crowded, usual = portions_of(number_of, rows * top, reach, lean, True), portions_of(number_of, rows * top, reach, lean, False)
    places = jnp.arange(number_of)

    def named(tallies, turn):
        used = int((tallies > 0).sum())
        fixed = max(1, used // 4)
        passed = fixed + (places - fixed + turn * (used - fixed)) % max(1, number_of - fixed)
        return jnp.zeros((number_of,), jnp.int32).at[ranking[jnp.where(places < fixed, places, passed)]].set(jnp.asarray(tallies, jnp.int32))

    tallies = jnp.where(number % 4 == 0, named(crowded, number // 4), named(usual, number - number // 4 - 1))
    mixed = jax.random.permutation(jax.random.fold_in(own, 3), number_of)
    donor, sink = mixed[0:number_of // 2 * 2:2], mixed[1:number_of // 2 * 2:2]
    slack = jnp.minimum(tallies[donor] - 1, reach - tallies[sink]) // 2
    slack = jnp.where((donor == ranking[0]) | (sink == ranking[0]) | (tallies[sink] == 0), 0, jnp.maximum(slack, 0))
    passed = jax.random.randint(jax.random.fold_in(own, 4), (number_of // 2,), 0, 1 << 20) % (slack + 1)
    tallies = tallies.at[donor].add(-passed).at[sink].add(passed)
    labels = jnp.searchsorted(jnp.cumsum(tallies), jnp.arange(rows * top), side="right").astype(jnp.int32)
    listing = labels.reshape(top, rows).T
    listing = listing[jax.random.permutation(jax.random.fold_in(own, 1), rows)]
    turn = jax.random.randint(jax.random.fold_in(own, 2), (rows, 1), 0, top)
    return jnp.take_along_axis(listing, (jnp.arange(top)[None, :] + turn) % top, axis=1)


def portions_of(count, total, bound, lean, full):
    weights = [(1 << 20) // math.isqrt(grade ** lean) + 1 for grade in range(1, count + 1)]
    largest = bound if full else min(bound, max(-(-total // count), total * weights[0] // sum(weights)))
    least = 1 if total - largest >= count - 1 else 0
    given, spare = [largest] + [least] * (count - 1), total - largest - least * (count - 1)
    while spare > 0:
        free = [i for i in range(1, count) if given[i] < largest] or [i for i in range(1, count) if given[i] < bound]
        mass, budget = sum([weights[i] for i in free]), spare
        for i in free:
            extra = min(bound - given[i], max(1, budget * weights[i] // mass), spare)
            given[i] = given[i] + extra
            spare = spare - extra
    return np.array(given)


def bell_draw(rng, extent, width, bound, pieces=(), kind=jnp.bfloat16):
    level = block_scale(rng, extent, pieces, -0.22, 0.18) if pieces else 1.0
    drawn = jax.random.normal(rng, extent, jnp.float32) * width * level
    return jnp.minimum(jnp.maximum(drawn, -bound), bound).astype(kind)


def setup_inputs(seed: int = 0) -> dict:
    key_list = jax.random.split(jax.random.key(seed), 13)
    means = bell_draw(key_list[0], (3, PRIMS), 1.0, 4.0, ((1, 8),), jnp.float32)
    inv_scales = jnp.clip(jnp.exp(math.log(0.6) - 1.3862944 * jax.random.uniform(key_list[1], (2, PRIMS), jnp.float32) ** block_scale(key_list[1], (2, PRIMS), ((1, 8),), -0.2, 0.2)), 0.15, 0.6)
    correlation = jnp.clip(jax.random.uniform(key_list[2], (PRIMS,), jnp.float32, -0.6, 0.6) * block_scale(key_list[2], (PRIMS,), ((0, 8),), -0.4, 0.0), -0.6, 0.6)
    opacity = jnp.clip(-7.0 + 11.0 * jax.random.uniform(key_list[3], (PRIMS,), jnp.float32) ** block_scale(key_list[3], (PRIMS,), ((0, 8),), -0.2, 0.2), -7.0, 4.0)
    features = bell_draw(key_list[4], (PRIMS, CH), 8.0, 48.0, ((0, 8),), jnp.float32)
    cameras = jnp.clip(jax.random.uniform(key_list[5], (VIEWS, 2, 4), jnp.float32, -0.8, 0.8) * block_scale(key_list[5], (VIEWS, 2, 4), ((0, 4),), -0.4, 0.0), -0.8, 0.8)
    owners_keys = jax.random.split(jax.random.fold_in(key_list[6], 1), VIEWS * TILES * CAP // (TILES_DEV * CAP))
    owners_turns = jax.random.permutation(jax.random.fold_in(key_list[6], 3), VIEWS * TILES * CAP // (TILES_DEV * CAP))
    owners = jax.vmap(lambda own, number: deal_out(jax.random.fold_in(key_list[6], 2), own, number, TILES_DEV * CAP, N_STRIP, 1, BUCKET, 2))(owners_keys, owners_turns).reshape((VIEWS, TILES, CAP, 1))
    slots = with_ends(jax.random.randint(key_list[7], (VIEWS, TILES, CAP), 0, P_DEV), jax.random.fold_in(key_list[7], 1), 0, P_DEV - 1).astype(jnp.int32)
    lengths = jax.vmap(lambda own: ragged_sizes(own, TILES, (TILES * CAP * 5) // 8, CAP, 2))(jax.random.split(key_list[8], VIEWS)).reshape((VIEWS, TILES)).astype(jnp.int32)
    target = bell_draw(key_list[9], (VIEWS, IMG_ROWS, IMG_COLS, CH), 1.0, 6.0, ((0, 4), (1, 8)), jnp.float32)
    weights = bell_draw(key_list[10], (3, 3, CH, CH), (9 * CH) ** -0.5, 0.1875, (), jnp.float32)
    bias = bell_draw(key_list[11], (CH,), 0.5, 3.0, (), jnp.float32)
    return dict(means=means, inv_scales=inv_scales, correlation=correlation, opacity=opacity, features=features, cameras=cameras, owners=owners, slots=slots, lengths=lengths, target=target, weights=weights, bias=bias)


HIGHEST = lax.Precision.HIGHEST

def render_tile(geometry, feature, length, camera):
    entries = geometry.shape[0]
    pixels = jnp.arange(256, dtype=jnp.int32)
    across = (pixels % 16).astype(jnp.float32) + 0.5
    downward = (pixels // 16).astype(jnp.float32) + 0.5
    center_col = 8.0 + 4.0 * (camera[0, 0] * geometry[:, 0] + camera[0, 1] * geometry[:, 1] + camera[0, 2] * geometry[:, 2] + camera[0, 3])
    center_row = 8.0 + 4.0 * (camera[1, 0] * geometry[:, 0] + camera[1, 1] * geometry[:, 1] + camera[1, 2] * geometry[:, 2] + camera[1, 3])
    scaled_col = geometry[:, 3][None, :] * (across[:, None] - center_col[None, :])
    scaled_row = geometry[:, 4][None, :] * (downward[:, None] - center_row[None, :])
    exponent = -0.5 * (scaled_col * scaled_col + 2.0 * geometry[:, 5][None, :] * scaled_col * scaled_row + scaled_row * scaled_row)
    alive_mask = (jnp.arange(entries, dtype=jnp.int32) < length).astype(jnp.float32)
    coverage = jnp.minimum(jax.nn.sigmoid(geometry[:, 6])[None, :] * jnp.exp(exponent), 0.99) * alive_mask[None, :]
    log_keep = jnp.log1p(-coverage)
    transmit = jnp.exp(jnp.cumsum(log_keep, axis=1) - log_keep)
    return jnp.dot(coverage * transmit, feature, precision=HIGHEST)

def convolve(padded, kernel, height, breadth):
    channels = padded.shape[-1]
    total = jnp.zeros((height * breadth, kernel.shape[-1]), jnp.float32)
    for tap_row in range(3):
        for tap_col in range(3):
            piece = padded[tap_row:tap_row + height, tap_col:tap_col + breadth].reshape(height * breadth, channels)
            total = total + jnp.dot(piece, kernel[tap_row, tap_col], precision=HIGHEST)
    return total

def reference(means, inv_scales, correlation, opacity, features, cameras, owners, slots, lengths, target, weights, bias):
    table = jnp.concatenate([means, inv_scales, correlation[None, :], opacity[None, :]], axis=0).T
    index = owners[..., 0] * P_DEV + slots
    height = target.shape[1]
    breadth = target.shape[2]
    channels = target.shape[3]
    geometry_total = jnp.zeros(table.shape, jnp.float32)
    feature_total = jnp.zeros(features.shape, jnp.float32)
    kernel_total = jnp.zeros(weights.shape, jnp.float32)
    bias_total = jnp.zeros(bias.shape, jnp.float32)
    flipped = jnp.transpose(weights[::-1, ::-1], (0, 1, 3, 2))
    for view in range(VIEWS):
        picked = index[view]
        geometry = table[picked]
        feature = features[picked]
        camera = cameras[view]
        view_lengths = lengths[view]

        def render_all(geometry, feature):

            def single(packed):
                return render_tile(packed[0], packed[1], packed[2], camera)
            return lax.map(jax.checkpoint(single), (geometry, feature, view_lengths))
        tiles, pullback = jax.vjp(render_all, geometry, feature)
        image = tiles.reshape(N_STRIP, TILES_DEV, 16, 16, channels).transpose(0, 2, 1, 3, 4).reshape(height, breadth, channels)
        padded = jnp.pad(image, ((1, 1), (1, 1), (0, 0)))
        decoded = convolve(padded, weights, height, breadth) + bias[None, :]
        residual = decoded - target[view].reshape(height * breadth, channels)
        tap_terms = []
        for tap_row in range(3):
            for tap_col in range(3):
                piece = padded[tap_row:tap_row + height, tap_col:tap_col + breadth].reshape(height * breadth, channels)
                tap_terms.append(jnp.dot(piece.T, residual, precision=HIGHEST))
        kernel_total = kernel_total + jnp.stack(tap_terms).reshape(3, 3, channels, channels)
        bias_total = bias_total + lax.optimization_barrier(jnp.sum(residual, axis=0))
        beside_all = jnp.pad(residual.reshape(height, breadth, channels), ((1, 1), (1, 1), (0, 0)))
        image_grad = convolve(beside_all, flipped, height, breadth)
        tile_grad = image_grad.reshape(N_STRIP, 16, TILES_DEV, 16, channels).transpose(0, 2, 1, 3, 4).reshape(TILES, 256, channels)
        geometry_grad, feature_grad = pullback(tile_grad)
        flat_index = picked.reshape(-1)
        geometry_total = geometry_total.at[flat_index].add(geometry_grad.reshape(-1, 7))
        feature_total = feature_total.at[flat_index].add(feature_grad.reshape(-1, channels))
    return (geometry_total.T, feature_total, kernel_total, bias_total)
```

```python
import functools

import jax
import jax.numpy as jnp
from jax import lax
from jax.experimental import pallas as pl
from jax.experimental.pallas import tpu as pltpu
from jax.sharding import PartitionSpec as P

HIGHEST = lax.Precision.HIGHEST
F32 = jnp.float32
BF16 = jnp.bfloat16
LANES = 128
WIDTH = 16
VMEM = pl.BlockSpec(memory_space=pltpu.VMEM)
SMEM = pl.BlockSpec(memory_space=pltpu.SMEM)


def iota(shape, dim):
    return lax.broadcasted_iota(jnp.int32, shape, dim)


def onehot(mask):
    return jnp.where(mask, 1.0, 0.0).astype(BF16)


def split2(x):
    high = x.astype(BF16)
    return high, (x - high.astype(F32)).astype(BF16)


def split3(x):
    high = x.astype(BF16)
    rest = x - high.astype(F32)
    middle = rest.astype(BF16)
    return high, middle, (rest - middle.astype(F32)).astype(BF16)


def dot(a, b):
    return jnp.dot(a, b, preferred_element_type=F32)


def dot_nt(a, b):
    return lax.dot_general(a, b, (((1,), (1,)), ((), ())), preferred_element_type=F32)


def call(kernel, out_shape, in_specs, scratch=(), flops=0, moved=0):
    return pl.pallas_call(
        kernel,
        out_shape=out_shape,
        in_specs=in_specs,
        out_specs=jax.tree.map(lambda _: VMEM, out_shape),
        scratch_shapes=list(scratch),
        compiler_params=pltpu.CompilerParams(vmem_limit_bytes=48 * 2**20),
        cost_estimate=pl.CostEstimate(flops=flops, bytes_accessed=moved, transcendentals=0),
    )


def route_kernel(bucket, rows, owner_ref, slot_ref, request_ref, pos_row_ref, pos_col_ref):
    groups = request_ref.shape[0]
    count = owner_ref.shape[1]
    owner_row = owner_ref[...].astype(F32)
    down, across = iota((count, count), 0), iota((count, count), 1)
    owner_col = jnp.sum(jnp.where(down == across, owner_row, 0.0), axis=1, keepdims=True)
    same = owner_col == owner_row
    rank_row = jnp.sum(jnp.where(same & (down < across), 1.0, 0.0), axis=0, keepdims=True)
    rank_col = jnp.sum(jnp.where(same & (across < down), 1.0, 0.0), axis=1, keepdims=True)
    pos_row = (owner_row * bucket + rank_row).astype(jnp.int32)
    pos_col = (owner_col * bucket + rank_col).astype(jnp.int32)
    pos_row_ref[...] = pos_row
    pos_col_ref[...] = pos_col
    shift = rows.bit_length() - 1
    left = jnp.where(
        iota((groups, count), 0) == lax.shift_right_logical(pos_row, shift),
        slot_ref[...].astype(F32),
        0.0,
    )
    right = jnp.where(iota((count, LANES), 1) == (pos_col & (rows - 1)), 1.0, 0.0)
    wanted = jnp.dot(left, right, precision=HIGHEST, preferred_element_type=F32)
    for group in range(groups):
        request_ref[group] = wanted[group : group + 1]


def reply_kernel(
    rows,
    asked_ref,
    means_ref,
    scales_ref,
    correlation_ref,
    opacity_ref,
    feature_ref,
    reply_ref,
    table_ref,
    pick_ref,
    half_ref,
):
    groups = asked_ref.shape[0]
    owned = feature_ref.shape[0]
    channels = feature_ref.shape[1]
    blocks = owned // LANES
    feature = feature_ref[...]
    high, low = split2(feature)
    half_ref[:, :channels] = high
    half_ref[:, channels:] = low
    asked = jnp.concatenate([asked_ref[group] for group in range(groups)], axis=0)
    padded = jnp.concatenate([asked, jnp.zeros((LANES - groups, LANES), F32)], axis=0)
    columns = padded.T.astype(jnp.int32)
    place = iota((rows, owned), 1)
    for group in range(groups):
        pick_ref[group * rows : (group + 1) * rows] = onehot(
            columns[:rows, group : group + 1] == place
        )
    found = dot(pick_ref[...], half_ref[...])
    found = found[:, :channels] + found[:, channels:]

    table_ref[0:3] = means_ref[...]
    table_ref[3:5] = scales_ref[...]
    table_ref[5:6] = correlation_ref[...]
    table_ref[6:7] = opacity_ref[...]
    table_ref[7:8] = jnp.zeros((1, owned), F32)
    table = table_ref[...]
    stacked = jnp.concatenate(
        [table[:, a * LANES : (a + 1) * LANES] for a in range(blocks)], axis=0
    )
    parts = jnp.concatenate(split3(stacked), axis=0)
    slots = asked.astype(jnp.int32)
    slots_row = jnp.concatenate([slots[group : group + 1] for group in range(groups)], axis=1)
    wide = slots_row.shape[1]
    minor = onehot((slots_row & (LANES - 1)) == iota((LANES, wide), 0))
    product = dot(parts, minor)
    deep = blocks * 8
    product = product[:deep] + product[deep : 2 * deep] + product[2 * deep :]
    major = lax.shift_right_logical(slots_row, 7)
    geometry = jnp.zeros((8, wide), F32)
    for a in range(blocks):
        geometry = geometry + jnp.where(major == a, product[a * 8 : (a + 1) * 8], 0.0)
    for group in range(groups):
        reply_ref[group, 0:rows] = found[group * rows : (group + 1) * rows]
        reply_ref[group, rows : rows + 8] = geometry[:, group * LANES : (group + 1) * LANES]


def weights_kernel(weights_ref, straight_ref, turned_ref):
    size = weights_ref.shape[2]
    for i in range(3):
        for j in range(3):
            block = weights_ref[i, j]
            high, low = split2(block)
            straight_ref[i, j * size : (j + 1) * size, :size] = high
            straight_ref[i, j * size : (j + 1) * size, size:] = low
            high, low = split2(block.T)
            a, b = 2 - i, 2 - j
            turned_ref[a, b * size : (b + 1) * size, :size] = high
            turned_ref[a, b * size : (b + 1) * size, size:] = low


def centers(camera_ref, geometry):
    found = []
    for axis in range(2):
        found.append(
            8.0
            + 4.0
            * (
                camera_ref[axis, 0] * geometry[0:1]
                + camera_ref[axis, 1] * geometry[1:2]
                + camera_ref[axis, 2] * geometry[2:3]
                + camera_ref[axis, 3]
            )
        )
    return found


def offsets(camera_ref, geometry, pixels):
    center_col, center_row = centers(camera_ref, geometry)
    pixel = iota((pixels, geometry.shape[1]), 0)
    across = (pixel & (WIDTH - 1)).astype(F32) + 0.5
    downward = lax.shift_right_logical(pixel, WIDTH.bit_length() - 1).astype(F32) + 0.5
    return across - center_col, downward - center_row


def render_kernel(
    rows,
    camera_ref,
    length_ref,
    fetched_ref,
    pos_row_ref,
    pos_col_ref,
    target_ref,
    tile_ref,
    send_up_ref,
    send_down_ref,
    weight_ref,
    ratio_ref,
    geometry_ref,
    feature_ref,
):
    groups = fetched_ref.shape[0]
    count = pos_row_ref.shape[1]
    places = groups * rows
    pixels, channels = tile_ref.shape
    pick = onehot(pos_col_ref[...] == iota((count, places), 1))
    pick_t = onehot(pos_row_ref[...] == iota((places, count), 0))
    sent = jnp.concatenate([fetched_ref[group, 0:rows] for group in range(groups)], axis=0)
    feature = dot(pick, jnp.concatenate(split2(sent), axis=1)).astype(BF16)
    feature_ref[...] = feature
    sent = jnp.concatenate(
        [fetched_ref[group, rows : rows + 8][:, :rows] for group in range(groups)], axis=1
    )
    geometry = dot(jnp.concatenate(split3(sent), axis=0), pick_t)
    geometry = geometry[0:8] + geometry[8:16] + geometry[16:24]
    geometry_ref[...] = geometry
    du, dv = offsets(camera_ref, geometry, pixels)
    a = geometry[3:4] * du
    b = geometry[4:5] * dv
    exponent = -0.5 * (a * a + 2.0 * geometry[5:6] * a * b + b * b)
    alive = iota((1, count), 1) < length_ref[0, 0]
    sigmoid = 1.0 / (1.0 + jnp.exp(-geometry[6:7]))
    raw = sigmoid * jnp.exp(exponent)
    alpha = jnp.where(alive, jnp.minimum(raw, 0.99), 0.0)
    keep = 1.0 - alpha
    log_keep = jnp.log(keep)
    before = onehot(iota((count, count), 0) < iota((count, count), 1))
    high, low = split2(log_keep)
    weight = alpha * jnp.exp(dot(high, before) + dot(low, before))
    weight_ref[...] = weight
    ratio_ref[...] = jnp.where(raw < 0.99, alpha, 0.0) / keep
    high, low = split2(weight)
    tile = dot(high, feature)
    tile = tile[:, :channels] + tile[:, channels:] + dot(low, feature[:, :channels])
    tile_ref[...] = tile
    send_up_ref[0 : 2 * WIDTH] = tile[0 : 2 * WIDTH]
    send_up_ref[2 * WIDTH :] = target_ref[0:WIDTH]
    send_down_ref[0 : 2 * WIDTH] = tile[pixels - 2 * WIDTH :]
    send_down_ref[2 * WIDTH :] = target_ref[pixels - WIDTH : pixels]


def spread_kernel(pos_row_ref, weight_ref, spread_ref):
    places = spread_ref.shape[0]
    pixels, count = weight_ref.shape
    pick_t = onehot(pos_row_ref[...] == iota((places, count), 0))
    high, low = split2(weight_ref[...])
    spread_ref[:, :pixels] = dot_nt(pick_t, high).astype(BF16)
    spread_ref[:, pixels:] = dot_nt(pick_t, low).astype(BF16)


def shifted(value, scratch_ref):
    count = value.shape[0]
    scratch_ref[8 : 8 + count] = value
    column = iota((count, 1), 0) & (WIDTH - 1)
    left = jnp.where(column == 0, 0.0, scratch_ref[7 : 7 + count])
    right = jnp.where(column == WIDTH - 1, 0.0, scratch_ref[9 : 9 + count])
    return jnp.concatenate([left, value, right], axis=1)


def taps(wide, kernel_ref, count, channels):
    high, low = split2(wide)
    total = jnp.zeros((count, channels), F32)
    for i in range(3):
        part = dot(high[WIDTH * i : WIDTH * i + count], kernel_ref[i])
        total = total + part[:, :channels] + part[:, channels:]
        total = total + dot(low[WIDTH * i : WIDTH * i + count], kernel_ref[i][:, :channels])
    return total


def decode_kernel(
    place_ref,
    tile_ref,
    above_ref,
    below_ref,
    target_ref,
    kernel_ref,
    bias_ref,
    residual_ref,
    keep_ref,
    send_ref,
    scratch_ref,
    sum_ref,
):
    pixels, channels = tile_ref.shape
    edge = 2 * WIDTH
    scratch_ref[0:8] = jnp.zeros((8, channels), F32)
    padded = jnp.concatenate([above_ref[0:edge], tile_ref[...], below_ref[0:edge]], axis=0)
    count = pixels + 2 * WIDTH
    scratch_ref[8 + count + 2 * WIDTH : 16 + count + 2 * WIDTH] = jnp.zeros((8, channels), F32)
    wide = shifted(padded, scratch_ref)
    goal = jnp.concatenate([above_ref[edge:], target_ref[...], below_ref[edge:]], axis=0)
    residual = taps(wide, kernel_ref, count, channels) + bias_ref[...] - goal
    pixel = iota((count, 1), 0)
    outside = ((pixel < WIDTH) & (place_ref[0] == 1)) | (
        (pixel >= count - WIDTH) & (place_ref[1] == 1)
    )
    residual = jnp.where(outside, 0.0, residual)
    residual_ref[...] = residual

    own = residual[WIDTH : WIDTH + pixels]
    turned_high, turned_low = split2(own.T)
    high, low = split2(wide)
    for i in range(3):
        first = WIDTH * (1 + i)
        part = (
            dot(turned_high, high[first : first + pixels])
            + dot(turned_high, low[first : first + pixels])
            + dot(turned_low, high[first : first + pixels])
        )
        for j in range(3):
            block = (3 * i + j) * channels
            sum_ref[block : block + channels] = part[:, j * channels : (j + 1) * channels].T
    block = 9 * channels
    sum_ref[block:] = jnp.zeros((sum_ref.shape[0] - block, channels), F32)
    sum_ref[block : block + 1] = jnp.sum(own, axis=0, keepdims=True)
    half = keep_ref.shape[0]

    @pl.when(place_ref[2] == 0)
    def _():
        keep_ref[...] = sum_ref[0:half]
        send_ref[...] = sum_ref[half:]

    @pl.when(place_ref[2] == 1)
    def _():
        keep_ref[...] = sum_ref[half:]
        send_ref[...] = sum_ref[0:half]


def back_kernel(
    rows,
    camera_ref,
    residual_ref,
    kernel_ref,
    weight_ref,
    ratio_ref,
    geometry_ref,
    feature_ref,
    spread_ref,
    pos_col_ref,
    slot_ref,
    back_ref,
    scratch_ref,
):
    groups = back_ref.shape[0]
    pixels, count = weight_ref.shape
    channels = residual_ref.shape[1]
    places = groups * rows
    extent = residual_ref.shape[0]
    scratch_ref[0:8] = jnp.zeros((8, channels), F32)
    scratch_ref[8 + extent : 16 + extent] = jnp.zeros((8, channels), F32)
    wide = shifted(residual_ref[...], scratch_ref)
    grad = taps(wide, kernel_ref, pixels, channels)
    high, low = split2(grad)
    both = jnp.concatenate([high, low], axis=1)
    part = dot(spread_ref[:, :pixels], both)
    part = part[:, :channels] + part[:, channels:] + dot(spread_ref[:, pixels:], high)
    for group in range(groups):
        back_ref[group, 0:rows] = part[group * rows : (group + 1) * rows]

    near, far = feature_ref[:, :channels], feature_ref[:, channels:]
    weight_grad = dot_nt(high, near) + dot_nt(high, far) + dot_nt(low, near)
    pull = weight_grad * weight_ref[...]
    behind = onehot(iota((count, count), 0) > iota((count, count), 1))
    high, low = split2(pull)
    suffix = dot(high, behind) + dot(low, behind)
    ratio = ratio_ref[...]
    change = jnp.where(ratio > 0.0, pull - ratio * suffix, 0.0)

    geometry = geometry_ref[...]
    du, dv = offsets(camera_ref, geometry, pixels)

    def total(x):
        return jnp.sum(x, axis=0, keepdims=True)

    change_u, change_v = change * du, change * dv
    m, mu, mv = total(change), total(change_u), total(change_v)
    muu, muv, mvv = total(change_u * du), total(change_u * dv), total(change_v * dv)
    g3, g4, g5, g6 = (geometry[i : i + 1] for i in range(3, 7))
    center_col = g3 * (g3 * mu + g5 * g4 * mv)
    center_row = g4 * (g5 * g3 * mu + g4 * mv)
    lines = [
        4.0 * (camera_ref[0, i] * center_col + camera_ref[1, i] * center_row) for i in range(3)
    ]
    lines.append(-(g3 * muu + g5 * g4 * muv))
    lines.append(-(g4 * mvv + g5 * g3 * muv))
    lines.append(-(g3 * g4 * muv))
    lines.append(m / (1.0 + jnp.exp(g6)))
    lines.append(slot_ref[...].astype(F32))
    pick = onehot(pos_col_ref[...] == iota((count, places), 1))
    moved = dot(jnp.concatenate(split3(jnp.concatenate(lines, axis=0)), axis=0), pick)
    moved = moved[0:8] + moved[8:16] + moved[16:24]
    for group in range(groups):
        piece = moved[:, group * rows : (group + 1) * rows]
        if rows < LANES:
            piece = jnp.concatenate([piece, jnp.zeros((8, LANES - rows), F32)], axis=1)
        back_ref[group, rows : rows + 8] = piece


def gather_kernel(rows, arrived_ref, geometry_ref, feature_ref, half_ref):
    pieces = arrived_ref.shape[0]
    owned, channels = feature_ref.shape
    blocks = owned // LANES
    lines = []
    for piece in range(pieces):
        high, low = split2(arrived_ref[piece, 0:rows])
        half_ref[piece * rows : (piece + 1) * rows, :channels] = high
        half_ref[piece * rows : (piece + 1) * rows, channels:] = low
        lines.append(arrived_ref[piece, rows : rows + 8][:, :rows])
    lines = jnp.concatenate(lines, axis=1)
    amount = pieces * rows
    slot_row = lines[7:8].astype(jnp.int32)
    tile = 256
    for first in range(0, owned, tile):
        pick_t = onehot(slot_row == iota((tile, amount), 0) + first)
        part = dot(pick_t, half_ref[...])
        feature_ref[first : first + tile] = part[:, :channels] + part[:, channels:]
    minor = onehot((slot_row & (LANES - 1)) == iota((LANES, amount), 0))
    major = lax.shift_right_logical(slot_row, 7)
    stacked = jnp.concatenate([jnp.where(major == a, lines, 0.0) for a in range(blocks)], axis=0)
    high, low = split2(stacked)
    product = dot_nt(high, minor) + dot_nt(low, minor)
    for a in range(blocks):
        geometry_ref[:, a * LANES : (a + 1) * LANES] = product[a * 8 : a * 8 + 7]


def scatter_sum_kernel(place_ref, mine_ref, other_ref, *out_refs):
    parts = len(out_refs)
    rows = mine_ref.shape[0] // parts
    view = place_ref[3]
    for m in range(parts):
        start = pl.multiple_of((view ^ m) * rows, 8)
        out_refs[m][...] = mine_ref[pl.ds(start, rows)] + other_ref[pl.ds(start, rows)]


def sum_kernel(*refs):
    total = refs[0][...]
    for ref in refs[1:-1]:
        total = total + ref[...]
    refs[-1][...] = total


def join_kernel(place_ref, *refs):
    parts = len(refs) - 1
    rows = refs[0].shape[0]
    view = place_ref[3]
    for m in range(parts):
        start = pl.multiple_of((view ^ m) * rows, 8)
        refs[-1][pl.ds(start, rows)] = refs[m][...]


def finish_kernel(place_ref, mine_ref, other_ref, kernel_ref, bias_ref, sum_ref):
    half = mine_ref.shape[0]
    size = kernel_ref.shape[0]

    @pl.when(place_ref[2] == 0)
    def _():
        sum_ref[0:half] = mine_ref[...]
        sum_ref[half:] = other_ref[...]

    @pl.when(place_ref[2] == 1)
    def _():
        sum_ref[0:half] = other_ref[...]
        sum_ref[half:] = mine_ref[...]

    kernel_ref[...] = sum_ref[0:size]
    bias_ref[...] = sum_ref[size : size + 1]


def swap(value, axis, mask):
    count = lax.axis_size(axis)
    return lax.ppermute(value, axis, [(i, i ^ mask) for i in range(count)])


def decoder_sum(place, keep, send, views, strips):
    shape = jax.ShapeDtypeStruct
    half, channels = keep.shape
    rows = half // views
    part = shape((rows, channels), F32)
    other = swap(send, "strip", 1)
    parts = call(scatter_sum_kernel, [part] * views, [SMEM, VMEM, VMEM])(place, keep, other)
    parts = [parts[0]] + [swap(parts[m], "view", m) for m in range(1, views)]
    total = call(sum_kernel, part, [VMEM] * len(parts))(*parts)
    chips = strips // 2
    step = 1
    while chips > 1:
        near = 4 if chips % 4 == 0 else 2
        parts = [total] + [swap(total, "strip", 2 * step * m) for m in range(1, near)]
        total = call(sum_kernel, part, [VMEM] * len(parts))(*parts)
        step, chips = step * near, chips // near
    parts = [total] + [swap(total, "view", m) for m in range(1, views)]
    joined = call(join_kernel, shape((half, channels), F32), [SMEM] + [VMEM] * views)(place, *parts)
    other = swap(joined, "strip", 1)
    return call(
        finish_kernel,
        [shape((9 * channels, channels), F32), shape((1, channels), F32)],
        [SMEM, VMEM, VMEM],
        [pltpu.VMEM((2 * half, channels), F32)],
    )(place, joined, other)


def per_device(
    means,
    inv_scales,
    correlation,
    opacity,
    features,
    cameras,
    owners,
    slots,
    lengths,
    target,
    weights,
    bias,
):
    shape = jax.ShapeDtypeStruct
    strips = lax.axis_size("strip")
    views = lax.axis_size("view")
    count = slots.shape[1] * slots.shape[2]
    owned, channels = features.shape
    height, breadth = target.shape[1], target.shape[2]
    pixels = height * breadth
    assert slots.shape[1] == 1 and breadth == WIDTH and channels == LANES
    bucket = max(4, 2 * count // strips)
    places = strips * bucket
    rows = bucket if bucket % 8 == 0 else 64
    groups = places // rows
    direct = rows == bucket
    lead = rows + 8
    wire_lead = bucket + 8

    def to_wire(value):
        if direct:
            return value
        top = value[:, :rows].reshape(strips, bucket, LANES)
        low = value[:, rows:, :rows].transpose(1, 0, 2).reshape(8, strips, bucket)
        low = jnp.pad(low.transpose(1, 0, 2), ((0, 0), (0, 0), (0, LANES - bucket)))
        return jnp.concatenate([top, low], axis=1)

    def from_wire(value):
        if direct:
            return value
        top = value[:, :bucket].reshape(groups, rows, LANES)
        low = value[:, bucket:, :bucket].transpose(1, 0, 2).reshape(8, groups, rows)
        low = jnp.pad(low.transpose(1, 0, 2), ((0, 0), (0, 0), (0, LANES - rows)))
        return jnp.concatenate([top, low], axis=1)

    def exchange(value):
        return lax.all_to_all(value, "strip", split_axis=0, concat_axis=0, tiled=True)

    view, strip = lax.axis_index("view"), lax.axis_index("strip")
    place = jnp.stack([strip == 0, strip == strips - 1, strip % 2, view]).astype(jnp.int32)
    camera = cameras[0]
    slot_row = slots.reshape(1, count)
    goal = target.reshape(pixels, channels)

    request, pos_row, pos_col = call(
        functools.partial(route_kernel, bucket, rows),
        [
            shape((groups, 1, LANES), F32),
            shape((1, count), jnp.int32),
            shape((count, 1), jnp.int32),
        ],
        [VMEM] * 2,
    )(owners.reshape(1, count), slot_row)
    if not direct:
        request = request[:, 0, :rows].reshape(strips, 1, bucket)
        request = jnp.pad(request, ((0, 0), (0, 0), (0, LANES - bucket)))
    asked = exchange(request)
    if not direct:
        asked = asked[:, 0, :bucket].reshape(groups, 1, rows)
        asked = jnp.pad(asked, ((0, 0), (0, 0), (0, LANES - rows)))

    straight, turned = call(
        weights_kernel, [shape((3, 3 * channels, 2 * channels), BF16)] * 2, [VMEM], moved=2**21
    )(weights)

    reply = call(
        functools.partial(reply_kernel, rows),
        shape((groups, lead, LANES), F32),
        [VMEM] * 6,
        [
            pltpu.VMEM((8, owned), F32),
            pltpu.VMEM((places, owned), BF16),
            pltpu.VMEM((owned, 2 * channels), BF16),
        ],
    )(asked, means, inv_scales, correlation[None, :], opacity[None, :], features)
    fetched = from_wire(exchange(to_wire(reply)))

    tile, send_up, send_down, weight, ratio, geometry, feature = call(
        functools.partial(render_kernel, rows),
        [
            shape((pixels, channels), F32),
            shape((3 * WIDTH, channels), F32),
            shape((3 * WIDTH, channels), F32),
            shape((pixels, count), F32),
            shape((pixels, count), F32),
            shape((8, count), F32),
            shape((count, 2 * channels), BF16),
        ],
        [SMEM, SMEM] + [VMEM] * 4,
    )(camera, lengths, fetched, pos_row, pos_col, goal)
    above = lax.ppermute(send_down, "strip", [(i, i + 1) for i in range(strips - 1)])
    below = lax.ppermute(send_up, "strip", [(i + 1, i) for i in range(strips - 1)])
    spread = call(
        spread_kernel, shape((places, 2 * pixels), BF16), [VMEM] * 2, moved=2**21
    )(pos_row, weight)

    unit = 16 * views
    padded_rows = -(-(9 * channels + 1) // unit) * unit
    half = padded_rows // 2
    residual, keep, send = call(
        decode_kernel,
        [
            shape((pixels + 2 * WIDTH, channels), F32),
            shape((half, channels), F32),
            shape((half, channels), F32),
        ],
        [SMEM] + [VMEM] * 6,
        [
            pltpu.VMEM((pixels + 4 * WIDTH + 16, channels), F32),
            pltpu.VMEM((padded_rows, channels), F32),
        ],
    )(place, tile, above, below, goal, straight, bias[None, :])

    back = call(
        functools.partial(back_kernel, rows),
        shape((groups, lead, LANES), F32),
        [SMEM] + [VMEM] * 9,
        [pltpu.VMEM((pixels + 2 * WIDTH + 16, channels), F32)],
        flops=2**30,
        moved=2**22,
    )(camera, residual, turned, weight, ratio, geometry, feature, spread, pos_col, slot_row)
    returned = from_wire(exchange(to_wire(back)))
    copies = jnp.broadcast_to(returned[None], (views,) + returned.shape)
    arrived = lax.all_to_all(copies, "view", split_axis=0, concat_axis=0, tiled=True)
    arrived = arrived.reshape(views * groups, lead, LANES)
    geometry_grad, feature_grad = call(
        functools.partial(gather_kernel, rows),
        [shape((7, owned), F32), shape((owned, channels), F32)],
        [VMEM],
        [pltpu.VMEM((views * places, 2 * channels), BF16)],
        flops=2**32,
        moved=2**23,
    )(arrived)

    kernel_grad, bias_grad = decoder_sum(place, keep, send, views, strips)
    return (
        geometry_grad,
        feature_grad,
        kernel_grad.reshape(weights.shape),
        bias_grad.reshape(bias.shape),
    )


def solution(mesh):
    return jax.shard_map(
        per_device,
        mesh=mesh,
        in_specs=(
            P(None, "strip"),
            P(None, "strip"),
            P("strip"),
            P("strip"),
            P("strip", None),
            P("view", None, None),
            P("view", "strip", None, None),
            P("view", "strip", None),
            P("view", "strip"),
            P("view", "strip", None, None),
            P(),
            P(),
        ),
        out_specs=(P(None, "strip"), P("strip", None), P(), P()),
        check_vma=False,
    )
```

```python
import functools

import jax
import jax.numpy as jnp
from jax import lax
from jax.experimental import pallas as pl
from jax.experimental.pallas import tpu as pltpu
from jax.sharding import PartitionSpec as P

HIGHEST = lax.Precision.HIGHEST
F32 = jnp.float32
BF16 = jnp.bfloat16
LANES = 128
WIDTH = 16
VMEM = pl.BlockSpec(memory_space=pltpu.VMEM)
SMEM = pl.BlockSpec(memory_space=pltpu.SMEM)
ANY = pl.BlockSpec(memory_space=pl.ANY)
HBM = pl.BlockSpec(memory_space=pltpu.HBM)


def iota(shape, dim):
    return lax.broadcasted_iota(jnp.int32, shape, dim)


def onehot(mask):
    return jnp.where(mask, 1.0, 0.0).astype(BF16)


def split2(x):
    high = x.astype(BF16)
    return high, (x - high.astype(F32)).astype(BF16)


def split3(x):
    high = x.astype(BF16)
    rest = x - high.astype(F32)
    middle = rest.astype(BF16)
    return high, middle, (rest - middle.astype(F32)).astype(BF16)


def dot(a, b):
    return jnp.dot(a, b, preferred_element_type=F32)


def dot_nt(a, b):
    return lax.dot_general(a, b, (((1,), (1,)), ((), ())), preferred_element_type=F32)


def call(kernel, out_shape, in_specs, scratch=(), flops=0, moved=0, out=VMEM):
    return pl.pallas_call(
        kernel,
        out_shape=out_shape,
        in_specs=in_specs,
        out_specs=jax.tree.map(lambda _: out, out_shape),
        scratch_shapes=list(scratch),
        compiler_params=pltpu.CompilerParams(vmem_limit_bytes=48 * 2**20),
        cost_estimate=pl.CostEstimate(flops=flops, bytes_accessed=moved, transcendentals=0),
    )


def route_kernel(
    bucket,
    rows,
    owner_hbm,
    slot_hbm,
    request_ref,
    pos_row_ref,
    pos_col_ref,
    slot_copy_ref,
    owner_ref,
    slot_ref,
    sems,
):
    copies = [
        pltpu.make_async_copy(owner_hbm, owner_ref, sems.at[0]),
        pltpu.make_async_copy(slot_hbm, slot_ref, sems.at[1]),
    ]
    for copy in copies:
        copy.start()
    for copy in copies:
        copy.wait()
    slot_copy_ref[...] = slot_ref[...]
    groups = request_ref.shape[0]
    count = owner_ref.shape[1]
    owner_row = owner_ref[...].astype(F32)
    down, across = iota((count, count), 0), iota((count, count), 1)
    owner_col = jnp.sum(jnp.where(down == across, owner_row, 0.0), axis=1, keepdims=True)
    same = owner_col == owner_row
    rank_row = jnp.sum(jnp.where(same & (down < across), 1.0, 0.0), axis=0, keepdims=True)
    rank_col = jnp.sum(jnp.where(same & (across < down), 1.0, 0.0), axis=1, keepdims=True)
    pos_row = (owner_row * bucket + rank_row).astype(jnp.int32)
    pos_col = (owner_col * bucket + rank_col).astype(jnp.int32)
    pos_row_ref[...] = pos_row
    pos_col_ref[...] = pos_col
    shift = rows.bit_length() - 1
    left = jnp.where(
        iota((groups, count), 0) == lax.shift_right_logical(pos_row, shift),
        slot_ref[...].astype(F32),
        0.0,
    )
    right = jnp.where(iota((count, LANES), 1) == (pos_col & (rows - 1)), 1.0, 0.0)
    wanted = jnp.dot(left, right, precision=HIGHEST, preferred_element_type=F32)
    for group in range(groups):
        request_ref[group] = wanted[group : group + 1]


def prepare_kernel(
    token_ref,
    means_hbm,
    scales_hbm,
    correlation_hbm,
    opacity_hbm,
    feature_hbm,
    weights_hbm,
    half_ref,
    parts_ref,
    straight_ref,
    turned_ref,
    table_ref,
    correlation_ref,
    opacity_ref,
    means_ref,
    scales_ref,
    feature_ref,
    weights_ref,
    sems,
):
    copies = [
        pltpu.make_async_copy(source, goal, sems.at[i])
        for i, (source, goal) in enumerate(
            [
                (feature_hbm, feature_ref),
                (weights_hbm, weights_ref),
                (means_hbm, means_ref),
                (scales_hbm, scales_ref),
                (correlation_hbm, correlation_ref),
                (opacity_hbm, opacity_ref),
            ]
        )
    ]
    for copy in copies:
        copy.start()
    for copy in copies:
        copy.wait()
    owned, channels = feature_ref.shape
    blocks = owned // LANES
    high, low = split2(feature_ref[...])
    half_ref[:, :channels] = high
    half_ref[:, channels:] = low
    table_ref[0:3] = means_ref[...]
    table_ref[3:5] = scales_ref[...]
    table_ref[5:6] = correlation_ref[...]
    table_ref[6:7] = opacity_ref[...]
    table_ref[7:8] = jnp.zeros((1, owned), F32)
    table = table_ref[...]
    stacked = jnp.concatenate(
        [table[:, a * LANES : (a + 1) * LANES] for a in range(blocks)], axis=0
    )
    parts_ref[...] = jnp.concatenate(split3(stacked), axis=0)
    size = weights_ref.shape[2]
    for i in range(3):
        for j in range(3):
            block = weights_ref[i, j]
            high, low = split2(block)
            straight_ref[i, j * size : (j + 1) * size, :size] = high
            straight_ref[i, j * size : (j + 1) * size, size:] = low
            high, low = split2(block.T)
            a, b = 2 - i, 2 - j
            turned_ref[a, b * size : (b + 1) * size, :size] = high
            turned_ref[a, b * size : (b + 1) * size, size:] = low


def reply_kernel(rows, asked_ref, half_ref, parts_ref, reply_ref, pick_ref):
    groups = asked_ref.shape[0]
    owned = half_ref.shape[0]
    channels = half_ref.shape[1] // 2
    blocks = owned // LANES
    asked = jnp.concatenate([asked_ref[group] for group in range(groups)], axis=0)
    padded = jnp.concatenate([asked, jnp.zeros((LANES - groups, LANES), F32)], axis=0)
    columns = padded.T.astype(jnp.int32)
    place = iota((rows, owned), 1)
    for group in range(groups):
        pick_ref[group * rows : (group + 1) * rows] = onehot(
            columns[:rows, group : group + 1] == place
        )
    found = dot(pick_ref[...], half_ref[...])
    found = found[:, :channels] + found[:, channels:]
    slots = asked.astype(jnp.int32)
    slots_row = jnp.concatenate([slots[group : group + 1] for group in range(groups)], axis=1)
    wide = slots_row.shape[1]
    minor = onehot((slots_row & (LANES - 1)) == iota((LANES, wide), 0))
    product = dot(parts_ref[...], minor)
    deep = blocks * 8
    product = product[:deep] + product[deep : 2 * deep] + product[2 * deep :]
    major = lax.shift_right_logical(slots_row, 7)
    geometry = jnp.zeros((8, wide), F32)
    for a in range(blocks):
        geometry = geometry + jnp.where(major == a, product[a * 8 : (a + 1) * 8], 0.0)
    for group in range(groups):
        reply_ref[group, 0:rows] = found[group * rows : (group + 1) * rows]
        reply_ref[group, rows : rows + 8] = geometry[:, group * LANES : (group + 1) * LANES]


def centers(camera_ref, geometry):
    found = []
    for axis in range(2):
        found.append(
            8.0
            + 4.0
            * (
                camera_ref[axis, 0] * geometry[0:1]
                + camera_ref[axis, 1] * geometry[1:2]
                + camera_ref[axis, 2] * geometry[2:3]
                + camera_ref[axis, 3]
            )
        )
    return found


def offsets(camera_ref, geometry, pixels):
    center_col, center_row = centers(camera_ref, geometry)
    pixel = iota((pixels, geometry.shape[1]), 0)
    across = (pixel & (WIDTH - 1)).astype(F32) + 0.5
    downward = lax.shift_right_logical(pixel, WIDTH.bit_length() - 1).astype(F32) + 0.5
    return across - center_col, downward - center_row


def render_kernel(
    rows,
    camera_ref,
    length_ref,
    fetched_ref,
    pos_row_ref,
    pos_col_ref,
    target_ref,
    tile_ref,
    send_up_ref,
    send_down_ref,
    weight_ref,
    ratio_ref,
    geometry_ref,
    feature_ref,
):
    groups = fetched_ref.shape[0]
    count = pos_row_ref.shape[1]
    places = groups * rows
    pixels, channels = tile_ref.shape
    pick = onehot(pos_col_ref[...] == iota((count, places), 1))
    pick_t = onehot(pos_row_ref[...] == iota((places, count), 0))
    sent = jnp.concatenate([fetched_ref[group, 0:rows] for group in range(groups)], axis=0)
    feature = dot(pick, jnp.concatenate(split2(sent), axis=1)).astype(BF16)
    feature_ref[...] = feature
    sent = jnp.concatenate(
        [fetched_ref[group, rows : rows + 8][:, :rows] for group in range(groups)], axis=1
    )
    geometry = dot(jnp.concatenate(split3(sent), axis=0), pick_t)
    geometry = geometry[0:8] + geometry[8:16] + geometry[16:24]
    geometry_ref[...] = geometry
    du, dv = offsets(camera_ref, geometry, pixels)
    a = geometry[3:4] * du
    b = geometry[4:5] * dv
    exponent = -0.5 * (a * a + 2.0 * geometry[5:6] * a * b + b * b)
    alive = iota((1, count), 1) < length_ref[0, 0]
    sigmoid = 1.0 / (1.0 + jnp.exp(-geometry[6:7]))
    raw = sigmoid * jnp.exp(exponent)
    alpha = jnp.where(alive, jnp.minimum(raw, 0.99), 0.0)
    keep = 1.0 - alpha
    log_keep = jnp.log(keep)
    before = onehot(iota((count, count), 0) < iota((count, count), 1))
    high, low = split2(log_keep)
    weight = alpha * jnp.exp(dot(high, before) + dot(low, before))
    weight_ref[...] = weight
    ratio_ref[...] = jnp.where(raw < 0.99, alpha, 0.0) / keep
    high, low = split2(weight)
    tile = dot(high, feature)
    tile = tile[:, :channels] + tile[:, channels:] + dot(low, feature[:, :channels])
    tile_ref[...] = tile
    send_up_ref[0 : 2 * WIDTH] = tile[0 : 2 * WIDTH]
    send_up_ref[2 * WIDTH :] = target_ref[0:WIDTH]
    send_down_ref[0 : 2 * WIDTH] = tile[pixels - 2 * WIDTH :]
    send_down_ref[2 * WIDTH :] = target_ref[pixels - WIDTH : pixels]


def spread_kernel(pos_row_ref, weight_ref, spread_ref):
    places = spread_ref.shape[0]
    pixels, count = weight_ref.shape
    pick_t = onehot(pos_row_ref[...] == iota((places, count), 0))
    high, low = split2(weight_ref[...])
    spread_ref[:, :pixels] = dot_nt(pick_t, high).astype(BF16)
    spread_ref[:, pixels:] = dot_nt(pick_t, low).astype(BF16)


def shifted(value, scratch_ref):
    count = value.shape[0]
    scratch_ref[8 : 8 + count] = value
    column = iota((count, 1), 0) & (WIDTH - 1)
    left = jnp.where(column == 0, 0.0, scratch_ref[7 : 7 + count])
    right = jnp.where(column == WIDTH - 1, 0.0, scratch_ref[9 : 9 + count])
    return jnp.concatenate([left, value, right], axis=1)


def taps(wide, kernel_ref, count, channels):
    high, low = split2(wide)
    total = jnp.zeros((count, channels), F32)
    for i in range(3):
        part = dot(high[WIDTH * i : WIDTH * i + count], kernel_ref[i])
        total = total + part[:, :channels] + part[:, channels:]
        total = total + dot(low[WIDTH * i : WIDTH * i + count], kernel_ref[i][:, :channels])
    return total


def decode_kernel(
    place_ref,
    tile_ref,
    above_ref,
    below_ref,
    target_ref,
    kernel_ref,
    bias_ref,
    residual_ref,
    keep_ref,
    send_ref,
    scratch_ref,
    sum_ref,
):
    pixels, channels = tile_ref.shape
    edge = 2 * WIDTH
    scratch_ref[0:8] = jnp.zeros((8, channels), F32)
    padded = jnp.concatenate([above_ref[0:edge], tile_ref[...], below_ref[0:edge]], axis=0)
    count = pixels + 2 * WIDTH
    scratch_ref[8 + count + 2 * WIDTH : 16 + count + 2 * WIDTH] = jnp.zeros((8, channels), F32)
    wide = shifted(padded, scratch_ref)
    goal = jnp.concatenate([above_ref[edge:], target_ref[...], below_ref[edge:]], axis=0)
    residual = taps(wide, kernel_ref, count, channels) + bias_ref[...] - goal
    pixel = iota((count, 1), 0)
    outside = ((pixel < WIDTH) & (place_ref[0] == 1)) | (
        (pixel >= count - WIDTH) & (place_ref[1] == 1)
    )
    residual = jnp.where(outside, 0.0, residual)
    residual_ref[...] = residual

    own = residual[WIDTH : WIDTH + pixels]
    turned_high, turned_low = split2(own.T)
    high, low = split2(wide)
    for i in range(3):
        first = WIDTH * (1 + i)
        part = (
            dot(turned_high, high[first : first + pixels])
            + dot(turned_high, low[first : first + pixels])
            + dot(turned_low, high[first : first + pixels])
        )
        for j in range(3):
            block = (3 * i + j) * channels
            sum_ref[block : block + channels] = part[:, j * channels : (j + 1) * channels].T
    block = 9 * channels
    sum_ref[block:] = jnp.zeros((sum_ref.shape[0] - block, channels), F32)
    sum_ref[block : block + 1] = jnp.sum(own, axis=0, keepdims=True)
    half = keep_ref.shape[0]

    @pl.when(place_ref[2] == 0)
    def _():
        keep_ref[...] = sum_ref[0:half]
        send_ref[...] = sum_ref[half:]

    @pl.when(place_ref[2] == 1)
    def _():
        keep_ref[...] = sum_ref[half:]
        send_ref[...] = sum_ref[0:half]


def back_kernel(
    rows,
    camera_ref,
    residual_ref,
    kernel_ref,
    weight_ref,
    ratio_ref,
    geometry_ref,
    feature_ref,
    spread_ref,
    pos_col_ref,
    slot_ref,
    back_ref,
    scratch_ref,
):
    groups = back_ref.shape[0]
    pixels, count = weight_ref.shape
    channels = residual_ref.shape[1]
    places = groups * rows
    extent = residual_ref.shape[0]
    scratch_ref[0:8] = jnp.zeros((8, channels), F32)
    scratch_ref[8 + extent : 16 + extent] = jnp.zeros((8, channels), F32)
    wide = shifted(residual_ref[...], scratch_ref)
    grad = taps(wide, kernel_ref, pixels, channels)
    high, low = split2(grad)
    both = jnp.concatenate([high, low], axis=1)
    part = dot(spread_ref[:, :pixels], both)
    part = part[:, :channels] + part[:, channels:] + dot(spread_ref[:, pixels:], high)
    for group in range(groups):
        back_ref[group, 0:rows] = part[group * rows : (group + 1) * rows]

    near, far = feature_ref[:, :channels], feature_ref[:, channels:]
    weight_grad = dot_nt(high, near) + dot_nt(high, far) + dot_nt(low, near)
    pull = weight_grad * weight_ref[...]
    behind = onehot(iota((count, count), 0) > iota((count, count), 1))
    high, low = split2(pull)
    suffix = dot(high, behind) + dot(low, behind)
    ratio = ratio_ref[...]
    change = jnp.where(ratio > 0.0, pull - ratio * suffix, 0.0)

    geometry = geometry_ref[...]
    du, dv = offsets(camera_ref, geometry, pixels)

    def total(x):
        return jnp.sum(x, axis=0, keepdims=True)

    change_u, change_v = change * du, change * dv
    m, mu, mv = total(change), total(change_u), total(change_v)
    muu, muv, mvv = total(change_u * du), total(change_u * dv), total(change_v * dv)
    g3, g4, g5, g6 = (geometry[i : i + 1] for i in range(3, 7))
    center_col = g3 * (g3 * mu + g5 * g4 * mv)
    center_row = g4 * (g5 * g3 * mu + g4 * mv)
    lines = [
        4.0 * (camera_ref[0, i] * center_col + camera_ref[1, i] * center_row) for i in range(3)
    ]
    lines.append(-(g3 * muu + g5 * g4 * muv))
    lines.append(-(g4 * mvv + g5 * g3 * muv))
    lines.append(-(g3 * g4 * muv))
    lines.append(m / (1.0 + jnp.exp(g6)))
    lines.append(slot_ref[...].astype(F32))
    pick = onehot(pos_col_ref[...] == iota((count, places), 1))
    moved = dot(jnp.concatenate(split3(jnp.concatenate(lines, axis=0)), axis=0), pick)
    moved = moved[0:8] + moved[8:16] + moved[16:24]
    for group in range(groups):
        piece = moved[:, group * rows : (group + 1) * rows]
        if rows < LANES:
            piece = jnp.concatenate([piece, jnp.zeros((8, LANES - rows), F32)], axis=1)
        back_ref[group, rows : rows + 8] = piece


def copies_kernel(token_ref, value_ref, copies_hbm, sems):
    copies = [
        pltpu.make_async_copy(value_ref, copies_hbm.at[i], sems.at[i])
        for i in range(copies_hbm.shape[0])
    ]
    for copy in copies:
        copy.start()
    for copy in copies:
        copy.wait()


def gather_kernel(rows, token_ref, arrived_ref, geometry_ref, feature_ref, half_ref):
    pieces = arrived_ref.shape[0]
    owned, channels = feature_ref.shape
    blocks = owned // LANES
    lines = []
    for piece in range(pieces):
        high, low = split2(arrived_ref[piece, 0:rows])
        half_ref[piece * rows : (piece + 1) * rows, :channels] = high
        half_ref[piece * rows : (piece + 1) * rows, channels:] = low
        lines.append(arrived_ref[piece, rows : rows + 8][:, :rows])
    lines = jnp.concatenate(lines, axis=1)
    amount = pieces * rows
    slot_row = lines[7:8].astype(jnp.int32)
    tile = 256
    for first in range(0, owned, tile):
        pick_t = onehot(slot_row == iota((tile, amount), 0) + first)
        part = dot(pick_t, half_ref[...])
        feature_ref[first : first + tile] = part[:, :channels] + part[:, channels:]
    minor = onehot((slot_row & (LANES - 1)) == iota((LANES, amount), 0))
    major = lax.shift_right_logical(slot_row, 7)
    stacked = jnp.concatenate([jnp.where(major == a, lines, 0.0) for a in range(blocks)], axis=0)
    high, low = split2(stacked)
    product = dot_nt(high, minor) + dot_nt(low, minor)
    for a in range(blocks):
        geometry_ref[:, a * LANES : (a + 1) * LANES] = product[a * 8 : a * 8 + 7]


def scatter_sum_kernel(place_ref, mine_ref, other_ref, *out_refs):
    parts = len(out_refs)
    rows = mine_ref.shape[0] // parts
    view = place_ref[3]
    for m in range(parts):
        start = pl.multiple_of((view ^ m) * rows, 8)
        out_refs[m][...] = mine_ref[pl.ds(start, rows)] + other_ref[pl.ds(start, rows)]


def sum_kernel(*refs):
    total = refs[0][...]
    for ref in refs[1:-1]:
        total = total + ref[...]
    refs[-1][...] = total


def join_kernel(place_ref, *refs):
    parts = len(refs) - 1
    rows = refs[0].shape[0]
    view = place_ref[3]
    for m in range(parts):
        start = pl.multiple_of((view ^ m) * rows, 8)
        refs[-1][pl.ds(start, rows)] = refs[m][...]


def finish_kernel(place_ref, mine_ref, other_ref, kernel_hbm, bias_hbm, sems):
    half = mine_ref.shape[0]
    size = kernel_hbm.shape[0]

    def move(first, second):
        copies = [
            pltpu.make_async_copy(first, kernel_hbm.at[0:half], sems.at[0]),
            pltpu.make_async_copy(
                second.at[0 : size - half], kernel_hbm.at[half:size], sems.at[1]
            ),
            pltpu.make_async_copy(second.at[size - half : size - half + 1], bias_hbm, sems.at[2]),
        ]
        for copy in copies:
            copy.start()
        for copy in copies:
            copy.wait()

    @pl.when(place_ref[2] == 0)
    def _():
        move(mine_ref, other_ref)

    @pl.when(place_ref[2] == 1)
    def _():
        move(other_ref, mine_ref)


def swap(value, axis, mask):
    count = lax.axis_size(axis)
    return lax.ppermute(value, axis, [(i, i ^ mask) for i in range(count)])


def near_sum(value, axis, unit, amount):
    step = unit
    while amount > 1:
        near = 4 if amount % 4 == 0 else 2
        parts = [value] + [swap(value, axis, step * m) for m in range(1, near)]
        value = call(sum_kernel, jax.ShapeDtypeStruct(value.shape, F32), [VMEM] * near)(*parts)
        step, amount = step * near, amount // near
    return value


def per_device(
    means,
    inv_scales,
    correlation,
    opacity,
    features,
    cameras,
    owners,
    slots,
    lengths,
    target,
    weights,
    bias,
):
    shape = jax.ShapeDtypeStruct
    strips = lax.axis_size("strip")
    views = lax.axis_size("view")
    count = slots.shape[1] * slots.shape[2]
    owned, channels = features.shape
    height, breadth = target.shape[1], target.shape[2]
    pixels = height * breadth
    assert slots.shape[1] == 1 and breadth == WIDTH and channels == LANES
    bucket = max(4, 2 * count // strips)
    places = strips * bucket
    rows = bucket if bucket % 8 == 0 else 64
    groups = places // rows
    direct = rows == bucket
    lead = rows + 8
    wire_lead = bucket + 8

    def to_wire(value):
        if direct:
            return value
        top = value[:, :rows].reshape(strips, bucket, LANES)
        low = value[:, rows:, :rows].transpose(1, 0, 2).reshape(8, strips, bucket)
        low = jnp.pad(low.transpose(1, 0, 2), ((0, 0), (0, 0), (0, LANES - bucket)))
        return jnp.concatenate([top, low], axis=1)

    def from_wire(value):
        if direct:
            return value
        top = value[:, :bucket].reshape(groups, rows, LANES)
        low = value[:, bucket:, :bucket].transpose(1, 0, 2).reshape(8, groups, rows)
        low = jnp.pad(low.transpose(1, 0, 2), ((0, 0), (0, 0), (0, LANES - rows)))
        return jnp.concatenate([top, low], axis=1)

    def exchange(value):
        return lax.all_to_all(value, "strip", split_axis=0, concat_axis=0, tiled=True)

    view, strip = lax.axis_index("view"), lax.axis_index("strip")
    place = jnp.stack([strip == 0, strip == strips - 1, strip % 2, view]).astype(jnp.int32)
    camera = cameras[0]
    goal = target.reshape(pixels, channels)

    request, pos_row, pos_col, slot_row = call(
        functools.partial(route_kernel, bucket, rows),
        [
            shape((groups, 1, LANES), F32),
            shape((1, count), jnp.int32),
            shape((count, 1), jnp.int32),
            shape((1, count), jnp.int32),
        ],
        [HBM] * 2,
        [pltpu.VMEM((1, count), jnp.int32)] * 2 + [pltpu.SemaphoreType.DMA((2,))],
    )(owners.reshape(1, count), slots.reshape(1, count))
    if not direct:
        request = request[:, 0, :rows].reshape(strips, 1, bucket)
        request = jnp.pad(request, ((0, 0), (0, 0), (0, LANES - bucket)))
    asked = exchange(request)
    if not direct:
        asked = asked[:, 0, :bucket].reshape(groups, 1, rows)
        asked = jnp.pad(asked, ((0, 0), (0, 0), (0, LANES - rows)))

    half, parts, straight, turned = call(
        prepare_kernel,
        [
            shape((owned, 2 * channels), BF16),
            shape((3 * 8 * (owned // LANES), LANES), BF16),
            shape((3, 3 * channels, 2 * channels), BF16),
            shape((3, 3 * channels, 2 * channels), BF16),
        ],
        [ANY] + [HBM] * 6,
        [
            pltpu.VMEM((8, owned), F32),
            pltpu.VMEM((1, owned), F32),
            pltpu.VMEM((1, owned), F32),
            pltpu.VMEM(means.shape, F32),
            pltpu.VMEM(inv_scales.shape, F32),
            pltpu.VMEM(features.shape, F32),
            pltpu.VMEM(weights.shape, F32),
            pltpu.SemaphoreType.DMA((6,)),
        ],
        flops=2**33,
        moved=2**24,
    )(pos_row, means, inv_scales, correlation[None, :], opacity[None, :], features, weights)

    reply = call(
        functools.partial(reply_kernel, rows),
        shape((groups, lead, LANES), F32),
        [VMEM] * 3,
        [pltpu.VMEM((places, owned), BF16)],
    )(asked, half, parts)
    fetched = from_wire(exchange(to_wire(reply)))

    tile, send_up, send_down, weight, ratio, geometry, feature = call(
        functools.partial(render_kernel, rows),
        [
            shape((pixels, channels), F32),
            shape((3 * WIDTH, channels), F32),
            shape((3 * WIDTH, channels), F32),
            shape((pixels, count), F32),
            shape((pixels, count), F32),
            shape((8, count), F32),
            shape((count, 2 * channels), BF16),
        ],
        [SMEM, SMEM] + [VMEM] * 4,
    )(camera, lengths, fetched, pos_row, pos_col, goal)
    above = lax.ppermute(send_down, "strip", [(i, i + 1) for i in range(strips - 1)])
    below = lax.ppermute(send_up, "strip", [(i + 1, i) for i in range(strips - 1)])
    spread = call(
        spread_kernel, shape((places, 2 * pixels), BF16), [VMEM] * 2, moved=2**21
    )(pos_row, weight)

    unit = 16 * views
    padded_rows = -(-(9 * channels + 1) // unit) * unit
    half = padded_rows // 2
    residual, keep, send = call(
        decode_kernel,
        [
            shape((pixels + 2 * WIDTH, channels), F32),
            shape((half, channels), F32),
            shape((half, channels), F32),
        ],
        [SMEM] + [VMEM] * 6,
        [
            pltpu.VMEM((pixels + 4 * WIDTH + 16, channels), F32),
            pltpu.VMEM((padded_rows, channels), F32),
        ],
    )(place, tile, above, below, goal, straight, bias[None, :])

    back = call(
        functools.partial(back_kernel, rows),
        shape((groups, lead, LANES), F32),
        [SMEM] + [VMEM] * 9,
        [pltpu.VMEM((pixels + 2 * WIDTH + 16, channels), F32)],
        flops=2**30,
        moved=2**22,
    )(camera, residual, turned, weight, ratio, geometry, feature, spread, pos_col, slot_row)
    returned = from_wire(exchange(to_wire(back)))

    piece = shape((half // views, channels), F32)
    other = swap(send, "strip", 1)
    parts = call(scatter_sum_kernel, [piece] * views, [SMEM, VMEM, VMEM])(place, keep, other)
    parts = [parts[0]] + [swap(parts[m], "view", m) for m in range(1, views)]
    part = call(sum_kernel, piece, [VMEM] * views)(*parts)

    copies = call(
        copies_kernel,
        shape((views, groups, lead, LANES), F32),
        [ANY, VMEM],
        [pltpu.SemaphoreType.DMA((views,))],
        out=HBM,
    )(part, returned)
    arrived = lax.all_to_all(copies, "view", split_axis=0, concat_axis=0, tiled=True)
    arrived = arrived.reshape(views * groups, lead, LANES)

    part = near_sum(part, "strip", 2, strips // 2)
    parts = [part] + [swap(part, "view", m) for m in range(1, views)]
    joined = call(join_kernel, shape((half, channels), F32), [SMEM] + [VMEM] * views)(place, *parts)

    geometry_grad, feature_grad = call(
        functools.partial(gather_kernel, rows),
        [shape((7, owned), F32), shape((owned, channels), F32)],
        [ANY, VMEM],
        [pltpu.VMEM((views * places, 2 * channels), BF16)],
        flops=2**32,
        moved=2**23,
    )(joined, arrived)

    other = swap(joined, "strip", 1)
    kernel_grad, bias_grad = call(
        finish_kernel,
        [shape((9 * channels, channels), F32), shape((1, channels), F32)],
        [SMEM, ANY, ANY],
        [pltpu.SemaphoreType.DMA((3,))],
        out=HBM,
    )(place, joined, other)
    return (
        geometry_grad,
        feature_grad,
        kernel_grad.reshape(weights.shape),
        bias_grad.reshape(bias.shape),
    )


def solution(mesh):
    return jax.shard_map(
        per_device,
        mesh=mesh,
        in_specs=(
            P(None, "strip"),
            P(None, "strip"),
            P("strip"),
            P("strip"),
            P("strip", None),
            P("view", None, None),
            P("view", "strip", None, None),
            P("view", "strip", None),
            P("view", "strip"),
            P("view", "strip", None, None),
            P(),
            P(),
        ),
        out_specs=(P(None, "strip"), P("strip", None), P(), P()),
        check_vma=False,
    )
```

```python
import functools

import jax
import jax.numpy as jnp
from jax import lax
from jax.experimental import pallas as pl
from jax.experimental.pallas import tpu as pltpu
from jax.sharding import PartitionSpec as P

HIGHEST = lax.Precision.HIGHEST
F32 = jnp.float32
BF16 = jnp.bfloat16
LANES = 128
WIDTH = 16
VMEM = pl.BlockSpec(memory_space=pltpu.VMEM)
SMEM = pl.BlockSpec(memory_space=pltpu.SMEM)
ANY = pl.BlockSpec(memory_space=pl.ANY)
HBM = pl.BlockSpec(memory_space=pltpu.HBM)


def iota(shape, dim):
    return lax.broadcasted_iota(jnp.int32, shape, dim)


def onehot(mask):
    return jnp.where(mask, 1.0, 0.0).astype(BF16)


def split2(x):
    high = x.astype(BF16)
    return high, (x - high.astype(F32)).astype(BF16)


def split3(x):
    high = x.astype(BF16)
    rest = x - high.astype(F32)
    middle = rest.astype(BF16)
    return high, middle, (rest - middle.astype(F32)).astype(BF16)


def dot(a, b):
    return jnp.dot(a, b, preferred_element_type=F32)


def dot_nt(a, b):
    return lax.dot_general(a, b, (((1,), (1,)), ((), ())), preferred_element_type=F32)


def call(kernel, out_shape, in_specs, scratch=(), flops=0, moved=0, out=VMEM):
    return pl.pallas_call(
        kernel,
        out_shape=out_shape,
        in_specs=in_specs,
        out_specs=jax.tree.map(lambda _: out, out_shape),
        scratch_shapes=list(scratch),
        compiler_params=pltpu.CompilerParams(vmem_limit_bytes=48 * 2**20),
        cost_estimate=pl.CostEstimate(flops=flops, bytes_accessed=moved, transcendentals=0),
    )


def route_kernel(
    bucket,
    rows,
    paired,
    owner_hbm,
    slot_hbm,
    request_ref,
    pos_row_ref,
    pos_col_ref,
    slot_copy_ref,
    owner_ref,
    slot_ref,
    sems,
):
    copies = [
        pltpu.make_async_copy(owner_hbm, owner_ref, sems.at[0]),
        pltpu.make_async_copy(slot_hbm, slot_ref, sems.at[1]),
    ]
    for copy in copies:
        copy.start()
    for copy in copies:
        copy.wait()
    slot_copy_ref[...] = slot_ref[...]
    groups = request_ref.shape[0]
    count = owner_ref.shape[1]
    owner_row = owner_ref[...].astype(F32)
    down, across = iota((count, count), 0), iota((count, count), 1)
    owner_col = jnp.sum(jnp.where(down == across, owner_row, 0.0), axis=1, keepdims=True)
    same = owner_col == owner_row
    rank_row = jnp.sum(jnp.where(same & (down < across), 1.0, 0.0), axis=0, keepdims=True)
    rank_col = jnp.sum(jnp.where(same & (across < down), 1.0, 0.0), axis=1, keepdims=True)
    pos_row = (owner_row * bucket + rank_row).astype(jnp.int32)
    pos_col = (owner_col * bucket + rank_col).astype(jnp.int32)
    mask = lax.axis_index("strip") * bucket if paired else 0
    pos_row_ref[...] = pos_row ^ mask
    pos_col_ref[...] = pos_col ^ mask
    shift = rows.bit_length() - 1
    left = jnp.where(
        iota((groups, count), 0) == lax.shift_right_logical(pos_row, shift),
        slot_ref[...].astype(F32),
        0.0,
    )
    right = jnp.where(iota((count, LANES), 1) == (pos_col & (rows - 1)), 1.0, 0.0)
    wanted = jnp.dot(left, right, precision=HIGHEST, preferred_element_type=F32)
    for group in range(groups):
        request_ref[group] = wanted[group : group + 1]


def prepare_kernel(
    token_ref,
    means_hbm,
    scales_hbm,
    correlation_hbm,
    opacity_hbm,
    feature_hbm,
    weights_hbm,
    half_ref,
    parts_ref,
    straight_ref,
    turned_ref,
    table_ref,
    correlation_ref,
    opacity_ref,
    means_ref,
    scales_ref,
    feature_ref,
    weights_ref,
    sems,
):
    copies = [
        pltpu.make_async_copy(source, goal, sems.at[i])
        for i, (source, goal) in enumerate(
            [
                (feature_hbm, feature_ref),
                (weights_hbm, weights_ref),
                (means_hbm, means_ref),
                (scales_hbm, scales_ref),
                (correlation_hbm, correlation_ref),
                (opacity_hbm, opacity_ref),
            ]
        )
    ]
    for copy in copies:
        copy.start()
    for copy in copies:
        copy.wait()
    owned, channels = feature_ref.shape
    blocks = owned // LANES
    high, low = split2(feature_ref[...])
    half_ref[:, :channels] = high
    half_ref[:, channels:] = low
    table_ref[0:3] = means_ref[...]
    table_ref[3:5] = scales_ref[...]
    table_ref[5:6] = correlation_ref[...]
    table_ref[6:7] = opacity_ref[...]
    table_ref[7:8] = jnp.zeros((1, owned), F32)
    table = table_ref[...]
    stacked = jnp.concatenate(
        [table[:, a * LANES : (a + 1) * LANES] for a in range(blocks)], axis=0
    )
    parts_ref[...] = jnp.concatenate(split3(stacked), axis=0)
    size = weights_ref.shape[2]
    for i in range(3):
        for j in range(3):
            block = weights_ref[i, j]
            high, low = split2(block)
            straight_ref[i, j * size : (j + 1) * size, :size] = high
            straight_ref[i, j * size : (j + 1) * size, size:] = low
            high, low = split2(block.T)
            a, b = 2 - i, 2 - j
            turned_ref[a, b * size : (b + 1) * size, :size] = high
            turned_ref[a, b * size : (b + 1) * size, size:] = low


def reply_kernel(rows, paired, asked_ref, half_ref, parts_ref, *refs):
    pick_ref = refs[-1]
    groups = asked_ref.shape[0]
    first = lax.axis_index("strip") if paired else 0
    replies = list(refs[:-1]) if paired else [refs[0].at[group] for group in range(groups)]
    owned = half_ref.shape[0]
    channels = half_ref.shape[1] // 2
    blocks = owned // LANES
    asked = jnp.concatenate([asked_ref[group ^ first] for group in range(groups)], axis=0)
    padded = jnp.concatenate([asked, jnp.zeros((LANES - groups, LANES), F32)], axis=0)
    columns = padded.T.astype(jnp.int32)
    place = iota((rows, owned), 1)
    for group in range(groups):
        pick_ref[group * rows : (group + 1) * rows] = onehot(
            columns[:rows, group : group + 1] == place
        )
    found = dot(pick_ref[...], half_ref[...])
    found = found[:, :channels] + found[:, channels:]
    slots = asked.astype(jnp.int32)
    slots_row = jnp.concatenate([slots[group : group + 1] for group in range(groups)], axis=1)
    wide = slots_row.shape[1]
    minor = onehot((slots_row & (LANES - 1)) == iota((LANES, wide), 0))
    product = dot(parts_ref[...], minor)
    deep = blocks * 8
    product = product[:deep] + product[deep : 2 * deep] + product[2 * deep :]
    major = lax.shift_right_logical(slots_row, 7)
    geometry = jnp.zeros((8, wide), F32)
    for a in range(blocks):
        geometry = geometry + jnp.where(major == a, product[a * 8 : (a + 1) * 8], 0.0)
    for group in range(groups):
        replies[group][0:rows] = found[group * rows : (group + 1) * rows]
        replies[group][rows : rows + 8] = geometry[:, group * LANES : (group + 1) * LANES]


def centers(camera_ref, geometry):
    found = []
    for axis in range(2):
        found.append(
            8.0
            + 4.0
            * (
                camera_ref[axis, 0] * geometry[0:1]
                + camera_ref[axis, 1] * geometry[1:2]
                + camera_ref[axis, 2] * geometry[2:3]
                + camera_ref[axis, 3]
            )
        )
    return found


def offsets(camera_ref, geometry, pixels):
    center_col, center_row = centers(camera_ref, geometry)
    pixel = iota((pixels, geometry.shape[1]), 0)
    across = (pixel & (WIDTH - 1)).astype(F32) + 0.5
    downward = lax.shift_right_logical(pixel, WIDTH.bit_length() - 1).astype(F32) + 0.5
    return across - center_col, downward - center_row


def render_kernel(
    rows,
    groups,
    paired,
    camera_ref,
    length_ref,
    pos_row_ref,
    pos_col_ref,
    target_ref,
    *refs,
):
    fetched = list(refs[:-7]) if paired else [refs[0].at[group] for group in range(groups)]
    tile_ref, send_near_ref, send_far_ref, weight_ref, ratio_ref, geometry_ref, feature_ref = refs[-7:]
    count = pos_row_ref.shape[1]
    places = groups * rows
    pixels, channels = tile_ref.shape
    pick = onehot(pos_col_ref[...] == iota((count, places), 1))
    pick_t = onehot(pos_row_ref[...] == iota((places, count), 0))
    sent = jnp.concatenate([fetched[group][0:rows] for group in range(groups)], axis=0)
    feature = dot(pick, jnp.concatenate(split2(sent), axis=1)).astype(BF16)
    feature_ref[...] = feature
    sent = jnp.concatenate(
        [fetched[group][rows : rows + 8][:, :rows] for group in range(groups)], axis=1
    )
    geometry = dot(jnp.concatenate(split3(sent), axis=0), pick_t)
    geometry = geometry[0:8] + geometry[8:16] + geometry[16:24]
    geometry_ref[...] = geometry
    du, dv = offsets(camera_ref, geometry, pixels)
    a = geometry[3:4] * du
    b = geometry[4:5] * dv
    exponent = -0.5 * (a * a + 2.0 * geometry[5:6] * a * b + b * b)
    alive = iota((1, count), 1) < length_ref[0, 0]
    sigmoid = 1.0 / (1.0 + jnp.exp(-geometry[6:7]))
    raw = sigmoid * jnp.exp(exponent)
    alpha = jnp.where(alive, jnp.minimum(raw, 0.99), 0.0)
    keep = 1.0 - alpha
    log_keep = jnp.log(keep)
    before = onehot(iota((count, count), 0) < iota((count, count), 1))
    high, low = split2(log_keep)
    weight = alpha * jnp.exp(dot(high, before) + dot(low, before))
    weight_ref[...] = weight
    ratio_ref[...] = jnp.where(raw < 0.99, alpha, 0.0) / keep
    high, low = split2(weight)
    tile = dot(high, feature)
    tile = tile[:, :channels] + tile[:, channels:] + dot(low, feature[:, :channels])
    tile_ref[...] = tile
    top = jnp.concatenate([tile[0 : 2 * WIDTH], target_ref[0:WIDTH]], axis=0)
    bottom = jnp.concatenate([tile[pixels - 2 * WIDTH :], target_ref[pixels - WIDTH : pixels]], axis=0)
    even = lax.axis_index("strip") % 2 == 0
    send_near_ref[...] = jnp.where(even, bottom, top)
    send_far_ref[...] = jnp.where(even, top, bottom)


def spread_kernel(pos_row_ref, weight_ref, spread_ref):
    places = spread_ref.shape[0]
    pixels, count = weight_ref.shape
    pick_t = onehot(pos_row_ref[...] == iota((places, count), 0))
    high, low = split2(weight_ref[...])
    spread_ref[:, :pixels] = dot_nt(pick_t, high).astype(BF16)
    spread_ref[:, pixels:] = dot_nt(pick_t, low).astype(BF16)


def shifted(value, scratch_ref):
    count = value.shape[0]
    scratch_ref[8 : 8 + count] = value
    column = iota((count, 1), 0) & (WIDTH - 1)
    left = jnp.where(column == 0, 0.0, scratch_ref[7 : 7 + count])
    right = jnp.where(column == WIDTH - 1, 0.0, scratch_ref[9 : 9 + count])
    return jnp.concatenate([left, value, right], axis=1)


def taps(wide, kernel_ref, count, channels):
    high, low = split2(wide)
    total = jnp.zeros((count, channels), F32)
    for i in range(3):
        part = dot(high[WIDTH * i : WIDTH * i + count], kernel_ref[i])
        total = total + part[:, :channels] + part[:, channels:]
        total = total + dot(low[WIDTH * i : WIDTH * i + count], kernel_ref[i][:, :channels])
    return total


def decode(tile_ref, near_ref, far_ref, target_ref, kernel_ref, bias_ref, scratch_ref, sum_ref):
    pixels, channels = tile_ref.shape
    edge = 2 * WIDTH
    strip = lax.axis_index("strip")
    even = strip % 2 == 0
    near, far = near_ref[...], far_ref[...]
    above, below = jnp.where(even, far, near), jnp.where(even, near, far)
    scratch_ref[0:8] = jnp.zeros((8, channels), F32)
    padded = jnp.concatenate([above[0:edge], tile_ref[...], below[0:edge]], axis=0)
    count = pixels + 2 * WIDTH
    scratch_ref[8 + count + 2 * WIDTH : 16 + count + 2 * WIDTH] = jnp.zeros((8, channels), F32)
    wide = shifted(padded, scratch_ref)
    goal = jnp.concatenate([above[edge:], target_ref[...], below[edge:]], axis=0)
    residual = taps(wide, kernel_ref, count, channels) + bias_ref[...] - goal
    pixel = iota((count, 1), 0)
    outside = ((pixel < WIDTH) & (strip == 0)) | (
        (pixel >= count - WIDTH) & (strip == lax.axis_size("strip") - 1)
    )
    residual = jnp.where(outside, 0.0, residual)

    own = residual[WIDTH : WIDTH + pixels]
    turned_high, turned_low = split2(own.T)
    high, low = split2(wide)
    for i in range(3):
        first = WIDTH * (1 + i)
        part = (
            dot(turned_high, high[first : first + pixels])
            + dot(turned_high, low[first : first + pixels])
            + dot(turned_low, high[first : first + pixels])
        )
        for j in range(3):
            block = (3 * i + j) * channels
            sum_ref[block : block + channels] = part[:, j * channels : (j + 1) * channels].T
    block = 9 * channels
    sum_ref[block:] = jnp.zeros((sum_ref.shape[0] - block, channels), F32)
    sum_ref[block : block + 1] = jnp.sum(own, axis=0, keepdims=True)
    return residual


def back_kernel(
    rows,
    groups,
    paired,
    camera_ref,
    tile_ref,
    near_ref,
    far_ref,
    target_ref,
    straight_ref,
    bias_ref,
    turned_ref,
    weight_ref,
    ratio_ref,
    geometry_ref,
    feature_ref,
    spread_ref,
    pos_col_ref,
    slot_ref,
    same_ref,
    cross_ref,
    keep_ref,
    scratch_ref,
    sum_ref,
):
    pixels, count = weight_ref.shape
    channels = tile_ref.shape[1]
    places = groups * rows
    lead = rows + 8
    half = keep_ref.shape[0]
    residual = decode(
        tile_ref, near_ref, far_ref, target_ref, straight_ref, bias_ref, scratch_ref, sum_ref
    )
    start = cross_ref.shape[0] - half
    even = lax.axis_index("strip") % 2 == 0
    keep_ref[...] = jnp.where(even, sum_ref[0:half], sum_ref[half:])
    cross_ref[start:] = jnp.where(even, sum_ref[half:], sum_ref[0:half])

    def put(group, first, value):
        amount = value.shape[0]
        if not paired:
            same_ref[group, first : first + amount] = value
        elif group % 2 == 0:
            same_ref[group // 2, first : first + amount] = value
        else:
            first = group // 2 * lead + first
            cross_ref[first : first + amount] = value

    extent = residual.shape[0]
    scratch_ref[8 + extent : 16 + extent] = jnp.zeros((8, channels), F32)
    wide = shifted(residual, scratch_ref)
    grad = taps(wide, turned_ref, pixels, channels)
    high, low = split2(grad)
    both = jnp.concatenate([high, low], axis=1)
    part = dot(spread_ref[:, :pixels], both)
    part = part[:, :channels] + part[:, channels:] + dot(spread_ref[:, pixels:], high)
    for group in range(groups):
        put(group, 0, part[group * rows : (group + 1) * rows])

    near, far = feature_ref[:, :channels], feature_ref[:, channels:]
    weight_grad = dot_nt(high, near) + dot_nt(high, far) + dot_nt(low, near)
    pull = weight_grad * weight_ref[...]
    behind = onehot(iota((count, count), 0) > iota((count, count), 1))
    high, low = split2(pull)
    suffix = dot(high, behind) + dot(low, behind)
    ratio = ratio_ref[...]
    change = jnp.where(ratio > 0.0, pull - ratio * suffix, 0.0)

    geometry = geometry_ref[...]
    du, dv = offsets(camera_ref, geometry, pixels)

    def total(x):
        return jnp.sum(x, axis=0, keepdims=True)

    change_u, change_v = change * du, change * dv
    m, mu, mv = total(change), total(change_u), total(change_v)
    muu, muv, mvv = total(change_u * du), total(change_u * dv), total(change_v * dv)
    g3, g4, g5, g6 = (geometry[i : i + 1] for i in range(3, 7))
    center_col = g3 * (g3 * mu + g5 * g4 * mv)
    center_row = g4 * (g5 * g3 * mu + g4 * mv)
    lines = [
        4.0 * (camera_ref[0, i] * center_col + camera_ref[1, i] * center_row) for i in range(3)
    ]
    lines.append(-(g3 * muu + g5 * g4 * muv))
    lines.append(-(g4 * mvv + g5 * g3 * muv))
    lines.append(-(g3 * g4 * muv))
    lines.append(m / (1.0 + jnp.exp(g6)))
    lines.append(slot_ref[...].astype(F32))
    pick = onehot(pos_col_ref[...] == iota((count, places), 1))
    moved = dot(jnp.concatenate(split3(jnp.concatenate(lines, axis=0)), axis=0), pick)
    moved = moved[0:8] + moved[8:16] + moved[16:24]
    for group in range(groups):
        piece = moved[:, group * rows : (group + 1) * rows]
        if rows < LANES:
            piece = jnp.concatenate([piece, jnp.zeros((8, LANES - rows), F32)], axis=1)
        put(group, rows, piece)


def copies_kernel(token_ref, *refs):
    values, copies_ref, sems = refs[:-2], refs[-2], refs[-1]
    rows = values[0].shape[0]
    copies = [
        pltpu.make_async_copy(
            value, copies_ref.at[view, place * rows : (place + 1) * rows], sems.at[view, place]
        )
        for view in range(copies_ref.shape[0])
        for place, value in enumerate(values)
    ]
    for copy in copies:
        copy.start()
    for copy in copies:
        copy.wait()


def gather_kernel(rows, token_ref, arrived_ref, geometry_ref, feature_ref, half_ref):
    pieces = arrived_ref.shape[0]
    owned, channels = feature_ref.shape
    blocks = owned // LANES
    lines = []
    for piece in range(pieces):
        high, low = split2(arrived_ref[piece, 0:rows])
        half_ref[piece * rows : (piece + 1) * rows, :channels] = high
        half_ref[piece * rows : (piece + 1) * rows, channels:] = low
        lines.append(arrived_ref[piece, rows : rows + 8][:, :rows])
    lines = jnp.concatenate(lines, axis=1)
    amount = pieces * rows
    slot_row = lines[7:8].astype(jnp.int32)
    tile = 256
    for first in range(0, owned, tile):
        pick_t = onehot(slot_row == iota((tile, amount), 0) + first)
        part = dot(pick_t, half_ref[...])
        feature_ref[first : first + tile] = part[:, :channels] + part[:, channels:]
    minor = onehot((slot_row & (LANES - 1)) == iota((LANES, amount), 0))
    major = lax.shift_right_logical(slot_row, 7)
    stacked = jnp.concatenate([jnp.where(major == a, lines, 0.0) for a in range(blocks)], axis=0)
    high, low = split2(stacked)
    product = dot_nt(high, minor) + dot_nt(low, minor)
    for a in range(blocks):
        geometry_ref[:, a * LANES : (a + 1) * LANES] = product[a * 8 : a * 8 + 7]


def mix_kernel(pieces, same_ref, keep_ref, other_ref, *out_refs):
    parts = len(out_refs) - pieces
    rows = keep_ref.shape[0] // parts
    start = other_ref.shape[0] - keep_ref.shape[0]
    for m in range(pieces):
        lead = same_ref.shape[1]
        out_refs[m][0:lead] = same_ref[m]
        out_refs[m][lead:] = other_ref[m * lead : (m + 1) * lead]
    view = lax.axis_index("view")
    for m in range(parts):
        first = pl.multiple_of((view ^ m) * rows, 8)
        second = pl.multiple_of(start + (view ^ m) * rows, 8)
        out_refs[pieces + m][...] = keep_ref[pl.ds(first, rows)] + other_ref[pl.ds(second, rows)]


def sum_kernel(*refs):
    total = refs[0][...]
    for ref in refs[1:-1]:
        total = total + ref[...]
    refs[-1][...] = total


def join_kernel(token_ref, *refs):
    parts = len(refs) - 1
    rows = refs[0].shape[0]
    view = lax.axis_index("view")
    for m in range(parts):
        start = pl.multiple_of((view ^ m) * rows, 8)
        refs[-1][pl.ds(start, rows)] = refs[m][...]


def finish_kernel(mine_ref, other_ref, kernel_hbm, bias_hbm, sems):
    half = mine_ref.shape[0]
    size = kernel_hbm.shape[0]

    def move(first, second):
        copies = [
            pltpu.make_async_copy(first, kernel_hbm.at[0:half], sems.at[0]),
            pltpu.make_async_copy(
                second.at[0 : size - half], kernel_hbm.at[half:size], sems.at[1]
            ),
            pltpu.make_async_copy(second.at[size - half : size - half + 1], bias_hbm, sems.at[2]),
        ]
        for copy in copies:
            copy.start()
        for copy in copies:
            copy.wait()

    even = lax.axis_index("strip") % 2 == 0

    @pl.when(even)
    def _():
        move(mine_ref, other_ref)

    @pl.when(jnp.logical_not(even))
    def _():
        move(other_ref, mine_ref)


def swap(value, axis, mask):
    count = lax.axis_size(axis)
    return lax.ppermute(value, axis, [(i, i ^ mask) for i in range(count)])


def near_sum(value, axis, unit, amount):
    step = unit
    while amount > 1:
        near = 4 if amount % 4 == 0 else 2
        parts = [value] + [swap(value, axis, step * m) for m in range(1, near)]
        value = call(sum_kernel, jax.ShapeDtypeStruct(value.shape, F32), [VMEM] * near)(*parts)
        step, amount = step * near, amount // near
    return value


def per_device(
    means,
    inv_scales,
    correlation,
    opacity,
    features,
    cameras,
    owners,
    slots,
    lengths,
    target,
    weights,
    bias,
):
    shape = jax.ShapeDtypeStruct
    strips = lax.axis_size("strip")
    views = lax.axis_size("view")
    count = slots.shape[1] * slots.shape[2]
    owned, channels = features.shape
    height, breadth = target.shape[1], target.shape[2]
    pixels = height * breadth
    assert slots.shape[1] == 1 and breadth == WIDTH and channels == LANES
    bucket = max(4, 2 * count // strips)
    places = strips * bucket
    rows = bucket if bucket % 8 == 0 else 64
    groups = places // rows
    direct = rows == bucket
    paired = direct and strips <= 8
    lead = rows + 8
    wire_lead = bucket + 8

    def to_wire(value):
        if direct:
            return value
        top = value[:, :rows].reshape(strips, bucket, LANES)
        low = value[:, rows:, :rows].transpose(1, 0, 2).reshape(8, strips, bucket)
        low = jnp.pad(low.transpose(1, 0, 2), ((0, 0), (0, 0), (0, LANES - bucket)))
        return jnp.concatenate([top, low], axis=1)

    def from_wire(value):
        if direct:
            return value
        top = value[:, :bucket].reshape(groups, rows, LANES)
        low = value[:, bucket:, :bucket].transpose(1, 0, 2).reshape(8, groups, rows)
        low = jnp.pad(low.transpose(1, 0, 2), ((0, 0), (0, 0), (0, LANES - rows)))
        return jnp.concatenate([top, low], axis=1)

    def exchange(value):
        return lax.all_to_all(value, "strip", split_axis=0, concat_axis=0, tiled=True)

    camera = cameras[0]
    goal = target.reshape(pixels, channels)

    request, pos_row, pos_col, slot_row = call(
        functools.partial(route_kernel, bucket, rows, paired),
        [
            shape((groups, 1, LANES), F32),
            shape((1, count), jnp.int32),
            shape((count, 1), jnp.int32),
            shape((1, count), jnp.int32),
        ],
        [HBM] * 2,
        [pltpu.VMEM((1, count), jnp.int32)] * 2 + [pltpu.SemaphoreType.DMA((2,))],
    )(owners.reshape(1, count), slots.reshape(1, count))
    if not direct:
        request = request[:, 0, :rows].reshape(strips, 1, bucket)
        request = jnp.pad(request, ((0, 0), (0, 0), (0, LANES - bucket)))
    asked = exchange(request)
    if not direct:
        asked = asked[:, 0, :bucket].reshape(groups, 1, rows)
        asked = jnp.pad(asked, ((0, 0), (0, 0), (0, LANES - rows)))

    half, parts, straight, turned = call(
        prepare_kernel,
        [
            shape((owned, 2 * channels), BF16),
            shape((3 * 8 * (owned // LANES), LANES), BF16),
            shape((3, 3 * channels, 2 * channels), BF16),
            shape((3, 3 * channels, 2 * channels), BF16),
        ],
        [ANY] + [HBM] * 6,
        [
            pltpu.VMEM((8, owned), F32),
            pltpu.VMEM((1, owned), F32),
            pltpu.VMEM((1, owned), F32),
            pltpu.VMEM(means.shape, F32),
            pltpu.VMEM(inv_scales.shape, F32),
            pltpu.VMEM(features.shape, F32),
            pltpu.VMEM(weights.shape, F32),
            pltpu.SemaphoreType.DMA((6,)),
        ],
        flops=2**33,
        moved=2**24,
    )(pos_row, means, inv_scales, correlation[None, :], opacity[None, :], features, weights)

    chunk = shape((lead, LANES), F32)
    replies = call(
        functools.partial(reply_kernel, rows, paired),
        [chunk] * groups if paired else [shape((groups, lead, LANES), F32)],
        [VMEM] * 3,
        [pltpu.VMEM((places, owned), BF16)],
    )(asked, half, parts)
    if paired:
        order = sorted(range(1, groups), key=lambda m: (-(m // 2), m))
        far = {m: swap(replies[m], "strip", m) for m in order}
        fetched = [replies[0]] + [far[m] for m in range(1, groups)]
    else:
        fetched = [from_wire(exchange(to_wire(replies[0])))]

    tile, send_near, send_far, weight, ratio, geometry, feature = call(
        functools.partial(render_kernel, rows, groups, paired),
        [
            shape((pixels, channels), F32),
            shape((3 * WIDTH, channels), F32),
            shape((3 * WIDTH, channels), F32),
            shape((pixels, count), F32),
            shape((pixels, count), F32),
            shape((8, count), F32),
            shape((count, 2 * channels), BF16),
        ],
        [SMEM, SMEM] + [VMEM] * (3 + len(fetched)),
    )(camera, lengths, pos_row, pos_col, goal, *fetched)
    between = [(i, i + 1) for i in range(1, strips - 1, 2)]
    far = lax.ppermute(send_far, "strip", between + [(b, a) for a, b in between])
    near = swap(send_near, "strip", 1)
    spread = call(
        spread_kernel, shape((places, 2 * pixels), BF16), [VMEM] * 2, moved=2**21
    )(pos_row, weight)

    unit = 16 * views
    padded_rows = -(-(9 * channels + 1) // unit) * unit
    half = padded_rows // 2
    pieces = strips // 2 if paired else 0
    same, cross, keep = call(
        functools.partial(back_kernel, rows, groups, paired),
        [
            shape((pieces if paired else groups, lead, LANES), F32),
            shape((pieces * lead + half, LANES), F32),
            shape((half, channels), F32),
        ],
        [SMEM] + [VMEM] * 14,
        [
            pltpu.VMEM((pixels + 4 * WIDTH + 16, channels), F32),
            pltpu.VMEM((padded_rows, channels), F32),
        ],
        flops=2**30,
        moved=2**22,
    )(
        camera,
        tile,
        near,
        far,
        goal,
        straight,
        bias[None, :],
        turned,
        weight,
        ratio,
        geometry,
        feature,
        spread,
        pos_col,
        slot_row,
    )
    other = swap(cross, "strip", 1)
    part = shape((half // views, channels), F32)
    mixed = call(
        functools.partial(mix_kernel, pieces),
        [shape((2 * lead, LANES), F32)] * pieces + [part] * views,
        [VMEM] * 3,
    )(same, keep, other)
    if paired:
        order = range(pieces - 1, 0, -1)
        moved = {m: swap(mixed[m], "strip", 2 * m) for m in order}
        returned = [mixed[0]] + [moved[m] for m in range(1, pieces)]
    else:
        returned = [from_wire(exchange(to_wire(same))).reshape(groups * lead, LANES)]
    parts = [mixed[pieces]] + [swap(mixed[pieces + m], "view", m) for m in range(1, views)]
    total = call(sum_kernel, part, [VMEM] * views)(*parts)

    copies = call(
        copies_kernel,
        shape((views, groups * lead, LANES), F32),
        [ANY] + [VMEM] * len(returned),
        [pltpu.SemaphoreType.DMA((views, len(returned)))],
        out=ANY,
    )(total, *returned)
    arrived = lax.all_to_all(copies, "view", split_axis=0, concat_axis=0, tiled=True)
    arrived = arrived.reshape(views * groups, lead, LANES)

    total = near_sum(total, "strip", 2, strips // 2)
    parts = [total] + [swap(total, "view", m) for m in range(1, views)]
    geometry_grad, feature_grad = call(
        functools.partial(gather_kernel, rows),
        [shape((7, owned), F32), shape((owned, channels), F32)],
        [ANY, VMEM],
        [pltpu.VMEM((views * places, 2 * channels), BF16)],
        flops=2**32,
        moved=2**23,
    )(total, arrived)
    joined = call(join_kernel, shape((half, channels), F32), [ANY] + [VMEM] * views)(
        geometry_grad, *parts
    )
    other = swap(joined, "strip", 1)
    kernel_grad, bias_grad = call(
        finish_kernel,
        [shape((9 * channels, channels), F32), shape((1, channels), F32)],
        [ANY, ANY],
        [pltpu.SemaphoreType.DMA((3,))],
        out=HBM,
    )(joined, other)
    return (
        geometry_grad,
        feature_grad,
        kernel_grad.reshape(weights.shape),
        bias_grad.reshape(bias.shape),
    )


def solution(mesh):
    return jax.shard_map(
        per_device,
        mesh=mesh,
        in_specs=(
            P(None, "strip"),
            P(None, "strip"),
            P("strip"),
            P("strip"),
            P("strip", None),
            P("view", None, None),
            P("view", "strip", None, None),
            P("view", "strip", None),
            P("view", "strip"),
            P("view", "strip", None, None),
            P(),
            P(),
        ),
        out_specs=(P(None, "strip"), P("strip", None), P(), P()),
        check_vma=False,
    )
```

```python
import functools

import jax
import jax.numpy as jnp
from jax import lax
from jax.experimental import pallas as pl
from jax.experimental.pallas import tpu as pltpu
from jax.sharding import PartitionSpec as P

HIGHEST = lax.Precision.HIGHEST
F32 = jnp.float32
BF16 = jnp.bfloat16
LANES = 128
WIDTH = 16
VMEM = pl.BlockSpec(memory_space=pltpu.VMEM)
SMEM = pl.BlockSpec(memory_space=pltpu.SMEM)
ANY = pl.BlockSpec(memory_space=pl.ANY)
HBM = pl.BlockSpec(memory_space=pltpu.HBM)


def iota(shape, dim):
    return lax.broadcasted_iota(jnp.int32, shape, dim)


def onehot(mask):
    return jnp.where(mask, 1.0, 0.0).astype(BF16)


def split2(x):
    high = x.astype(BF16)
    return high, (x - high.astype(F32)).astype(BF16)


def split3(x):
    high = x.astype(BF16)
    rest = x - high.astype(F32)
    middle = rest.astype(BF16)
    return high, middle, (rest - middle.astype(F32)).astype(BF16)


def dot(a, b):
    return jnp.dot(a, b, preferred_element_type=F32)


def dot_nt(a, b):
    return lax.dot_general(a, b, (((1,), (1,)), ((), ())), preferred_element_type=F32)


def call(kernel, out_shape, in_specs, scratch=(), flops=0, moved=0, out=VMEM, alias=None):
    return pl.pallas_call(
        kernel,
        out_shape=out_shape,
        in_specs=in_specs,
        out_specs=out if isinstance(out, list) else jax.tree.map(lambda _: out, out_shape),
        input_output_aliases=alias or {},
        scratch_shapes=list(scratch),
        compiler_params=pltpu.CompilerParams(vmem_limit_bytes=48 * 2**20),
        cost_estimate=pl.CostEstimate(flops=flops, bytes_accessed=moved, transcendentals=0),
    )


def route_kernel(
    bucket,
    rows,
    paired,
    entry_ref,
    request_ref,
    pos_row_ref,
    pos_col_ref,
    slot_copy_ref,
):
    owner_ref, slot_ref = entry_ref.at[0:1], entry_ref.at[1:2]
    slot_copy_ref[...] = slot_ref[...]
    groups = request_ref.shape[0]
    count = owner_ref.shape[1]
    owner_row = owner_ref[...].astype(F32)
    down, across = iota((count, count), 0), iota((count, count), 1)
    owner_col = jnp.sum(jnp.where(down == across, owner_row, 0.0), axis=1, keepdims=True)
    same = owner_col == owner_row
    rank_row = jnp.sum(jnp.where(same & (down < across), 1.0, 0.0), axis=0, keepdims=True)
    rank_col = jnp.sum(jnp.where(same & (across < down), 1.0, 0.0), axis=1, keepdims=True)
    pos_row = (owner_row * bucket + rank_row).astype(jnp.int32)
    pos_col = (owner_col * bucket + rank_col).astype(jnp.int32)
    mask = lax.axis_index("strip") * bucket if paired else 0
    pos_row_ref[...] = pos_row ^ mask
    pos_col_ref[...] = pos_col ^ mask
    shift = rows.bit_length() - 1
    left = jnp.where(
        iota((groups, count), 0) == lax.shift_right_logical(pos_row, shift),
        slot_ref[...].astype(F32),
        0.0,
    )
    right = jnp.where(iota((count, LANES), 1) == (pos_col & (rows - 1)), 1.0, 0.0)
    wanted = jnp.dot(left, right, precision=HIGHEST, preferred_element_type=F32)
    for group in range(groups):
        request_ref[group] = wanted[group : group + 1]


def prepare_kernel(token_ref, table_ref, feature_ref, half_ref, parts_ref):
    owned, channels = feature_ref.shape
    blocks = owned // LANES
    high, low = split2(feature_ref[...])
    half_ref[:, :channels] = high
    half_ref[:, channels:] = low
    table = table_ref[...]
    stacked = jnp.concatenate(
        [table[:, a * LANES : (a + 1) * LANES] for a in range(blocks)], axis=0
    )
    parts_ref[...] = jnp.concatenate(split3(stacked), axis=0)


def weights_kernel(token_ref, weights_ref, straight_ref, turned_ref):
    size = weights_ref.shape[2]
    for i in range(3):
        for j in range(3):
            block = weights_ref[i, j]
            high, low = split2(block)
            straight_ref[i, j * size : (j + 1) * size, :size] = high
            straight_ref[i, j * size : (j + 1) * size, size:] = low
            high, low = split2(block.T)
            a, b = 2 - i, 2 - j
            turned_ref[a, b * size : (b + 1) * size, :size] = high
            turned_ref[a, b * size : (b + 1) * size, size:] = low


def reply_kernel(rows, paired, asked_ref, half_ref, parts_ref, *refs):
    pick_ref = refs[-1]
    groups = asked_ref.shape[0]
    first = lax.axis_index("strip") if paired else 0
    replies = list(refs[:-1]) if paired else [refs[0].at[group] for group in range(groups)]
    owned = half_ref.shape[0]
    channels = half_ref.shape[1] // 2
    blocks = owned // LANES
    asked = jnp.concatenate([asked_ref[group ^ first] for group in range(groups)], axis=0)
    padded = jnp.concatenate([asked, jnp.zeros((LANES - groups, LANES), F32)], axis=0)
    columns = padded.T.astype(jnp.int32)
    place = iota((rows, owned), 1)
    for group in range(groups):
        pick_ref[group * rows : (group + 1) * rows] = onehot(
            columns[:rows, group : group + 1] == place
        )
    found = dot(pick_ref[...], half_ref[...])
    found = found[:, :channels] + found[:, channels:]
    slots = asked.astype(jnp.int32)
    slots_row = jnp.concatenate([slots[group : group + 1] for group in range(groups)], axis=1)
    wide = slots_row.shape[1]
    minor = onehot((slots_row & (LANES - 1)) == iota((LANES, wide), 0))
    product = dot(parts_ref[...], minor)
    deep = blocks * 8
    product = product[:deep] + product[deep : 2 * deep] + product[2 * deep :]
    major = lax.shift_right_logical(slots_row, 7)
    geometry = jnp.zeros((8, wide), F32)
    for a in range(blocks):
        geometry = geometry + jnp.where(major == a, product[a * 8 : (a + 1) * 8], 0.0)
    for group in range(groups):
        replies[group][0:rows] = found[group * rows : (group + 1) * rows]
        replies[group][rows : rows + 8] = geometry[:, group * LANES : (group + 1) * LANES]


def centers(camera_ref, geometry):
    found = []
    for axis in range(2):
        found.append(
            8.0
            + 4.0
            * (
                camera_ref[axis, 0] * geometry[0:1]
                + camera_ref[axis, 1] * geometry[1:2]
                + camera_ref[axis, 2] * geometry[2:3]
                + camera_ref[axis, 3]
            )
        )
    return found


def offsets(camera_ref, geometry, pixels):
    center_col, center_row = centers(camera_ref, geometry)
    pixel = iota((pixels, geometry.shape[1]), 0)
    across = (pixel & (WIDTH - 1)).astype(F32) + 0.5
    downward = lax.shift_right_logical(pixel, WIDTH.bit_length() - 1).astype(F32) + 0.5
    return across - center_col, downward - center_row


def render_kernel(
    rows,
    groups,
    paired,
    camera_ref,
    length_ref,
    pos_row_ref,
    pos_col_ref,
    target_ref,
    *refs,
):
    fetched = list(refs[:-7]) if paired else [refs[0].at[group] for group in range(groups)]
    tile_ref, send_near_ref, send_far_ref, weight_ref, ratio_ref, geometry_ref, feature_ref = refs[-7:]
    count = pos_row_ref.shape[1]
    places = groups * rows
    pixels, channels = tile_ref.shape
    pick = onehot(pos_col_ref[...] == iota((count, places), 1))
    pick_t = onehot(pos_row_ref[...] == iota((places, count), 0))
    sent = jnp.concatenate([fetched[group][0:rows] for group in range(groups)], axis=0)
    feature = dot(pick, jnp.concatenate(split2(sent), axis=1)).astype(BF16)
    feature_ref[...] = feature
    sent = jnp.concatenate(
        [fetched[group][rows : rows + 8][:, :rows] for group in range(groups)], axis=1
    )
    geometry = dot(jnp.concatenate(split3(sent), axis=0), pick_t)
    geometry = geometry[0:8] + geometry[8:16] + geometry[16:24]
    geometry_ref[...] = geometry
    du, dv = offsets(camera_ref, geometry, pixels)
    a = geometry[3:4] * du
    b = geometry[4:5] * dv
    exponent = -0.5 * (a * a + 2.0 * geometry[5:6] * a * b + b * b)
    alive = iota((1, count), 1) < length_ref[0, 0]
    sigmoid = 1.0 / (1.0 + jnp.exp(-geometry[6:7]))
    raw = sigmoid * jnp.exp(exponent)
    alpha = jnp.where(alive, jnp.minimum(raw, 0.99), 0.0)
    keep = 1.0 - alpha
    log_keep = jnp.log(keep)
    before = onehot(iota((count, count), 0) < iota((count, count), 1))
    high, low = split2(log_keep)
    weight = alpha * jnp.exp(dot(high, before) + dot(low, before))
    weight_ref[...] = weight
    ratio_ref[...] = jnp.where(raw < 0.99, alpha, 0.0) / keep
    high, low = split2(weight)
    tile = dot(high, feature)
    tile = tile[:, :channels] + tile[:, channels:] + dot(low, feature[:, :channels])
    tile_ref[...] = tile
    top = jnp.concatenate([tile[0 : 2 * WIDTH], target_ref[0:WIDTH]], axis=0)
    bottom = jnp.concatenate([tile[pixels - 2 * WIDTH :], target_ref[pixels - WIDTH : pixels]], axis=0)
    even = lax.axis_index("strip") % 2 == 0
    send_near_ref[...] = jnp.where(even, bottom, top)
    send_far_ref[...] = jnp.where(even, top, bottom)


def spread_kernel(pos_row_ref, weight_ref, spread_ref):
    places = spread_ref.shape[0]
    pixels, count = weight_ref.shape
    pick_t = onehot(pos_row_ref[...] == iota((places, count), 0))
    high, low = split2(weight_ref[...])
    spread_ref[:, :pixels] = dot_nt(pick_t, high).astype(BF16)
    spread_ref[:, pixels:] = dot_nt(pick_t, low).astype(BF16)


def shifted(value, scratch_ref):
    count = value.shape[0]
    scratch_ref[8 : 8 + count] = value
    column = iota((count, 1), 0) & (WIDTH - 1)
    left = jnp.where(column == 0, 0.0, scratch_ref[7 : 7 + count])
    right = jnp.where(column == WIDTH - 1, 0.0, scratch_ref[9 : 9 + count])
    return jnp.concatenate([left, value, right], axis=1)


def taps(wide, kernel_ref, count, channels):
    high, low = split2(wide)
    total = jnp.zeros((count, channels), F32)
    for i in range(3):
        part = dot(high[WIDTH * i : WIDTH * i + count], kernel_ref[i])
        total = total + part[:, :channels] + part[:, channels:]
        total = total + dot(low[WIDTH * i : WIDTH * i + count], kernel_ref[i][:, :channels])
    return total


def decode(tile_ref, near_ref, far_ref, target_ref, kernel_ref, bias_ref, scratch_ref, sum_ref):
    pixels, channels = tile_ref.shape
    edge = 2 * WIDTH
    strip = lax.axis_index("strip")
    even = strip % 2 == 0
    near, far = near_ref[...], far_ref[...]
    above, below = jnp.where(even, far, near), jnp.where(even, near, far)
    scratch_ref[0:8] = jnp.zeros((8, channels), F32)
    padded = jnp.concatenate([above[0:edge], tile_ref[...], below[0:edge]], axis=0)
    count = pixels + 2 * WIDTH
    scratch_ref[8 + count + 2 * WIDTH : 16 + count + 2 * WIDTH] = jnp.zeros((8, channels), F32)
    wide = shifted(padded, scratch_ref)
    goal = jnp.concatenate([above[edge:], target_ref[...], below[edge:]], axis=0)
    residual = taps(wide, kernel_ref, count, channels) + bias_ref[...] - goal
    pixel = iota((count, 1), 0)
    outside = ((pixel < WIDTH) & (strip == 0)) | (
        (pixel >= count - WIDTH) & (strip == lax.axis_size("strip") - 1)
    )
    residual = jnp.where(outside, 0.0, residual)

    own = residual[WIDTH : WIDTH + pixels]
    turned_high, turned_low = split2(own.T)
    high, low = split2(wide)
    for i in range(3):
        first = WIDTH * (1 + i)
        part = (
            dot(turned_high, high[first : first + pixels])
            + dot(turned_high, low[first : first + pixels])
            + dot(turned_low, high[first : first + pixels])
        )
        for j in range(3):
            block = (3 * i + j) * channels
            sum_ref[block : block + channels] = part[:, j * channels : (j + 1) * channels].T
    return residual, jnp.sum(own, axis=0, keepdims=True)


def back_kernel(
    rows,
    groups,
    paired,
    camera_ref,
    tile_ref,
    near_ref,
    far_ref,
    target_ref,
    straight_ref,
    bias_ref,
    turned_ref,
    weight_ref,
    ratio_ref,
    geometry_ref,
    feature_ref,
    spread_ref,
    pos_col_ref,
    slot_ref,
    same_ref,
    cross_ref,
    keep_ref,
    own_bias_ref,
    scratch_ref,
    sum_ref,
):
    pixels, count = weight_ref.shape
    channels = tile_ref.shape[1]
    places = groups * rows
    lead = rows + 8
    half = keep_ref.shape[0]
    residual, bias_grad = decode(
        tile_ref, near_ref, far_ref, target_ref, straight_ref, bias_ref, scratch_ref, sum_ref
    )
    start = cross_ref.shape[0] - half - 8
    bias_rows = jnp.where(iota((8, channels), 0) == 0, bias_grad, 0.0)
    own_bias_ref[...] = bias_rows
    cross_ref[start + half :] = bias_rows
    even = lax.axis_index("strip") % 2 == 0
    keep_ref[...] = jnp.where(even, sum_ref[0:half], sum_ref[half:])
    cross_ref[start : start + half] = jnp.where(even, sum_ref[half:], sum_ref[0:half])

    def put(group, first, value):
        amount = value.shape[0]
        if not paired:
            same_ref[group, first : first + amount] = value
        elif group % 2 == 0:
            same_ref[group // 2, first : first + amount] = value
        else:
            first = group // 2 * lead + first
            cross_ref[first : first + amount] = value

    extent = residual.shape[0]
    scratch_ref[8 + extent : 16 + extent] = jnp.zeros((8, channels), F32)
    wide = shifted(residual, scratch_ref)
    grad = taps(wide, turned_ref, pixels, channels)
    high, low = split2(grad)
    both = jnp.concatenate([high, low], axis=1)
    part = dot(spread_ref[:, :pixels], both)
    part = part[:, :channels] + part[:, channels:] + dot(spread_ref[:, pixels:], high)
    for group in range(groups):
        put(group, 0, part[group * rows : (group + 1) * rows])

    near, far = feature_ref[:, :channels], feature_ref[:, channels:]
    weight_grad = dot_nt(high, near) + dot_nt(high, far) + dot_nt(low, near)
    pull = weight_grad * weight_ref[...]
    behind = onehot(iota((count, count), 0) > iota((count, count), 1))
    high, low = split2(pull)
    suffix = dot(high, behind) + dot(low, behind)
    ratio = ratio_ref[...]
    change = jnp.where(ratio > 0.0, pull - ratio * suffix, 0.0)

    geometry = geometry_ref[...]
    du, dv = offsets(camera_ref, geometry, pixels)

    def total(x):
        return jnp.sum(x, axis=0, keepdims=True)

    change_u, change_v = change * du, change * dv
    m, mu, mv = total(change), total(change_u), total(change_v)
    muu, muv, mvv = total(change_u * du), total(change_u * dv), total(change_v * dv)
    g3, g4, g5, g6 = (geometry[i : i + 1] for i in range(3, 7))
    center_col = g3 * (g3 * mu + g5 * g4 * mv)
    center_row = g4 * (g5 * g3 * mu + g4 * mv)
    lines = [
        4.0 * (camera_ref[0, i] * center_col + camera_ref[1, i] * center_row) for i in range(3)
    ]
    lines.append(-(g3 * muu + g5 * g4 * muv))
    lines.append(-(g4 * mvv + g5 * g3 * muv))
    lines.append(-(g3 * g4 * muv))
    lines.append(m / (1.0 + jnp.exp(g6)))
    lines.append(slot_ref[...].astype(F32))
    pick = onehot(pos_col_ref[...] == iota((count, places), 1))
    moved = dot(jnp.concatenate(split3(jnp.concatenate(lines, axis=0)), axis=0), pick)
    moved = moved[0:8] + moved[8:16] + moved[16:24]
    for group in range(groups):
        piece = moved[:, group * rows : (group + 1) * rows]
        if rows < LANES:
            piece = jnp.concatenate([piece, jnp.zeros((8, LANES - rows), F32)], axis=1)
        put(group, rows, piece)


def copies_kernel(amount, paired, *refs):
    values, parts = refs[:amount], refs[amount:-4]
    copies_ref, sum_ref, bias_ref, sems = refs[-4:]
    rows = values[0].shape[0] - (8 if paired else 0)
    jobs = [(value.at[0:rows], place * rows, rows) for place, value in enumerate(values)]
    if paired:
        bias_rows = values[0][rows:]
        for value in values[1:]:
            bias_rows = bias_rows + value[rows:]
        bias_ref[...] = bias_rows
        jobs.append((bias_ref, amount * rows, 8))
    copies = [
        pltpu.make_async_copy(
            source, copies_ref.at[view, start : start + length], sems.at[view, place]
        )
        for view in range(copies_ref.shape[0])
        for place, (source, start, length) in enumerate(jobs)
    ]
    for copy in copies:
        copy.start()
    sum_kernel(*parts, sum_ref)
    for copy in copies:
        copy.wait()


def gather_rows(slot_row, half_ref, start, count):
    channels = half_ref.shape[1] // 2
    pick_t = onehot(slot_row == iota((count, half_ref.shape[0]), 0) + start)
    part = dot(pick_t, half_ref[...])
    return part[:, :channels] + part[:, channels:]


def gather_first_kernel(
    rows, groups, token_ref, arrived_ref, feature_ref, half_ref, lines_ref, bias_ref
):
    channels = feature_ref.shape[1]
    lead = rows + 8
    lines = []
    for view in range(arrived_ref.shape[0]):
        for group in range(groups):
            first = group * lead
            piece = view * groups + group
            high, low = split2(arrived_ref[view, first : first + rows])
            half_ref[piece * rows : (piece + 1) * rows, :channels] = high
            half_ref[piece * rows : (piece + 1) * rows, channels:] = low
            lines.append(arrived_ref[view, first + rows : first + lead][:, :rows])
    lines = jnp.concatenate(lines, axis=1)
    lines_ref[...] = lines
    if arrived_ref.shape[1] > groups * lead:
        bias = arrived_ref[0, groups * lead : groups * lead + 1]
        for view in range(1, arrived_ref.shape[0]):
            bias = bias + arrived_ref[view, groups * lead : groups * lead + 1]
        bias_ref[...] = bias
    else:
        bias_ref[...] = jnp.zeros(bias_ref.shape, F32)
    slot_row = lines[7:8].astype(jnp.int32)
    tile = 256
    for start in range(0, feature_ref.shape[0], tile):
        feature_ref[start : start + tile] = gather_rows(slot_row, half_ref, start, tile)


def gather_second_kernel(
    token_ref,
    half_ref,
    lines_ref,
    begun_ref,
    bias_in_ref,
    feature_hbm,
    geometry_hbm,
    bias_hbm,
    end_ref,
    geometry_ref,
    out_ref,
    sems,
):
    owned = feature_hbm.shape[0]
    begun = begun_ref.shape[0]
    blocks = owned // LANES
    lines = lines_ref[...]
    amount = lines.shape[1]
    copies = [
        pltpu.make_async_copy(begun_ref, feature_hbm.at[0:begun], sems.at[0]),
        pltpu.make_async_copy(bias_in_ref, bias_hbm, sems.at[1]),
    ]
    for copy in copies:
        copy.start()
    slot_row = lines[7:8].astype(jnp.int32)
    minor = onehot((slot_row & (LANES - 1)) == iota((LANES, amount), 0))
    major = lax.shift_right_logical(slot_row, 7)
    stacked = jnp.concatenate([jnp.where(major == a, lines, 0.0) for a in range(blocks)], axis=0)
    high, low = split2(stacked)
    product = dot_nt(high, minor) + dot_nt(low, minor)
    for a in range(blocks):
        geometry_ref[:, a * LANES : (a + 1) * LANES] = product[a * 8 : a * 8 + 7]
    copies.append(pltpu.make_async_copy(geometry_ref, geometry_hbm, sems.at[2]))
    copies[-1].start()
    tile = out_ref.shape[1]
    for step, start in enumerate(range(begun, owned, tile)):
        out_ref[step] = gather_rows(slot_row, half_ref, start, tile)
        copies.append(
            pltpu.make_async_copy(
                out_ref.at[step], feature_hbm.at[start : start + tile], sems.at[3 + step]
            )
        )
        copies[-1].start()
    end_ref[...] = jnp.zeros(end_ref.shape, F32)
    for copy in copies:
        copy.wait()


def mix_kernel(pieces, same_ref, keep_ref, own_bias_ref, other_ref, *out_refs):
    parts = len(out_refs) - pieces
    rows = keep_ref.shape[0] // parts
    start = other_ref.shape[0] - keep_ref.shape[0] - 8
    bias_rows = own_bias_ref[...] + other_ref[start + keep_ref.shape[0] :]
    for m in range(pieces):
        lead = same_ref.shape[1]
        out_refs[m][0:lead] = same_ref[m]
        out_refs[m][lead : 2 * lead] = other_ref[m * lead : (m + 1) * lead]
        out_refs[m][2 * lead :] = bias_rows
    view = lax.axis_index("view")
    for m in range(parts):
        first = pl.multiple_of((view ^ m) * rows, 8)
        second = pl.multiple_of(start + (view ^ m) * rows, 8)
        out_refs[pieces + m][...] = keep_ref[pl.ds(first, rows)] + other_ref[pl.ds(second, rows)]


def sum_kernel(*refs):
    total = refs[0][...]
    for ref in refs[1:-1]:
        total = total + ref[...]
    refs[-1][...] = total


def join_kernel(token_ref, *refs):
    parts = len(refs) - 1
    rows = refs[0].shape[0]
    view = lax.axis_index("view")
    for m in range(parts):
        start = pl.multiple_of((view ^ m) * rows, 8)
        refs[-1][pl.ds(start, rows)] = refs[m][...]


def finish_kernel(token_ref, mine_ref, other_ref, kernel_hbm, sems):
    half = mine_ref.shape[0]

    def move(first, second):
        copies = [
            pltpu.make_async_copy(first, kernel_hbm.at[0:half], sems.at[0]),
            pltpu.make_async_copy(second, kernel_hbm.at[half:], sems.at[1]),
        ]
        for copy in copies:
            copy.start()
        for copy in copies:
            copy.wait()

    even = lax.axis_index("strip") % 2 == 0

    @pl.when(even)
    def _():
        move(mine_ref, other_ref)

    @pl.when(jnp.logical_not(even))
    def _():
        move(other_ref, mine_ref)


def swap(value, axis, mask):
    count = lax.axis_size(axis)
    return lax.ppermute(value, axis, [(i, i ^ mask) for i in range(count)])


def near_sum(value, axis, unit, amount):
    step = unit
    while amount > 1:
        near = 4 if amount % 4 == 0 else 2
        parts = [value] + [swap(value, axis, step * m) for m in range(1, near)]
        value = call(sum_kernel, jax.ShapeDtypeStruct(value.shape, F32), [VMEM] * near)(*parts)
        step, amount = step * near, amount // near
    return value


def per_device(
    means,
    inv_scales,
    correlation,
    opacity,
    features,
    cameras,
    owners,
    slots,
    lengths,
    target,
    weights,
    bias,
):
    shape = jax.ShapeDtypeStruct
    strips = lax.axis_size("strip")
    views = lax.axis_size("view")
    count = slots.shape[1] * slots.shape[2]
    owned, channels = features.shape
    height, breadth = target.shape[1], target.shape[2]
    pixels = height * breadth
    assert slots.shape[1] == 1 and breadth == WIDTH and channels == LANES
    bucket = max(4, 2 * count // strips)
    places = strips * bucket
    rows = bucket if bucket % 8 == 0 else 64
    groups = places // rows
    direct = rows == bucket
    paired = direct and strips <= 8
    lead = rows + 8
    wire_lead = bucket + 8

    def to_wire(value):
        if direct:
            return value
        top = value[:, :rows].reshape(strips, bucket, LANES)
        low = value[:, rows:, :rows].transpose(1, 0, 2).reshape(8, strips, bucket)
        low = jnp.pad(low.transpose(1, 0, 2), ((0, 0), (0, 0), (0, LANES - bucket)))
        return jnp.concatenate([top, low], axis=1)

    def from_wire(value):
        if direct:
            return value
        top = value[:, :bucket].reshape(groups, rows, LANES)
        low = value[:, bucket:, :bucket].transpose(1, 0, 2).reshape(8, groups, rows)
        low = jnp.pad(low.transpose(1, 0, 2), ((0, 0), (0, 0), (0, LANES - rows)))
        return jnp.concatenate([top, low], axis=1)

    def exchange(value):
        return lax.all_to_all(value, "strip", split_axis=0, concat_axis=0, tiled=True)

    camera = cameras[0]
    goal = target.reshape(pixels, channels)

    request, pos_row, pos_col, slot_row = call(
        functools.partial(route_kernel, bucket, rows, paired),
        [
            shape((groups, 1, LANES), F32),
            shape((1, count), jnp.int32),
            shape((count, 1), jnp.int32),
            shape((1, count), jnp.int32),
        ],
        [VMEM],
    )(jnp.concatenate([owners.reshape(1, count), slots.reshape(1, count)], axis=0))
    if not direct:
        request = request[:, 0, :rows].reshape(strips, 1, bucket)
        request = jnp.pad(request, ((0, 0), (0, 0), (0, LANES - bucket)))
    asked = exchange(request)
    if not direct:
        asked = asked[:, 0, :bucket].reshape(groups, 1, rows)
        asked = jnp.pad(asked, ((0, 0), (0, 0), (0, LANES - rows)))

    table = jnp.concatenate(
        [
            means,
            inv_scales,
            correlation[None, :],
            opacity[None, :],
            jnp.zeros((1, owned), F32),
        ],
        axis=0,
    )
    half, parts = call(
        prepare_kernel,
        [
            shape((owned, 2 * channels), BF16),
            shape((3 * 8 * (owned // LANES), LANES), BF16),
        ],
        [ANY, VMEM, VMEM],
        flops=2**33,
        moved=2**24,
    )(pos_row, table, features)
    chunk = shape((lead, LANES), F32)
    replies = call(
        functools.partial(reply_kernel, rows, paired),
        [chunk] * groups if paired else [shape((groups, lead, LANES), F32)],
        [VMEM] * 3,
        [pltpu.VMEM((places, owned), BF16)],
    )(asked, half, parts)
    straight, turned = call(
        weights_kernel,
        [shape((3, 3 * channels, 2 * channels), BF16)] * 2,
        [ANY, VMEM],
        flops=2**32,
        moved=2**23,
    )(replies[0], weights)
    if paired:
        order = sorted(range(1, groups), key=lambda m: (-(m // 2), m))
        far = {m: swap(replies[m], "strip", m) for m in order}
        fetched = [replies[0]] + [far[m] for m in range(1, groups)]
    else:
        fetched = [from_wire(exchange(to_wire(replies[0])))]

    tile, send_near, send_far, weight, ratio, geometry, feature = call(
        functools.partial(render_kernel, rows, groups, paired),
        [
            shape((pixels, channels), F32),
            shape((3 * WIDTH, channels), F32),
            shape((3 * WIDTH, channels), F32),
            shape((pixels, count), F32),
            shape((pixels, count), F32),
            shape((8, count), F32),
            shape((count, 2 * channels), BF16),
        ],
        [SMEM, SMEM] + [VMEM] * (3 + len(fetched)),
    )(camera, lengths, pos_row, pos_col, goal, *fetched)
    between = [(i, i + 1) for i in range(1, strips - 1, 2)]
    far = lax.ppermute(send_far, "strip", between + [(b, a) for a, b in between])
    near = swap(send_near, "strip", 1)
    spread = call(
        spread_kernel, shape((places, 2 * pixels), BF16), [VMEM] * 2, moved=2**21
    )(pos_row, weight)

    half = 9 * channels // 2
    assert half % (8 * views) == 0
    pieces = strips // 2 if paired else 0
    same, cross, keep, own_bias = call(
        functools.partial(back_kernel, rows, groups, paired),
        [
            shape((pieces if paired else groups, lead, LANES), F32),
            shape((pieces * lead + half + 8, LANES), F32),
            shape((half, channels), F32),
            shape((8, channels), F32),
        ],
        [SMEM] + [VMEM] * 14,
        [
            pltpu.VMEM((pixels + 4 * WIDTH + 16, channels), F32),
            pltpu.VMEM((9 * channels, channels), F32),
        ],
        flops=2**30,
        moved=2**22,
    )(
        camera,
        tile,
        near,
        far,
        goal,
        straight,
        bias[None, :],
        turned,
        weight,
        ratio,
        geometry,
        feature,
        spread,
        pos_col,
        slot_row,
    )
    other = swap(cross, "strip", 1)
    part = shape((half // views, channels), F32)
    mixed = call(
        functools.partial(mix_kernel, pieces),
        [shape((2 * lead + 8, LANES), F32)] * pieces + [part] * views,
        [VMEM] * 4,
    )(same, keep, own_bias, other)
    if paired:
        order = range(pieces - 1, 0, -1)
        moved = {m: swap(mixed[m], "strip", 2 * m) for m in order}
        returned = [mixed[0]] + [moved[m] for m in range(1, pieces)]
    else:
        returned = [from_wire(exchange(to_wire(same))).reshape(groups * lead, LANES)]
    parts = [mixed[pieces]] + [swap(mixed[pieces + m], "view", m) for m in range(1, views)]
    length = groups * lead + (8 if paired else 0)
    copies, total = call(
        functools.partial(copies_kernel, len(returned), paired),
        [shape((views, length, LANES), F32), part],
        [VMEM] * (len(returned) + views),
        [pltpu.VMEM((8, channels), F32), pltpu.SemaphoreType.DMA((views, len(returned) + 1))],
        out=[ANY, VMEM],
    )(*returned, *parts)
    arrived = lax.all_to_all(copies, "view", split_axis=0, concat_axis=0, tiled=True)

    total = near_sum(total, "strip", 2, strips // 2)
    parts = [total] + [swap(total, "view", m) for m in range(1, views)]
    first = owned // 2
    feature_first, rowed, lines, bias_sum = call(
        functools.partial(gather_first_kernel, rows, groups),
        [
            shape((first, channels), F32),
            shape((views * places, 2 * channels), BF16),
            shape((8, views * places), F32),
            shape((1, channels), F32),
        ],
        [ANY, VMEM],
        flops=2**31,
        moved=2**22,
    )(total, arrived)
    if not paired:
        bias_sum = lax.psum(own_bias[0:1], ("view", "strip"))
    joined = call(join_kernel, shape((half, channels), F32), [ANY] + [VMEM] * views)(lines, *parts)
    other = swap(joined, "strip", 1)
    tile = 256
    feature_grad, geometry_grad, bias_grad, end = call(
        gather_second_kernel,
        [
            shape((owned, channels), F32),
            shape((7, owned), F32),
            shape((1, channels), F32),
            shape((8, LANES), F32),
        ],
        [ANY] + [VMEM] * 4,
        [
            pltpu.VMEM((7, owned), F32),
            pltpu.VMEM(((owned - first) // tile, tile, channels), F32),
            pltpu.SemaphoreType.DMA((3 + (owned - first) // tile,)),
        ],
        out=[HBM, HBM, HBM, VMEM],
        flops=2**31,
        moved=2**22,
    )(joined, rowed, lines, feature_first, bias_sum)
    kernel_grad = call(
        finish_kernel,
        shape((9 * channels, channels), F32),
        [ANY, ANY, ANY],
        [pltpu.SemaphoreType.DMA((2,))],
        out=HBM,
    )(end, joined, other)
    return (
        geometry_grad,
        feature_grad,
        kernel_grad.reshape(weights.shape),
        bias_grad.reshape(bias.shape),
    )


def solution(mesh):
    return jax.shard_map(
        per_device,
        mesh=mesh,
        in_specs=(
            P(None, "strip"),
            P(None, "strip"),
            P("strip"),
            P("strip"),
            P("strip", None),
            P("view", None, None),
            P("view", "strip", None, None),
            P("view", "strip", None),
            P("view", "strip"),
            P("view", "strip", None, None),
            P(),
            P(),
        ),
        out_specs=(P(None, "strip"), P("strip", None), P(), P()),
        check_vma=False,
    )
```

```python
import functools

import jax
import jax.numpy as jnp
from jax import lax
from jax.experimental import pallas as pl
from jax.experimental.pallas import tpu as pltpu
from jax.sharding import PartitionSpec as P

HIGHEST = lax.Precision.HIGHEST
F32 = jnp.float32
BF16 = jnp.bfloat16
LANES = 128
WIDTH = 16
VMEM = pl.BlockSpec(memory_space=pltpu.VMEM)
SMEM = pl.BlockSpec(memory_space=pltpu.SMEM)
ANY = pl.BlockSpec(memory_space=pl.ANY)
HBM = pl.BlockSpec(memory_space=pltpu.HBM)


def iota(shape, dim):
    return lax.broadcasted_iota(jnp.int32, shape, dim)


def onehot(mask):
    return jnp.where(mask, 1.0, 0.0).astype(BF16)


def split2(x):
    high = x.astype(BF16)
    return high, (x - high.astype(F32)).astype(BF16)


def split3(x):
    high = x.astype(BF16)
    rest = x - high.astype(F32)
    middle = rest.astype(BF16)
    return high, middle, (rest - middle.astype(F32)).astype(BF16)


def dot(a, b):
    return jnp.dot(a, b, preferred_element_type=F32)


def dot_nt(a, b):
    return lax.dot_general(a, b, (((1,), (1,)), ((), ())), preferred_element_type=F32)


def call(kernel, out_shape, in_specs, scratch=(), flops=0, moved=0, out=VMEM, alias=None):
    return pl.pallas_call(
        kernel,
        out_shape=out_shape,
        in_specs=in_specs,
        out_specs=out if isinstance(out, list) else jax.tree.map(lambda _: out, out_shape),
        input_output_aliases=alias or {},
        scratch_shapes=list(scratch),
        compiler_params=pltpu.CompilerParams(vmem_limit_bytes=48 * 2**20),
        cost_estimate=pl.CostEstimate(flops=flops, bytes_accessed=moved, transcendentals=0),
    )


def route_kernel(
    bucket,
    rows,
    paired,
    entry_ref,
    request_ref,
    pos_row_ref,
    pos_col_ref,
    slot_copy_ref,
):
    owner_ref, slot_ref = entry_ref.at[0:1], entry_ref.at[1:2]
    slot_copy_ref[...] = slot_ref[...]
    groups = request_ref.shape[0]
    count = owner_ref.shape[1]
    owner_row = owner_ref[...].astype(F32)
    down, across = iota((count, count), 0), iota((count, count), 1)
    owner_col = jnp.sum(jnp.where(down == across, owner_row, 0.0), axis=1, keepdims=True)
    same = owner_col == owner_row
    rank_row = jnp.sum(jnp.where(same & (down < across), 1.0, 0.0), axis=0, keepdims=True)
    rank_col = jnp.sum(jnp.where(same & (across < down), 1.0, 0.0), axis=1, keepdims=True)
    pos_row = (owner_row * bucket + rank_row).astype(jnp.int32)
    pos_col = (owner_col * bucket + rank_col).astype(jnp.int32)
    mask = lax.axis_index("strip") * bucket if paired else 0
    pos_row_ref[...] = pos_row ^ mask
    pos_col_ref[...] = pos_col ^ mask
    shift = rows.bit_length() - 1
    left = jnp.where(
        iota((groups, count), 0) == lax.shift_right_logical(pos_row, shift),
        slot_ref[...].astype(F32),
        0.0,
    )
    right = jnp.where(iota((count, LANES), 1) == (pos_col & (rows - 1)), 1.0, 0.0)
    wanted = jnp.dot(left, right, precision=HIGHEST, preferred_element_type=F32)
    for group in range(groups):
        request_ref[group] = wanted[group : group + 1]


def prepare_kernel(token_ref, table_ref, feature_ref, half_ref, parts_ref, small_ref):
    owned, channels = feature_ref.shape
    blocks = owned // LANES
    high, low = split2(feature_ref[...])
    half_ref[:, :channels] = high
    half_ref[:, channels:] = low
    small_ref[0:1] = table_ref[7:8, 0:LANES]
    small_ref[1:2] = table_ref[7:8, LANES : 2 * LANES]
    table = jnp.where(iota((8, owned), 0) < 7, table_ref[...], 0.0)
    stacked = jnp.concatenate(
        [table[:, a * LANES : (a + 1) * LANES] for a in range(blocks)], axis=0
    )
    parts_ref[...] = jnp.concatenate(split3(stacked), axis=0)


def relay_kernel(same_ref, other_ref, *out_refs):
    lead = same_ref.shape[1]
    for m, out_ref in enumerate(out_refs):
        out_ref[0:lead] = same_ref[m]
        out_ref[lead:] = other_ref[m * lead : (m + 1) * lead]


def weights_kernel(token_ref, weights_ref, straight_ref, turned_ref):
    size = weights_ref.shape[2]
    for i in range(3):
        for j in range(3):
            block = weights_ref[i, j]
            high, low = split2(block)
            straight_ref[i, j * size : (j + 1) * size, :size] = high
            straight_ref[i, j * size : (j + 1) * size, size:] = low
            high, low = split2(block.T)
            a, b = 2 - i, 2 - j
            turned_ref[a, b * size : (b + 1) * size, :size] = high
            turned_ref[a, b * size : (b + 1) * size, size:] = low


def reply_kernel(rows, paired, asked_ref, half_ref, parts_ref, *refs):
    pick_ref = refs[-1]
    groups = asked_ref.shape[0]
    first = lax.axis_index("strip") if paired else 0
    replies = [refs[0].at[group] for group in range(refs[0].shape[0])]
    if paired:
        others = [refs[1].at[m * (rows + 8) : (m + 1) * (rows + 8)] for m in range(len(replies))]
        replies = [ref for pair in zip(replies, others) for ref in pair]
    owned = half_ref.shape[0]
    channels = half_ref.shape[1] // 2
    blocks = owned // LANES
    asked = jnp.concatenate([asked_ref[group ^ first] for group in range(groups)], axis=0)
    padded = jnp.concatenate([asked, jnp.zeros((LANES - groups, LANES), F32)], axis=0)
    columns = padded.T.astype(jnp.int32)
    place = iota((rows, owned), 1)
    for group in range(groups):
        pick_ref[group * rows : (group + 1) * rows] = onehot(
            columns[:rows, group : group + 1] == place
        )
    found = dot(pick_ref[...], half_ref[...])
    found = found[:, :channels] + found[:, channels:]
    slots = asked.astype(jnp.int32)
    slots_row = jnp.concatenate([slots[group : group + 1] for group in range(groups)], axis=1)
    wide = slots_row.shape[1]
    minor = onehot((slots_row & (LANES - 1)) == iota((LANES, wide), 0))
    product = dot(parts_ref[...], minor)
    deep = blocks * 8
    product = product[:deep] + product[deep : 2 * deep] + product[2 * deep :]
    major = lax.shift_right_logical(slots_row, 7)
    geometry = jnp.zeros((8, wide), F32)
    for a in range(blocks):
        geometry = geometry + jnp.where(major == a, product[a * 8 : (a + 1) * 8], 0.0)
    for group in range(groups):
        replies[group][0:rows] = found[group * rows : (group + 1) * rows]
        replies[group][rows : rows + 8] = geometry[:, group * LANES : (group + 1) * LANES]


def camera_at(small_ref, axis, i):
    return small_ref[0:1, 4 * axis + i : 4 * axis + i + 1]


def centers(small_ref, geometry):
    found = []
    for axis in range(2):
        found.append(
            8.0
            + 4.0
            * (
                camera_at(small_ref, axis, 0) * geometry[0:1]
                + camera_at(small_ref, axis, 1) * geometry[1:2]
                + camera_at(small_ref, axis, 2) * geometry[2:3]
                + camera_at(small_ref, axis, 3)
            )
        )
    return found


def offsets(small_ref, geometry, pixels):
    center_col, center_row = centers(small_ref, geometry)
    pixel = iota((pixels, geometry.shape[1]), 0)
    across = (pixel & (WIDTH - 1)).astype(F32) + 0.5
    downward = lax.shift_right_logical(pixel, WIDTH.bit_length() - 1).astype(F32) + 0.5
    return across - center_col, downward - center_row


def render_kernel(
    rows,
    groups,
    paired,
    length_ref,
    small_ref,
    pos_row_ref,
    pos_col_ref,
    target_ref,
    *refs,
):
    fetched = [refs[0].at[group] for group in range(groups)] if not paired else []
    for ref in refs[:-7] if paired else []:
        fetched += [ref.at[0 : rows + 8], ref.at[rows + 8 : 2 * rows + 16]]
    tile_ref, send_near_ref, send_far_ref, weight_ref, ratio_ref, geometry_ref, feature_ref = refs[-7:]
    count = pos_row_ref.shape[1]
    places = groups * rows
    pixels, channels = tile_ref.shape
    pick = onehot(pos_col_ref[...] == iota((count, places), 1))
    pick_t = onehot(pos_row_ref[...] == iota((places, count), 0))
    sent = jnp.concatenate([fetched[group][0:rows] for group in range(groups)], axis=0)
    feature = dot(pick, jnp.concatenate(split2(sent), axis=1)).astype(BF16)
    feature_ref[...] = feature
    sent = jnp.concatenate(
        [fetched[group][rows : rows + 8][:, :rows] for group in range(groups)], axis=1
    )
    geometry = dot(jnp.concatenate(split3(sent), axis=0), pick_t)
    geometry = geometry[0:8] + geometry[8:16] + geometry[16:24]
    geometry_ref[...] = geometry
    du, dv = offsets(small_ref, geometry, pixels)
    a = geometry[3:4] * du
    b = geometry[4:5] * dv
    exponent = -0.5 * (a * a + 2.0 * geometry[5:6] * a * b + b * b)
    alive = iota((1, count), 1) < length_ref[0, 0]
    sigmoid = 1.0 / (1.0 + jnp.exp(-geometry[6:7]))
    raw = sigmoid * jnp.exp(exponent)
    alpha = jnp.where(alive, jnp.minimum(raw, 0.99), 0.0)
    keep = 1.0 - alpha
    log_keep = jnp.log(keep)
    before = onehot(iota((count, count), 0) < iota((count, count), 1))
    high, low = split2(log_keep)
    weight = alpha * jnp.exp(dot(high, before) + dot(low, before))
    weight_ref[...] = weight
    ratio_ref[...] = jnp.where(raw < 0.99, alpha, 0.0) / keep
    high, low = split2(weight)
    tile = dot(high, feature)
    tile = tile[:, :channels] + tile[:, channels:] + dot(low, feature[:, :channels])
    tile_ref[...] = tile
    top = jnp.concatenate([tile[0 : 2 * WIDTH], target_ref[0:WIDTH]], axis=0)
    bottom = jnp.concatenate([tile[pixels - 2 * WIDTH :], target_ref[pixels - WIDTH : pixels]], axis=0)
    even = lax.axis_index("strip") % 2 == 0
    send_near_ref[...] = jnp.where(even, bottom, top)
    send_far_ref[...] = jnp.where(even, top, bottom)


def spread_kernel(pos_row_ref, weight_ref, spread_ref):
    places = spread_ref.shape[0]
    pixels, count = weight_ref.shape
    pick_t = onehot(pos_row_ref[...] == iota((places, count), 0))
    high, low = split2(weight_ref[...])
    spread_ref[:, :pixels] = dot_nt(pick_t, high).astype(BF16)
    spread_ref[:, pixels:] = dot_nt(pick_t, low).astype(BF16)


def shifted(value, scratch_ref):
    count = value.shape[0]
    scratch_ref[8 : 8 + count] = value
    column = iota((count, 1), 0) & (WIDTH - 1)
    left = jnp.where(column == 0, 0.0, scratch_ref[7 : 7 + count])
    right = jnp.where(column == WIDTH - 1, 0.0, scratch_ref[9 : 9 + count])
    return jnp.concatenate([left, value, right], axis=1)


def taps(wide, kernel_ref, count, channels):
    high, low = split2(wide)
    total = jnp.zeros((count, channels), F32)
    for i in range(3):
        part = dot(high[WIDTH * i : WIDTH * i + count], kernel_ref[i])
        total = total + part[:, :channels] + part[:, channels:]
        total = total + dot(low[WIDTH * i : WIDTH * i + count], kernel_ref[i][:, :channels])
    return total


def decode(tile_ref, near_ref, far_ref, target_ref, kernel_ref, small_ref, scratch_ref, sum_ref):
    pixels, channels = tile_ref.shape
    edge = 2 * WIDTH
    strip = lax.axis_index("strip")
    even = strip % 2 == 0
    near, far = near_ref[...], far_ref[...]
    above, below = jnp.where(even, far, near), jnp.where(even, near, far)
    scratch_ref[0:8] = jnp.zeros((8, channels), F32)
    padded = jnp.concatenate([above[0:edge], tile_ref[...], below[0:edge]], axis=0)
    count = pixels + 2 * WIDTH
    scratch_ref[8 + count + 2 * WIDTH : 16 + count + 2 * WIDTH] = jnp.zeros((8, channels), F32)
    wide = shifted(padded, scratch_ref)
    goal = jnp.concatenate([above[edge:], target_ref[...], below[edge:]], axis=0)
    residual = taps(wide, kernel_ref, count, channels) + small_ref[1:2] - goal
    pixel = iota((count, 1), 0)
    outside = ((pixel < WIDTH) & (strip == 0)) | (
        (pixel >= count - WIDTH) & (strip == lax.axis_size("strip") - 1)
    )
    residual = jnp.where(outside, 0.0, residual)

    own = residual[WIDTH : WIDTH + pixels]
    turned_high, turned_low = split2(own.T)
    high, low = split2(wide)
    for i in range(3):
        first = WIDTH * (1 + i)
        part = (
            dot(turned_high, high[first : first + pixels])
            + dot(turned_high, low[first : first + pixels])
            + dot(turned_low, high[first : first + pixels])
        )
        for j in range(3):
            block = (3 * i + j) * channels
            sum_ref[block : block + channels] = part[:, j * channels : (j + 1) * channels].T
    return residual, jnp.sum(own, axis=0, keepdims=True)


def back_kernel(
    rows,
    groups,
    paired,
    small_ref,
    tile_ref,
    near_ref,
    far_ref,
    target_ref,
    straight_ref,
    turned_ref,
    weight_ref,
    ratio_ref,
    geometry_ref,
    feature_ref,
    spread_ref,
    pos_col_ref,
    slot_ref,
    same_ref,
    cross_ref,
    keep_ref,
    own_bias_ref,
    scratch_ref,
    sum_ref,
):
    pixels, count = weight_ref.shape
    channels = tile_ref.shape[1]
    places = groups * rows
    lead = rows + 8
    half = keep_ref.shape[0]
    residual, bias_grad = decode(
        tile_ref, near_ref, far_ref, target_ref, straight_ref, small_ref, scratch_ref, sum_ref
    )
    start = cross_ref.shape[0] - half - 8
    bias_rows = jnp.where(iota((8, channels), 0) == 0, bias_grad, 0.0)
    own_bias_ref[...] = bias_rows
    cross_ref[start + half :] = bias_rows
    even = lax.axis_index("strip") % 2 == 0
    keep_ref[...] = jnp.where(even, sum_ref[0:half], sum_ref[half:])
    cross_ref[start : start + half] = jnp.where(even, sum_ref[half:], sum_ref[0:half])

    def put(group, first, value):
        amount = value.shape[0]
        if not paired:
            same_ref[group, first : first + amount] = value
        elif group % 2 == 0:
            same_ref[group // 2, first : first + amount] = value
        else:
            first = group // 2 * lead + first
            cross_ref[first : first + amount] = value

    extent = residual.shape[0]
    scratch_ref[8 + extent : 16 + extent] = jnp.zeros((8, channels), F32)
    wide = shifted(residual, scratch_ref)
    grad = taps(wide, turned_ref, pixels, channels)
    high, low = split2(grad)
    both = jnp.concatenate([high, low], axis=1)
    part = dot(spread_ref[:, :pixels], both)
    part = part[:, :channels] + part[:, channels:] + dot(spread_ref[:, pixels:], high)
    for group in range(groups):
        put(group, 0, part[group * rows : (group + 1) * rows])

    near, far = feature_ref[:, :channels], feature_ref[:, channels:]
    weight_grad = dot_nt(high, near) + dot_nt(high, far) + dot_nt(low, near)
    pull = weight_grad * weight_ref[...]
    behind = onehot(iota((count, count), 0) > iota((count, count), 1))
    high, low = split2(pull)
    suffix = dot(high, behind) + dot(low, behind)
    ratio = ratio_ref[...]
    change = jnp.where(ratio > 0.0, pull - ratio * suffix, 0.0)

    geometry = geometry_ref[...]
    du, dv = offsets(small_ref, geometry, pixels)

    def total(x):
        return jnp.sum(x, axis=0, keepdims=True)

    change_u, change_v = change * du, change * dv
    m, mu, mv = total(change), total(change_u), total(change_v)
    muu, muv, mvv = total(change_u * du), total(change_u * dv), total(change_v * dv)
    g3, g4, g5, g6 = (geometry[i : i + 1] for i in range(3, 7))
    center_col = g3 * (g3 * mu + g5 * g4 * mv)
    center_row = g4 * (g5 * g3 * mu + g4 * mv)
    lines = [
        4.0 * (camera_at(small_ref, 0, i) * center_col + camera_at(small_ref, 1, i) * center_row)
        for i in range(3)
    ]
    lines.append(-(g3 * muu + g5 * g4 * muv))
    lines.append(-(g4 * mvv + g5 * g3 * muv))
    lines.append(-(g3 * g4 * muv))
    lines.append(m / (1.0 + jnp.exp(g6)))
    lines.append(slot_ref[...].astype(F32))
    pick = onehot(pos_col_ref[...] == iota((count, places), 1))
    moved = dot(jnp.concatenate(split3(jnp.concatenate(lines, axis=0)), axis=0), pick)
    moved = moved[0:8] + moved[8:16] + moved[16:24]
    for group in range(groups):
        piece = moved[:, group * rows : (group + 1) * rows]
        if rows < LANES:
            piece = jnp.concatenate([piece, jnp.zeros((8, LANES - rows), F32)], axis=1)
        put(group, rows, piece)


def pack_kernel(amount, paired, *refs):
    values, parts = refs[:amount], refs[amount:-2]
    packed_ref, sum_ref = refs[-2:]
    rows = values[0].shape[0] - (8 if paired else 0)
    for place, value in enumerate(values):
        packed_ref[place * rows : (place + 1) * rows] = value[0:rows]
    if paired:
        bias_rows = values[0][rows:]
        for value in values[1:]:
            bias_rows = bias_rows + value[rows:]
        packed_ref[amount * rows :] = bias_rows
    sum_kernel(*parts, sum_ref)


def gather_rows(slot_row, half_ref, start, count):
    channels = half_ref.shape[1] // 2
    pick_t = onehot(slot_row == iota((count, half_ref.shape[0]), 0) + start)
    part = dot(pick_t, half_ref[...])
    return part[:, :channels] + part[:, channels:]


def gather_first_kernel(rows, groups, views, token_ref, *refs):
    arrived = refs[:views]
    feature_ref, half_ref, lines_ref, bias_ref = refs[views:]
    channels = feature_ref.shape[1]
    lead = rows + 8
    lines = []
    for view in range(views):
        for group in range(groups):
            first = group * lead
            piece = view * groups + group
            high, low = split2(arrived[view][first : first + rows])
            half_ref[piece * rows : (piece + 1) * rows, :channels] = high
            half_ref[piece * rows : (piece + 1) * rows, channels:] = low
            lines.append(arrived[view][first + rows : first + lead][:, :rows])
    lines = jnp.concatenate(lines, axis=1)
    lines_ref[...] = lines
    if arrived[0].shape[0] > groups * lead:
        bias = arrived[0][groups * lead : groups * lead + 1]
        for value in arrived[1:]:
            bias = bias + value[groups * lead : groups * lead + 1]
        bias_ref[...] = bias
    else:
        bias_ref[...] = jnp.zeros(bias_ref.shape, F32)
    slot_row = lines[7:8].astype(jnp.int32)
    tile = 256
    for start in range(0, feature_ref.shape[0], tile):
        feature_ref[start : start + tile] = gather_rows(slot_row, half_ref, start, tile)


def gather_second_kernel(
    token_ref,
    half_ref,
    lines_ref,
    begun_ref,
    bias_in_ref,
    feature_hbm,
    geometry_hbm,
    bias_hbm,
    end_ref,
    geometry_ref,
    out_ref,
    sems,
):
    owned = feature_hbm.shape[0]
    begun = begun_ref.shape[0]
    blocks = owned // LANES
    lines = lines_ref[...]
    amount = lines.shape[1]
    copies = [
        pltpu.make_async_copy(begun_ref, feature_hbm.at[0:begun], sems.at[0]),
        pltpu.make_async_copy(bias_in_ref, bias_hbm, sems.at[1]),
    ]
    for copy in copies:
        copy.start()
    slot_row = lines[7:8].astype(jnp.int32)
    minor = onehot((slot_row & (LANES - 1)) == iota((LANES, amount), 0))
    major = lax.shift_right_logical(slot_row, 7)
    stacked = jnp.concatenate([jnp.where(major == a, lines, 0.0) for a in range(blocks)], axis=0)
    high, low = split2(stacked)
    product = dot_nt(high, minor) + dot_nt(low, minor)
    for a in range(blocks):
        geometry_ref[:, a * LANES : (a + 1) * LANES] = product[a * 8 : a * 8 + 7]
    copies.append(pltpu.make_async_copy(geometry_ref, geometry_hbm, sems.at[2]))
    copies[-1].start()
    tile = out_ref.shape[1]
    for step, start in enumerate(range(begun, owned, tile)):
        out_ref[step] = gather_rows(slot_row, half_ref, start, tile)
        copies.append(
            pltpu.make_async_copy(
                out_ref.at[step], feature_hbm.at[start : start + tile], sems.at[3 + step]
            )
        )
        copies[-1].start()
    end_ref[...] = jnp.zeros(end_ref.shape, F32)
    for copy in copies:
        copy.wait()


def mix_kernel(pieces, same_ref, keep_ref, own_bias_ref, other_ref, *out_refs):
    parts = len(out_refs) - pieces
    rows = keep_ref.shape[0] // parts
    start = other_ref.shape[0] - keep_ref.shape[0] - 8
    bias_rows = own_bias_ref[...] + other_ref[start + keep_ref.shape[0] :]
    for m in range(pieces):
        lead = same_ref.shape[1]
        out_refs[m][0:lead] = same_ref[m]
        out_refs[m][lead : 2 * lead] = other_ref[m * lead : (m + 1) * lead]
        out_refs[m][2 * lead :] = bias_rows
    view = lax.axis_index("view")
    for m in range(parts):
        first = pl.multiple_of((view ^ m) * rows, 8)
        second = pl.multiple_of(start + (view ^ m) * rows, 8)
        out_refs[pieces + m][...] = keep_ref[pl.ds(first, rows)] + other_ref[pl.ds(second, rows)]


def sum_kernel(*refs):
    total = refs[0][...]
    for ref in refs[1:-1]:
        total = total + ref[...]
    refs[-1][...] = total


def join_kernel(token_ref, *refs):
    parts = len(refs) - 1
    rows = refs[0].shape[0]
    view = lax.axis_index("view")
    for m in range(parts):
        start = pl.multiple_of((view ^ m) * rows, 8)
        refs[-1][pl.ds(start, rows)] = refs[m][...]


def finish_kernel(token_ref, mine_ref, other_ref, kernel_hbm, sems):
    half = mine_ref.shape[0]

    def move(first, second):
        copies = [
            pltpu.make_async_copy(first, kernel_hbm.at[0:half], sems.at[0]),
            pltpu.make_async_copy(second, kernel_hbm.at[half:], sems.at[1]),
        ]
        for copy in copies:
            copy.start()
        for copy in copies:
            copy.wait()

    even = lax.axis_index("strip") % 2 == 0

    @pl.when(even)
    def _():
        move(mine_ref, other_ref)

    @pl.when(jnp.logical_not(even))
    def _():
        move(other_ref, mine_ref)


def swap(value, axis, mask):
    count = lax.axis_size(axis)
    return lax.ppermute(value, axis, [(i, i ^ mask) for i in range(count)])


def near_sum(value, axis, unit, amount):
    step = unit
    while amount > 1:
        near = 4 if amount % 4 == 0 else 2
        parts = [value] + [swap(value, axis, step * m) for m in range(1, near)]
        value = call(sum_kernel, jax.ShapeDtypeStruct(value.shape, F32), [VMEM] * near)(*parts)
        step, amount = step * near, amount // near
    return value


def per_device(
    means,
    inv_scales,
    correlation,
    opacity,
    features,
    cameras,
    owners,
    slots,
    lengths,
    target,
    weights,
    bias,
):
    shape = jax.ShapeDtypeStruct
    strips = lax.axis_size("strip")
    views = lax.axis_size("view")
    count = slots.shape[1] * slots.shape[2]
    owned, channels = features.shape
    height, breadth = target.shape[1], target.shape[2]
    pixels = height * breadth
    assert slots.shape[1] == 1 and breadth == WIDTH and channels == LANES
    bucket = max(4, 2 * count // strips)
    places = strips * bucket
    rows = bucket if bucket % 8 == 0 else 64
    groups = places // rows
    direct = rows == bucket
    paired = direct and strips <= 8
    lead = rows + 8
    wire_lead = bucket + 8

    def to_wire(value):
        if direct:
            return value
        top = value[:, :rows].reshape(strips, bucket, LANES)
        low = value[:, rows:, :rows].transpose(1, 0, 2).reshape(8, strips, bucket)
        low = jnp.pad(low.transpose(1, 0, 2), ((0, 0), (0, 0), (0, LANES - bucket)))
        return jnp.concatenate([top, low], axis=1)

    def from_wire(value):
        if direct:
            return value
        top = value[:, :bucket].reshape(groups, rows, LANES)
        low = value[:, bucket:, :bucket].transpose(1, 0, 2).reshape(8, groups, rows)
        low = jnp.pad(low.transpose(1, 0, 2), ((0, 0), (0, 0), (0, LANES - rows)))
        return jnp.concatenate([top, low], axis=1)

    def exchange(value):
        return lax.all_to_all(value, "strip", split_axis=0, concat_axis=0, tiled=True)

    goal = target.reshape(pixels, channels)

    request, pos_row, pos_col, slot_row = call(
        functools.partial(route_kernel, bucket, rows, paired),
        [
            shape((groups, 1, LANES), F32),
            shape((1, count), jnp.int32),
            shape((count, 1), jnp.int32),
            shape((1, count), jnp.int32),
        ],
        [VMEM],
    )(jnp.concatenate([owners.reshape(1, count), slots.reshape(1, count)], axis=0))
    if not direct:
        request = request[:, 0, :rows].reshape(strips, 1, bucket)
        request = jnp.pad(request, ((0, 0), (0, 0), (0, LANES - bucket)))
    asked = exchange(request)
    if not direct:
        asked = asked[:, 0, :bucket].reshape(groups, 1, rows)
        asked = jnp.pad(asked, ((0, 0), (0, 0), (0, LANES - rows)))

    table = jnp.concatenate(
        [
            means,
            inv_scales,
            correlation[None, :],
            opacity[None, :],
            jnp.concatenate(
                [
                    cameras.reshape(1, 8),
                    jnp.zeros((1, channels - 8), F32),
                    bias[None, :],
                    jnp.zeros((1, owned - 2 * channels), F32),
                ],
                axis=1,
            ),
        ],
        axis=0,
    )
    half, parts, small = call(
        prepare_kernel,
        [
            shape((owned, 2 * channels), BF16),
            shape((3 * 8 * (owned // LANES), LANES), BF16),
            shape((2, LANES), F32),
        ],
        [ANY, VMEM, VMEM],
        flops=2**33,
        moved=2**24,
    )(pos_row, table, features)
    pieces = strips // 2 if paired else 0
    replies = call(
        functools.partial(reply_kernel, rows, paired),
        [shape((pieces, lead, LANES), F32), shape((pieces * lead, LANES), F32)]
        if paired
        else [shape((groups, lead, LANES), F32)],
        [VMEM] * 3,
        [pltpu.VMEM((places, owned), BF16)],
    )(asked, half, parts)
    straight, turned = call(
        weights_kernel,
        [shape((3, 3 * channels, 2 * channels), BF16)] * 2,
        [ANY, VMEM],
        flops=2**32,
        moved=2**23,
    )(replies[0], weights)
    if paired:
        same, cross = replies
        chips = call(
            relay_kernel, [shape((2 * lead, LANES), F32)] * pieces, [VMEM] * 2
        )(same, swap(cross, "strip", 1))
        far = {m: swap(chips[m], "strip", 2 * m) for m in range(pieces - 1, 0, -1)}
        fetched = [chips[0]] + [far[m] for m in range(1, pieces)]
    else:
        fetched = [from_wire(exchange(to_wire(replies[0])))]

    tile, send_near, send_far, weight, ratio, geometry, feature = call(
        functools.partial(render_kernel, rows, groups, paired),
        [
            shape((pixels, channels), F32),
            shape((3 * WIDTH, channels), F32),
            shape((3 * WIDTH, channels), F32),
            shape((pixels, count), F32),
            shape((pixels, count), F32),
            shape((8, count), F32),
            shape((count, 2 * channels), BF16),
        ],
        [SMEM] + [VMEM] * (4 + len(fetched)),
    )(lengths, small, pos_row, pos_col, goal, *fetched)
    between = [(i, i + 1) for i in range(1, strips - 1, 2)]
    far = lax.ppermute(send_far, "strip", between + [(b, a) for a, b in between])
    near = swap(send_near, "strip", 1)
    spread = call(
        spread_kernel, shape((places, 2 * pixels), BF16), [VMEM] * 2, moved=2**21
    )(pos_row, weight)

    half = 9 * channels // 2
    assert half % (8 * views) == 0
    same, cross, keep, own_bias = call(
        functools.partial(back_kernel, rows, groups, paired),
        [
            shape((pieces if paired else groups, lead, LANES), F32),
            shape((pieces * lead + half + 8, LANES), F32),
            shape((half, channels), F32),
            shape((8, channels), F32),
        ],
        [VMEM] * 14,
        [
            pltpu.VMEM((pixels + 4 * WIDTH + 16, channels), F32),
            pltpu.VMEM((9 * channels, channels), F32),
        ],
        flops=2**30,
        moved=2**22,
    )(
        small,
        tile,
        near,
        far,
        goal,
        straight,
        turned,
        weight,
        ratio,
        geometry,
        feature,
        spread,
        pos_col,
        slot_row,
    )
    other = swap(cross, "strip", 1)
    part = shape((half // views, channels), F32)
    mixed = call(
        functools.partial(mix_kernel, pieces),
        [shape((2 * lead + 8, LANES), F32)] * pieces + [part] * views,
        [VMEM] * 4,
    )(same, keep, own_bias, other)
    if paired:
        order = range(pieces - 1, 0, -1)
        moved = {m: swap(mixed[m], "strip", 2 * m) for m in order}
        returned = [mixed[0]] + [moved[m] for m in range(1, pieces)]
    else:
        returned = [from_wire(exchange(to_wire(same))).reshape(groups * lead, LANES)]
    parts = [mixed[pieces]] + [swap(mixed[pieces + m], "view", m) for m in range(1, views)]
    length = groups * lead + (8 if paired else 0)
    packed, total = call(
        functools.partial(pack_kernel, len(returned), paired),
        [shape((length, LANES), F32), part],
        [VMEM] * (len(returned) + views),
    )(*returned, *parts)
    far = {m: swap(packed, "view", m) for m in range(views - 1, 0, -1)}
    arrived = [packed] + [far[m] for m in range(1, views)]

    total = near_sum(total, "strip", 2, strips // 2)
    parts = [total] + [swap(total, "view", m) for m in range(1, views)]
    first = owned // 2
    feature_first, rowed, lines, bias_sum = call(
        functools.partial(gather_first_kernel, rows, groups, views),
        [
            shape((first, channels), F32),
            shape((views * places, 2 * channels), BF16),
            shape((8, views * places), F32),
            shape((1, channels), F32),
        ],
        [ANY] + [VMEM] * views,
        flops=2**31,
        moved=2**22,
    )(total, *arrived)
    if not paired:
        bias_sum = lax.psum(own_bias[0:1], ("view", "strip"))
    joined = call(join_kernel, shape((half, channels), F32), [ANY] + [VMEM] * views)(lines, *parts)
    other = swap(joined, "strip", 1)
    tile = 256
    feature_grad, geometry_grad, bias_grad, end = call(
        gather_second_kernel,
        [
            shape((owned, channels), F32),
            shape((7, owned), F32),
            shape((1, channels), F32),
            shape((8, LANES), F32),
        ],
        [ANY] + [VMEM] * 4,
        [
            pltpu.VMEM((7, owned), F32),
            pltpu.VMEM(((owned - first) // tile, tile, channels), F32),
            pltpu.SemaphoreType.DMA((3 + (owned - first) // tile,)),
        ],
        out=[HBM, HBM, HBM, VMEM],
        flops=2**31,
        moved=2**22,
    )(joined, rowed, lines, feature_first, bias_sum)
    kernel_grad = call(
        finish_kernel,
        shape((9 * channels, channels), F32),
        [ANY, ANY, ANY],
        [pltpu.SemaphoreType.DMA((2,))],
        out=HBM,
    )(end, joined, other)
    return (
        geometry_grad,
        feature_grad,
        kernel_grad.reshape(weights.shape),
        bias_grad.reshape(bias.shape),
    )


def solution(mesh):
    return jax.shard_map(
        per_device,
        mesh=mesh,
        in_specs=(
            P(None, "strip"),
            P(None, "strip"),
            P("strip"),
            P("strip"),
            P("strip", None),
            P("view", None, None),
            P("view", "strip", None, None),
            P("view", "strip", None),
            P("view", "strip"),
            P("view", "strip", None, None),
            P(),
            P(),
        ),
        out_specs=(P(None, "strip"), P("strip", None), P(), P()),
        check_vma=False,
    )
```

```python
import functools

import jax
import jax.numpy as jnp
from jax import lax
from jax.experimental import pallas as pl
from jax.experimental.pallas import tpu as pltpu
from jax.sharding import PartitionSpec as P

HIGHEST = lax.Precision.HIGHEST
F32 = jnp.float32
BF16 = jnp.bfloat16
LANES = 128
WIDTH = 16
VMEM = pl.BlockSpec(memory_space=pltpu.VMEM)
SMEM = pl.BlockSpec(memory_space=pltpu.SMEM)
ANY = pl.BlockSpec(memory_space=pl.ANY)
HBM = pl.BlockSpec(memory_space=pltpu.HBM)


def iota(shape, dim):
    return lax.broadcasted_iota(jnp.int32, shape, dim)


def onehot(mask):
    return jnp.where(mask, 1.0, 0.0).astype(BF16)


def split2(x):
    high = x.astype(BF16)
    return high, (x - high.astype(F32)).astype(BF16)


def split3(x):
    high = x.astype(BF16)
    rest = x - high.astype(F32)
    middle = rest.astype(BF16)
    return high, middle, (rest - middle.astype(F32)).astype(BF16)


def dot(a, b):
    return jnp.dot(a, b, preferred_element_type=F32)


def dot_nt(a, b):
    return lax.dot_general(a, b, (((1,), (1,)), ((), ())), preferred_element_type=F32)


def call(kernel, out_shape, in_specs, scratch=(), flops=0, moved=0, out=VMEM, alias=None):
    return pl.pallas_call(
        kernel,
        out_shape=out_shape,
        in_specs=in_specs,
        out_specs=out if isinstance(out, list) else jax.tree.map(lambda _: out, out_shape),
        input_output_aliases=alias or {},
        scratch_shapes=list(scratch),
        compiler_params=pltpu.CompilerParams(vmem_limit_bytes=48 * 2**20),
        cost_estimate=pl.CostEstimate(flops=flops, bytes_accessed=moved, transcendentals=0),
    )


def route_kernel(
    bucket,
    rows,
    paired,
    entry_ref,
    request_ref,
    pos_row_ref,
    pos_col_ref,
    slot_copy_ref,
):
    owner_ref, slot_ref = entry_ref.at[0:1], entry_ref.at[1:2]
    slot_copy_ref[...] = slot_ref[...]
    groups = request_ref.shape[0]
    count = owner_ref.shape[1]
    owner_row = owner_ref[...].astype(F32)
    down, across = iota((count, count), 0), iota((count, count), 1)
    owner_col = jnp.sum(jnp.where(down == across, owner_row, 0.0), axis=1, keepdims=True)
    same = owner_col == owner_row
    rank_row = jnp.sum(jnp.where(same & (down < across), 1.0, 0.0), axis=0, keepdims=True)
    rank_col = jnp.sum(jnp.where(same & (across < down), 1.0, 0.0), axis=1, keepdims=True)
    pos_row = (owner_row * bucket + rank_row).astype(jnp.int32)
    pos_col = (owner_col * bucket + rank_col).astype(jnp.int32)
    mask = lax.axis_index("strip") * bucket if paired else 0
    pos_row_ref[...] = pos_row ^ mask
    pos_col_ref[...] = pos_col ^ mask
    shift = rows.bit_length() - 1
    left = jnp.where(
        iota((groups, count), 0) == lax.shift_right_logical(pos_row, shift),
        slot_ref[...].astype(F32),
        0.0,
    )
    right = jnp.where(iota((count, LANES), 1) == (pos_col & (rows - 1)), 1.0, 0.0)
    wanted = jnp.dot(left, right, precision=HIGHEST, preferred_element_type=F32)
    for group in range(groups):
        request_ref[group] = wanted[group : group + 1]


def prepare_kernel(token_ref, table_ref, feature_ref, half_ref, parts_ref, small_ref):
    owned, channels = feature_ref.shape
    blocks = owned // LANES
    high, low = split2(feature_ref[...])
    half_ref[:, :channels] = high
    half_ref[:, channels:] = low
    small_ref[0:1] = table_ref[7:8, 0:LANES]
    small_ref[1:2] = table_ref[7:8, LANES : 2 * LANES]
    table = jnp.where(iota((8, owned), 0) < 7, table_ref[...], 0.0)
    stacked = jnp.concatenate(
        [table[:, a * LANES : (a + 1) * LANES] for a in range(blocks)], axis=0
    )
    parts_ref[...] = jnp.concatenate(split3(stacked), axis=0)


def join_pair(same, other, out_ref):
    rows = same.shape[0] - 8
    out_ref[0:rows] = same[0:rows]
    out_ref[rows : 2 * rows] = other[0:rows]
    out_ref[2 * rows : 2 * rows + 8] = jnp.concatenate(
        [same[rows:][:, :rows], other[rows:][:, :rows]], axis=1
    )


def relay_kernel(same_ref, other_ref, *out_refs):
    lead = same_ref.shape[1]
    for m, out_ref in enumerate(out_refs):
        join_pair(same_ref[m], other_ref[m * lead : (m + 1) * lead], out_ref)


def weights_kernel(token_ref, weights_ref, straight_ref, turned_ref):
    size = weights_ref.shape[2]
    for i in range(3):
        for j in range(3):
            block = weights_ref[i, j]
            high, low = split2(block)
            straight_ref[i, j * size : (j + 1) * size, :size] = high
            straight_ref[i, j * size : (j + 1) * size, size:] = low
            high, low = split2(block.T)
            a, b = 2 - i, 2 - j
            turned_ref[a, b * size : (b + 1) * size, :size] = high
            turned_ref[a, b * size : (b + 1) * size, size:] = low


def reply_kernel(rows, paired, asked_ref, half_ref, parts_ref, *refs):
    pick_ref = refs[-1]
    groups = asked_ref.shape[0]
    first = lax.axis_index("strip") if paired else 0
    replies = [refs[0].at[group] for group in range(refs[0].shape[0])]
    if paired:
        others = [refs[1].at[m * (rows + 8) : (m + 1) * (rows + 8)] for m in range(len(replies))]
        replies = [ref for pair in zip(replies, others) for ref in pair]
    owned = half_ref.shape[0]
    channels = half_ref.shape[1] // 2
    blocks = owned // LANES
    asked = jnp.concatenate([asked_ref[group ^ first] for group in range(groups)], axis=0)
    padded = jnp.concatenate([asked, jnp.zeros((LANES - groups, LANES), F32)], axis=0)
    columns = padded.T.astype(jnp.int32)
    place = iota((rows, owned), 1)
    for group in range(groups):
        pick_ref[group * rows : (group + 1) * rows] = onehot(
            columns[:rows, group : group + 1] == place
        )
    found = dot(pick_ref[...], half_ref[...])
    found = found[:, :channels] + found[:, channels:]
    slots = asked.astype(jnp.int32)
    slots_row = jnp.concatenate([slots[group : group + 1] for group in range(groups)], axis=1)
    wide = slots_row.shape[1]
    minor = onehot((slots_row & (LANES - 1)) == iota((LANES, wide), 0))
    product = dot(parts_ref[...], minor)
    deep = blocks * 8
    product = product[:deep] + product[deep : 2 * deep] + product[2 * deep :]
    major = lax.shift_right_logical(slots_row, 7)
    geometry = jnp.zeros((8, wide), F32)
    for a in range(blocks):
        geometry = geometry + jnp.where(major == a, product[a * 8 : (a + 1) * 8], 0.0)
    for group in range(groups):
        replies[group][0:rows] = found[group * rows : (group + 1) * rows]
        replies[group][rows : rows + 8] = geometry[:, group * LANES : (group + 1) * LANES]


def camera_at(small_ref, axis, i):
    return small_ref[0:1, 4 * axis + i : 4 * axis + i + 1]


def centers(small_ref, geometry):
    found = []
    for axis in range(2):
        found.append(
            8.0
            + 4.0
            * (
                camera_at(small_ref, axis, 0) * geometry[0:1]
                + camera_at(small_ref, axis, 1) * geometry[1:2]
                + camera_at(small_ref, axis, 2) * geometry[2:3]
                + camera_at(small_ref, axis, 3)
            )
        )
    return found


def offsets(small_ref, geometry, pixels):
    center_col, center_row = centers(small_ref, geometry)
    pixel = iota((pixels, geometry.shape[1]), 0)
    across = (pixel & (WIDTH - 1)).astype(F32) + 0.5
    downward = lax.shift_right_logical(pixel, WIDTH.bit_length() - 1).astype(F32) + 0.5
    return across - center_col, downward - center_row


def render_kernel(
    rows,
    groups,
    paired,
    length_ref,
    small_ref,
    pos_row_ref,
    pos_col_ref,
    target_ref,
    *refs,
):
    received = refs[:-7][::-1]
    tile_ref, send_near_ref, send_far_ref, weight_ref, ratio_ref, geometry_ref, feature_ref = refs[-7:]
    count = pos_row_ref.shape[1]
    places = groups * rows
    pixels, channels = tile_ref.shape
    pick = onehot(pos_col_ref[...] == iota((count, places), 1))
    pick_t = onehot(pos_row_ref[...] == iota((places, count), 0))
    if paired:
        sent = jnp.concatenate([ref[0 : 2 * rows] for ref in received], axis=0)
        lines = jnp.concatenate([ref[2 * rows :] for ref in received], axis=1)
    else:
        sent = jnp.concatenate([received[0][group, 0:rows] for group in range(groups)], axis=0)
        lines = jnp.concatenate(
            [received[0][group, rows:][:, :rows] for group in range(groups)], axis=1
        )
    feature = dot(pick, jnp.concatenate(split2(sent), axis=1)).astype(BF16)
    feature_ref[...] = feature
    geometry = dot(jnp.concatenate(split3(lines), axis=0), pick_t)
    geometry = geometry[0:8] + geometry[8:16] + geometry[16:24]
    geometry_ref[...] = geometry
    du, dv = offsets(small_ref, geometry, pixels)
    a = geometry[3:4] * du
    b = geometry[4:5] * dv
    exponent = -0.5 * (a * a + 2.0 * geometry[5:6] * a * b + b * b)
    alive = iota((1, count), 1) < length_ref[0, 0]
    sigmoid = 1.0 / (1.0 + jnp.exp(-geometry[6:7]))
    raw = sigmoid * jnp.exp(exponent)
    alpha = jnp.where(alive, jnp.minimum(raw, 0.99), 0.0)
    keep = 1.0 - alpha
    log_keep = jnp.log(keep)
    before = onehot(iota((count, count), 0) < iota((count, count), 1))
    high, low = split2(log_keep)
    weight = alpha * jnp.exp(dot(high, before) + dot(low, before))
    weight_ref[...] = weight
    ratio_ref[...] = jnp.where(raw < 0.99, alpha, 0.0) / keep
    high, low = split2(weight)
    tile = dot(high, feature)
    tile = tile[:, :channels] + tile[:, channels:] + dot(low, feature[:, :channels])
    tile_ref[...] = tile
    top = jnp.concatenate([tile[0 : 2 * WIDTH], target_ref[0:WIDTH]], axis=0)
    bottom = jnp.concatenate([tile[pixels - 2 * WIDTH :], target_ref[pixels - WIDTH : pixels]], axis=0)
    even = lax.axis_index("strip") % 2 == 0
    send_near_ref[...] = jnp.where(even, bottom, top)
    send_far_ref[...] = jnp.where(even, top, bottom)


def spread_kernel(pos_row_ref, weight_ref, spread_ref):
    places = spread_ref.shape[0]
    pixels, count = weight_ref.shape
    pick_t = onehot(pos_row_ref[...] == iota((places, count), 0))
    high, low = split2(weight_ref[...])
    spread_ref[:, :pixels] = dot_nt(pick_t, high).astype(BF16)
    spread_ref[:, pixels:] = dot_nt(pick_t, low).astype(BF16)


def shifted(value, scratch_ref):
    count = value.shape[0]
    scratch_ref[8 : 8 + count] = value
    column = iota((count, 1), 0) & (WIDTH - 1)
    left = jnp.where(column == 0, 0.0, scratch_ref[7 : 7 + count])
    right = jnp.where(column == WIDTH - 1, 0.0, scratch_ref[9 : 9 + count])
    return jnp.concatenate([left, value, right], axis=1)


def taps(wide, kernel_ref, count, channels):
    high, low = split2(wide)
    total = jnp.zeros((count, channels), F32)
    for i in range(3):
        part = dot(high[WIDTH * i : WIDTH * i + count], kernel_ref[i])
        total = total + part[:, :channels] + part[:, channels:]
        total = total + dot(low[WIDTH * i : WIDTH * i + count], kernel_ref[i][:, :channels])
    return total


def decode(tile_ref, near_ref, far_ref, target_ref, kernel_ref, small_ref, scratch_ref, sum_ref):
    pixels, channels = tile_ref.shape
    edge = 2 * WIDTH
    strip = lax.axis_index("strip")
    even = strip % 2 == 0
    near, far = near_ref[...], far_ref[...]
    above, below = jnp.where(even, far, near), jnp.where(even, near, far)
    scratch_ref[0:8] = jnp.zeros((8, channels), F32)
    padded = jnp.concatenate([above[0:edge], tile_ref[...], below[0:edge]], axis=0)
    count = pixels + 2 * WIDTH
    scratch_ref[8 + count + 2 * WIDTH : 16 + count + 2 * WIDTH] = jnp.zeros((8, channels), F32)
    wide = shifted(padded, scratch_ref)
    goal = jnp.concatenate([above[edge:], target_ref[...], below[edge:]], axis=0)
    residual = taps(wide, kernel_ref, count, channels) + small_ref[1:2] - goal
    pixel = iota((count, 1), 0)
    outside = ((pixel < WIDTH) & (strip == 0)) | (
        (pixel >= count - WIDTH) & (strip == lax.axis_size("strip") - 1)
    )
    residual = jnp.where(outside, 0.0, residual)

    own = residual[WIDTH : WIDTH + pixels]
    turned_high, turned_low = split2(own.T)
    high, low = split2(wide)
    for i in range(3):
        first = WIDTH * (1 + i)
        part = (
            dot(turned_high, high[first : first + pixels])
            + dot(turned_high, low[first : first + pixels])
            + dot(turned_low, high[first : first + pixels])
        )
        for j in range(3):
            block = (3 * i + j) * channels
            sum_ref[block : block + channels] = part[:, j * channels : (j + 1) * channels].T
    return residual, jnp.sum(own, axis=0, keepdims=True)


def back_kernel(
    rows,
    groups,
    paired,
    small_ref,
    tile_ref,
    far_ref,
    near_ref,
    target_ref,
    straight_ref,
    turned_ref,
    weight_ref,
    ratio_ref,
    geometry_ref,
    feature_ref,
    spread_ref,
    pos_col_ref,
    slot_ref,
    same_ref,
    cross_ref,
    keep_ref,
    own_bias_ref,
    scratch_ref,
    sum_ref,
):
    pixels, count = weight_ref.shape
    channels = tile_ref.shape[1]
    places = groups * rows
    lead = rows + 8
    half = keep_ref.shape[0]
    residual, bias_grad = decode(
        tile_ref, near_ref, far_ref, target_ref, straight_ref, small_ref, scratch_ref, sum_ref
    )
    start = cross_ref.shape[0] - half - 8
    bias_rows = jnp.where(iota((8, channels), 0) == 0, bias_grad, 0.0)
    own_bias_ref[...] = bias_rows
    cross_ref[start + half :] = bias_rows
    even = lax.axis_index("strip") % 2 == 0
    keep_ref[...] = jnp.where(even, sum_ref[0:half], sum_ref[half:])
    cross_ref[start : start + half] = jnp.where(even, sum_ref[half:], sum_ref[0:half])

    def put(group, first, value):
        amount = value.shape[0]
        if not paired:
            same_ref[group, first : first + amount] = value
        elif group % 2 == 0:
            same_ref[group // 2, first : first + amount] = value
        else:
            first = group // 2 * lead + first
            cross_ref[first : first + amount] = value

    extent = residual.shape[0]
    scratch_ref[8 + extent : 16 + extent] = jnp.zeros((8, channels), F32)
    wide = shifted(residual, scratch_ref)
    grad = taps(wide, turned_ref, pixels, channels)
    high, low = split2(grad)
    both = jnp.concatenate([high, low], axis=1)
    part = dot(spread_ref[:, :pixels], both)
    part = part[:, :channels] + part[:, channels:] + dot(spread_ref[:, pixels:], high)
    for group in range(groups):
        put(group, 0, part[group * rows : (group + 1) * rows])

    near, far = feature_ref[:, :channels], feature_ref[:, channels:]
    weight_grad = dot_nt(high, near) + dot_nt(high, far) + dot_nt(low, near)
    pull = weight_grad * weight_ref[...]
    behind = onehot(iota((count, count), 0) > iota((count, count), 1))
    high, low = split2(pull)
    suffix = dot(high, behind) + dot(low, behind)
    ratio = ratio_ref[...]
    change = jnp.where(ratio > 0.0, pull - ratio * suffix, 0.0)

    geometry = geometry_ref[...]
    du, dv = offsets(small_ref, geometry, pixels)

    def total(x):
        return jnp.sum(x, axis=0, keepdims=True)

    change_u, change_v = change * du, change * dv
    m, mu, mv = total(change), total(change_u), total(change_v)
    muu, muv, mvv = total(change_u * du), total(change_u * dv), total(change_v * dv)
    g3, g4, g5, g6 = (geometry[i : i + 1] for i in range(3, 7))
    center_col = g3 * (g3 * mu + g5 * g4 * mv)
    center_row = g4 * (g5 * g3 * mu + g4 * mv)
    lines = [
        4.0 * (camera_at(small_ref, 0, i) * center_col + camera_at(small_ref, 1, i) * center_row)
        for i in range(3)
    ]
    lines.append(-(g3 * muu + g5 * g4 * muv))
    lines.append(-(g4 * mvv + g5 * g3 * muv))
    lines.append(-(g3 * g4 * muv))
    lines.append(m / (1.0 + jnp.exp(g6)))
    lines.append(slot_ref[...].astype(F32))
    pick = onehot(pos_col_ref[...] == iota((count, places), 1))
    moved = dot(jnp.concatenate(split3(jnp.concatenate(lines, axis=0)), axis=0), pick)
    moved = moved[0:8] + moved[8:16] + moved[16:24]
    for group in range(groups):
        piece = moved[:, group * rows : (group + 1) * rows]
        if rows < LANES:
            piece = jnp.concatenate([piece, jnp.zeros((8, LANES - rows), F32)], axis=1)
        put(group, rows, piece)


def pack_kernel(places, amount, paired, *refs):
    inputs = [refs[place] for place in places]
    values, parts = inputs[:amount], inputs[amount:]
    packed_ref, sum_ref = refs[-2:]
    rows = values[0].shape[0] - (8 if paired else 0)
    for place, value in enumerate(values):
        packed_ref[place * rows : (place + 1) * rows] = value[0:rows]
    if paired:
        bias_rows = values[0][rows:]
        for value in values[1:]:
            bias_rows = bias_rows + value[rows:]
        packed_ref[amount * rows :] = bias_rows
    sum_kernel(*parts, sum_ref)


def gather_rows(slot_row, half_ref, start, count):
    channels = half_ref.shape[1] // 2
    pick_t = onehot(slot_row == iota((count, half_ref.shape[0]), 0) + start)
    part = dot(pick_t, half_ref[...])
    return part[:, :channels] + part[:, channels:]


def gather_first_kernel(rows, groups, views, paired, token_ref, *refs):
    arrived = refs[:views]
    feature_ref, half_ref, lines_ref, bias_ref, geometry_ref = refs[views:]
    blocks = geometry_ref.shape[1] // LANES
    channels = feature_ref.shape[1]
    step = 2 * rows if paired else rows
    pieces = groups * rows // step
    amount = views * groups * rows
    lines = []
    for view in range(views):
        for group in range(pieces):
            first = group * (step + 8)
            piece = view * pieces + group
            high, low = split2(arrived[view][first : first + step])
            half_ref[piece * step : (piece + 1) * step, :channels] = high
            half_ref[piece * step : (piece + 1) * step, channels:] = low
            lines.append(arrived[view][first + step : first + step + 8][:, :step])
    lines = jnp.concatenate(lines, axis=1)
    lines_ref[...] = lines
    if paired:
        last = arrived[0].shape[0] - 8
        bias = arrived[0][last : last + 1]
        for value in arrived[1:]:
            bias = bias + value[last : last + 1]
        bias_ref[...] = bias
    else:
        bias_ref[...] = jnp.zeros(bias_ref.shape, F32)
    slot_row = lines[7:8].astype(jnp.int32)
    minor = onehot((slot_row & (LANES - 1)) == iota((LANES, amount), 0))
    major = lax.shift_right_logical(slot_row, 7)
    stacked = jnp.concatenate([jnp.where(major == a, lines, 0.0) for a in range(blocks)], axis=0)
    high, low = split2(stacked)
    product = dot_nt(high, minor) + dot_nt(low, minor)
    for a in range(blocks):
        geometry_ref[:, a * LANES : (a + 1) * LANES] = product[a * 8 : a * 8 + 7]
    tile = 256
    for start in range(0, feature_ref.shape[0], tile):
        feature_ref[start : start + tile] = gather_rows(slot_row, half_ref, start, tile)


def gather_second_kernel(
    token_ref,
    half_ref,
    lines_ref,
    begun_ref,
    bias_in_ref,
    geometry_ref,
    feature_hbm,
    geometry_hbm,
    bias_hbm,
    end_ref,
    out_ref,
    sems,
):
    owned = feature_hbm.shape[0]
    begun = begun_ref.shape[0]
    lines = lines_ref[...]
    copies = [
        pltpu.make_async_copy(geometry_ref, geometry_hbm, sems.at[2]),
        pltpu.make_async_copy(begun_ref, feature_hbm.at[0:begun], sems.at[0]),
        pltpu.make_async_copy(bias_in_ref, bias_hbm, sems.at[1]),
    ]
    for copy in copies:
        copy.start()
    slot_row = lines[7:8].astype(jnp.int32)
    tile = out_ref.shape[1]
    for step, start in enumerate(range(begun, owned, tile)):
        out_ref[step] = gather_rows(slot_row, half_ref, start, tile)
        copies.append(
            pltpu.make_async_copy(
                out_ref.at[step], feature_hbm.at[start : start + tile], sems.at[3 + step]
            )
        )
        copies[-1].start()
    end_ref[...] = jnp.zeros(end_ref.shape, F32)
    for copy in copies:
        copy.wait()


def mix_kernel(pieces, same_ref, keep_ref, own_bias_ref, other_ref, *out_refs):
    parts = len(out_refs) - pieces
    rows = keep_ref.shape[0] // parts
    start = other_ref.shape[0] - keep_ref.shape[0] - 8
    bias_rows = own_bias_ref[...] + other_ref[start + keep_ref.shape[0] :]
    for m in range(pieces):
        lead = same_ref.shape[1]
        join_pair(same_ref[m], other_ref[m * lead : (m + 1) * lead], out_refs[m])
        out_refs[m][2 * lead - 8 :] = bias_rows
    view = lax.axis_index("view")
    for m in range(parts):
        first = pl.multiple_of((view ^ m) * rows, 8)
        second = pl.multiple_of(start + (view ^ m) * rows, 8)
        out_refs[pieces + m][...] = keep_ref[pl.ds(first, rows)] + other_ref[pl.ds(second, rows)]


def sum_kernel(*refs):
    total = refs[0][...]
    for ref in refs[1:-1]:
        total = total + ref[...]
    refs[-1][...] = total


def join_kernel(token_ref, *refs):
    parts = len(refs) - 1
    rows = refs[0].shape[0]
    view = lax.axis_index("view")
    for m in range(parts):
        start = pl.multiple_of((view ^ m) * rows, 8)
        refs[-1][pl.ds(start, rows)] = refs[m][...]


def finish_kernel(token_ref, mine_ref, other_ref, kernel_hbm, sems):
    half = mine_ref.shape[0]

    def move(first, second):
        copies = [
            pltpu.make_async_copy(first, kernel_hbm.at[0:half], sems.at[0]),
            pltpu.make_async_copy(second, kernel_hbm.at[half:], sems.at[1]),
        ]
        for copy in copies:
            copy.start()
        for copy in copies:
            copy.wait()

    even = lax.axis_index("strip") % 2 == 0

    @pl.when(even)
    def _():
        move(mine_ref, other_ref)

    @pl.when(jnp.logical_not(even))
    def _():
        move(other_ref, mine_ref)


def swap(value, axis, mask):
    count = lax.axis_size(axis)
    return lax.ppermute(value, axis, [(i, i ^ mask) for i in range(count)])


def near_sum(value, axis, unit, amount):
    step = unit
    while amount > 1:
        near = 4 if amount % 4 == 0 else 2
        parts = [value] + [swap(value, axis, step * m) for m in ((2, 3, 1) if near == 4 else (1,))]
        value = call(sum_kernel, jax.ShapeDtypeStruct(value.shape, F32), [VMEM] * near)(*parts)
        step, amount = step * near, amount // near
    return value


def per_device(
    means,
    inv_scales,
    correlation,
    opacity,
    features,
    cameras,
    owners,
    slots,
    lengths,
    target,
    weights,
    bias,
):
    shape = jax.ShapeDtypeStruct
    strips = lax.axis_size("strip")
    views = lax.axis_size("view")
    count = slots.shape[1] * slots.shape[2]
    owned, channels = features.shape
    height, breadth = target.shape[1], target.shape[2]
    pixels = height * breadth
    assert slots.shape[1] == 1 and breadth == WIDTH and channels == LANES
    bucket = max(4, 2 * count // strips)
    places = strips * bucket
    rows = bucket if bucket % 8 == 0 else 64
    groups = places // rows
    direct = rows == bucket
    paired = direct and strips <= 8 and 2 * rows == LANES
    lead = rows + 8
    wire_lead = bucket + 8

    def to_wire(value):
        if direct:
            return value
        top = value[:, :rows].reshape(strips, bucket, LANES)
        low = value[:, rows:, :rows].transpose(1, 0, 2).reshape(8, strips, bucket)
        low = jnp.pad(low.transpose(1, 0, 2), ((0, 0), (0, 0), (0, LANES - bucket)))
        return jnp.concatenate([top, low], axis=1)

    def from_wire(value):
        if direct:
            return value
        top = value[:, :bucket].reshape(groups, rows, LANES)
        low = value[:, bucket:, :bucket].transpose(1, 0, 2).reshape(8, groups, rows)
        low = jnp.pad(low.transpose(1, 0, 2), ((0, 0), (0, 0), (0, LANES - rows)))
        return jnp.concatenate([top, low], axis=1)

    def exchange(value):
        return lax.all_to_all(value, "strip", split_axis=0, concat_axis=0, tiled=True)

    goal = target.reshape(pixels, channels)

    request, pos_row, pos_col, slot_row = call(
        functools.partial(route_kernel, bucket, rows, paired),
        [
            shape((groups, 1, LANES), F32),
            shape((1, count), jnp.int32),
            shape((count, 1), jnp.int32),
            shape((1, count), jnp.int32),
        ],
        [VMEM],
    )(jnp.concatenate([owners.reshape(1, count), slots.reshape(1, count)], axis=0))
    if not direct:
        request = request[:, 0, :rows].reshape(strips, 1, bucket)
        request = jnp.pad(request, ((0, 0), (0, 0), (0, LANES - bucket)))
    asked = exchange(request)
    if not direct:
        asked = asked[:, 0, :bucket].reshape(groups, 1, rows)
        asked = jnp.pad(asked, ((0, 0), (0, 0), (0, LANES - rows)))

    table = jnp.concatenate(
        [
            means,
            inv_scales,
            correlation[None, :],
            opacity[None, :],
            jnp.concatenate(
                [
                    cameras.reshape(1, 8),
                    jnp.zeros((1, channels - 8), F32),
                    bias[None, :],
                    jnp.zeros((1, owned - 2 * channels), F32),
                ],
                axis=1,
            ),
        ],
        axis=0,
    )
    half, parts, small = call(
        prepare_kernel,
        [
            shape((owned, 2 * channels), BF16),
            shape((3 * 8 * (owned // LANES), LANES), BF16),
            shape((2, LANES), F32),
        ],
        [ANY, VMEM, VMEM],
        flops=2**33,
        moved=2**24,
    )(pos_row, table, features)
    pieces = strips // 2 if paired else 0
    replies = call(
        functools.partial(reply_kernel, rows, paired),
        [shape((pieces, lead, LANES), F32), shape((pieces * lead, LANES), F32)]
        if paired
        else [shape((groups, lead, LANES), F32)],
        [VMEM] * 3,
        [pltpu.VMEM((places, owned), BF16)],
    )(asked, half, parts)
    straight, turned = call(
        weights_kernel,
        [shape((3, 3 * channels, 2 * channels), BF16)] * 2,
        [ANY, VMEM],
        flops=2**32,
        moved=2**23,
    )(replies[0], weights)
    if paired:
        same, cross = replies
        chips = call(
            relay_kernel, [shape((2 * lead - 8, LANES), F32)] * pieces, [VMEM] * 2
        )(same, swap(cross, "strip", 1))
        far = {m: swap(chips[m], "strip", 2 * m) for m in range(pieces - 1, 0, -1)}
        fetched = [far[m] for m in range(pieces - 1, 0, -1)] + [chips[0]]
    else:
        fetched = [from_wire(exchange(to_wire(replies[0])))]

    tile, send_near, send_far, weight, ratio, geometry, feature = call(
        functools.partial(render_kernel, rows, groups, paired),
        [
            shape((pixels, channels), F32),
            shape((3 * WIDTH, channels), F32),
            shape((3 * WIDTH, channels), F32),
            shape((pixels, count), F32),
            shape((pixels, count), F32),
            shape((8, count), F32),
            shape((count, 2 * channels), BF16),
        ],
        [SMEM] + [VMEM] * (4 + len(fetched)),
    )(lengths, small, pos_row, pos_col, goal, *fetched)
    between = [(i, i + 1) for i in range(1, strips - 1, 2)]
    far = lax.ppermute(send_far, "strip", between + [(b, a) for a, b in between])
    near = swap(send_near, "strip", 1)
    spread = call(
        spread_kernel, shape((places, 2 * pixels), BF16), [VMEM] * 2, moved=2**21
    )(pos_row, weight)

    half = 9 * channels // 2
    assert half % (8 * views) == 0
    same, cross, keep, own_bias = call(
        functools.partial(back_kernel, rows, groups, paired),
        [
            shape((pieces if paired else groups, lead, LANES), F32),
            shape((pieces * lead + half + 8, LANES), F32),
            shape((half, channels), F32),
            shape((8, channels), F32),
        ],
        [VMEM] * 14,
        [
            pltpu.VMEM((pixels + 4 * WIDTH + 16, channels), F32),
            pltpu.VMEM((9 * channels, channels), F32),
        ],
        flops=2**30,
        moved=2**22,
    )(
        small,
        tile,
        far,
        near,
        goal,
        straight,
        turned,
        weight,
        ratio,
        geometry,
        feature,
        spread,
        pos_col,
        slot_row,
    )
    other = swap(cross, "strip", 1)
    part = shape((half // views, channels), F32)
    mixed = call(
        functools.partial(mix_kernel, pieces),
        [shape((2 * lead, LANES), F32)] * pieces + [part] * views,
        [VMEM] * 4,
    )(same, keep, own_bias, other)
    if paired:
        order = range(pieces - 1, 0, -1)
        moved = {m: swap(mixed[m], "strip", 2 * m) for m in order}
        returned = [moved[m] for m in order] + [mixed[0]]
    else:
        returned = [from_wire(exchange(to_wire(same))).reshape(groups * lead, LANES)]
    parts = [mixed[pieces]] + [swap(mixed[pieces + m], "view", m) for m in range(1, views)]
    length = pieces * (2 * lead - 8) + 8 if paired else groups * lead
    inputs = returned + parts
    issue = list(range(len(inputs)))
    if paired and pieces == 4 and views == 4:
        issue = [5, 0, 1, 7, 2, 6, 3, 4]
    packed, total = call(
        functools.partial(pack_kernel, [issue.index(i) for i in range(len(issue))], len(returned), paired),
        [shape((length, LANES), F32), part],
        [VMEM] * len(inputs),
    )(*[inputs[i] for i in issue])
    far = {m: swap(packed, "view", m) for m in range(views - 1, 0, -1)}
    arrived = [packed] + [far[m] for m in range(1, views)]

    total = near_sum(total, "strip", 2, strips // 2)
    parts = [total] + [swap(total, "view", m) for m in range(1, views)]
    first = owned // 2
    feature_first, rowed, lines, bias_sum, geometry_sum = call(
        functools.partial(gather_first_kernel, rows, groups, views, paired),
        [
            shape((first, channels), F32),
            shape((views * places, 2 * channels), BF16),
            shape((8, views * places), F32),
            shape((1, channels), F32),
            shape((7, owned), F32),
        ],
        [ANY] + [VMEM] * views,
        flops=2**31,
        moved=2**22,
    )(total, *arrived)
    if not paired:
        bias_sum = lax.psum(own_bias[0:1], ("view", "strip"))
    joined = call(join_kernel, shape((half, channels), F32), [ANY] + [VMEM] * views)(lines, *parts)
    other = swap(joined, "strip", 1)
    tile = 256
    feature_grad, geometry_grad, bias_grad, end = call(
        gather_second_kernel,
        [
            shape((owned, channels), F32),
            shape((7, owned), F32),
            shape((1, channels), F32),
            shape((8, LANES), F32),
        ],
        [ANY] + [VMEM] * 5,
        [
            pltpu.VMEM(((owned - first) // tile, tile, channels), F32),
            pltpu.SemaphoreType.DMA((3 + (owned - first) // tile,)),
        ],
        out=[HBM, HBM, HBM, VMEM],
        flops=2**31,
        moved=2**22,
    )(joined, rowed, lines, feature_first, bias_sum, geometry_sum)
    kernel_grad = call(
        finish_kernel,
        shape((9 * channels, channels), F32),
        [ANY, ANY, ANY],
        [pltpu.SemaphoreType.DMA((2,))],
        out=HBM,
    )(end, joined, other)
    return (
        geometry_grad,
        feature_grad,
        kernel_grad.reshape(weights.shape),
        bias_grad.reshape(bias.shape),
    )


def solution(mesh):
    return jax.shard_map(
        per_device,
        mesh=mesh,
        in_specs=(
            P(None, "strip"),
            P(None, "strip"),
            P("strip"),
            P("strip"),
            P("strip", None),
            P("view", None, None),
            P("view", "strip", None, None),
            P("view", "strip", None),
            P("view", "strip"),
            P("view", "strip", None, None),
            P(),
            P(),
        ),
        out_specs=(P(None, "strip"), P("strip", None), P(), P()),
        check_vma=False,
    )
```

```python
import functools

import jax
import jax.numpy as jnp
from jax import lax
from jax.experimental import pallas as pl
from jax.experimental.pallas import tpu as pltpu
from jax.sharding import PartitionSpec as P

HIGHEST = lax.Precision.HIGHEST
F32 = jnp.float32
BF16 = jnp.bfloat16
LANES = 128
WIDTH = 16
VMEM = pl.BlockSpec(memory_space=pltpu.VMEM)
SMEM = pl.BlockSpec(memory_space=pltpu.SMEM)
ANY = pl.BlockSpec(memory_space=pl.ANY)
HBM = pl.BlockSpec(memory_space=pltpu.HBM)


def iota(shape, dim):
    return lax.broadcasted_iota(jnp.int32, shape, dim)


def onehot(mask):
    return jnp.where(mask, 1.0, 0.0).astype(BF16)


def split2(x):
    high = x.astype(BF16)
    return high, (x - high.astype(F32)).astype(BF16)


def split3(x):
    high = x.astype(BF16)
    rest = x - high.astype(F32)
    middle = rest.astype(BF16)
    return high, middle, (rest - middle.astype(F32)).astype(BF16)


def dot(a, b):
    return jnp.dot(a, b, preferred_element_type=F32)


def dot_nt(a, b):
    return lax.dot_general(a, b, (((1,), (1,)), ((), ())), preferred_element_type=F32)


def call(kernel, out_shape, in_specs, scratch=(), flops=0, moved=0, out=VMEM, alias=None):
    return pl.pallas_call(
        kernel,
        out_shape=out_shape,
        in_specs=in_specs,
        out_specs=out if isinstance(out, list) else jax.tree.map(lambda _: out, out_shape),
        input_output_aliases=alias or {},
        scratch_shapes=list(scratch),
        compiler_params=pltpu.CompilerParams(vmem_limit_bytes=48 * 2**20),
        cost_estimate=pl.CostEstimate(flops=flops, bytes_accessed=moved, transcendentals=0),
    )


def route_kernel(
    bucket,
    rows,
    paired,
    groups,
    entry_ref,
    pos_row_ref,
    pos_col_ref,
    slot_copy_ref,
    *refs,
):
    owner_ref, slot_ref = entry_ref.at[0:1], entry_ref.at[1:2]
    slot_copy_ref[...] = slot_ref[...]
    count = owner_ref.shape[1]
    owner_row = owner_ref[...].astype(F32)
    down, across = iota((count, count), 0), iota((count, count), 1)
    owner_col = jnp.sum(jnp.where(down == across, owner_row, 0.0), axis=1, keepdims=True)
    same = owner_col == owner_row
    rank_row = jnp.sum(jnp.where(same & (down < across), 1.0, 0.0), axis=0, keepdims=True)
    rank_col = jnp.sum(jnp.where(same & (across < down), 1.0, 0.0), axis=1, keepdims=True)
    pos_row = (owner_row * bucket + rank_row).astype(jnp.int32)
    pos_col = (owner_col * bucket + rank_col).astype(jnp.int32)
    mask = lax.axis_index("strip") * bucket if paired else 0
    pos_row, pos_col = pos_row ^ mask, pos_col ^ mask
    pos_row_ref[...] = pos_row
    pos_col_ref[...] = pos_col
    shift = rows.bit_length() - 1
    left = jnp.where(
        iota((groups, count), 0) == lax.shift_right_logical(pos_row, shift),
        slot_ref[...].astype(F32),
        0.0,
    )
    right = jnp.where(iota((count, LANES), 1) == (pos_col & (rows - 1)), 1.0, 0.0)
    wanted = jnp.dot(left, right, precision=HIGHEST, preferred_element_type=F32)
    for group in range(groups):
        if paired:
            refs[group % 2][group // 2 : group // 2 + 1] = wanted[group : group + 1]
        else:
            refs[0][group] = wanted[group : group + 1]


def ask_kernel(same_ref, other_ref, *out_refs):
    for m, out_ref in enumerate(out_refs):
        out_ref[0:1] = same_ref[m : m + 1]
        out_ref[1:2] = other_ref[m : m + 1]


def prepare_kernel(token_ref, table_ref, feature_ref, half_ref, parts_ref):
    owned, channels = feature_ref.shape
    blocks = owned // LANES
    high, low = split2(feature_ref[...])
    half_ref[:, :channels] = high
    half_ref[:, channels:] = low
    table = jnp.concatenate([table_ref[...], jnp.zeros((1, owned), F32)], axis=0)
    stacked = jnp.concatenate(
        [table[:, a * LANES : (a + 1) * LANES] for a in range(blocks)], axis=0
    )
    parts_ref[...] = jnp.concatenate(split3(stacked), axis=0)


def join_pair(same, other, out_ref):
    rows = same.shape[0] - 8
    out_ref[0:rows] = same[0:rows]
    out_ref[rows : 2 * rows] = other[0:rows]
    out_ref[2 * rows : 2 * rows + 8] = jnp.concatenate(
        [same[rows:][:, :rows], other[rows:][:, :rows]], axis=1
    )


def relay_kernel(same_ref, other_ref, *out_refs):
    lead = same_ref.shape[1]
    for m, out_ref in enumerate(out_refs):
        join_pair(same_ref[m], other_ref[m * lead : (m + 1) * lead], out_ref)


def weights_kernel(token_ref, weights_ref, straight_ref, turned_ref):
    size = weights_ref.shape[2]
    for i in range(3):
        for j in range(3):
            block = weights_ref[i, j]
            high, low = split2(block)
            straight_ref[i, j * size : (j + 1) * size, :size] = high
            straight_ref[i, j * size : (j + 1) * size, size:] = low
            high, low = split2(block.T)
            a, b = 2 - i, 2 - j
            turned_ref[a, b * size : (b + 1) * size, :size] = high
            turned_ref[a, b * size : (b + 1) * size, size:] = low


def reply_kernel(rows, paired, groups, half_ref, parts_ref, *refs):
    pick_ref = refs[-1]
    if paired:
        asked = jnp.concatenate([ref[0:2] for ref in refs[: groups // 2][::-1]], axis=0)
        refs = refs[groups // 2 :]
    else:
        asked = jnp.concatenate([refs[0][group] for group in range(groups)], axis=0)
        refs = refs[1:]
    replies = [refs[0].at[group] for group in range(refs[0].shape[0])]
    if paired:
        others = [refs[1].at[m * (rows + 8) : (m + 1) * (rows + 8)] for m in range(len(replies))]
        replies = [ref for pair in zip(replies, others) for ref in pair]
    owned = half_ref.shape[0]
    channels = half_ref.shape[1] // 2
    blocks = owned // LANES
    padded = jnp.concatenate([asked, jnp.zeros((LANES - groups, LANES), F32)], axis=0)
    columns = padded.T.astype(jnp.int32)
    place = iota((rows, owned), 1)
    for group in range(groups):
        pick_ref[group * rows : (group + 1) * rows] = onehot(
            columns[:rows, group : group + 1] == place
        )
    found = dot(pick_ref[...], half_ref[...])
    found = found[:, :channels] + found[:, channels:]
    slots = asked.astype(jnp.int32)
    slots_row = jnp.concatenate([slots[group : group + 1] for group in range(groups)], axis=1)
    wide = slots_row.shape[1]
    minor = onehot((slots_row & (LANES - 1)) == iota((LANES, wide), 0))
    product = dot(parts_ref[...], minor)
    deep = blocks * 8
    product = product[:deep] + product[deep : 2 * deep] + product[2 * deep :]
    major = lax.shift_right_logical(slots_row, 7)
    geometry = jnp.zeros((8, wide), F32)
    for a in range(blocks):
        geometry = geometry + jnp.where(major == a, product[a * 8 : (a + 1) * 8], 0.0)
    for group in range(groups):
        replies[group][0:rows] = found[group * rows : (group + 1) * rows]
        replies[group][rows : rows + 8] = geometry[:, group * LANES : (group + 1) * LANES]


def camera_at(small_ref, axis, i):
    return small_ref[0:1, 4 * axis + i : 4 * axis + i + 1]


def centers(small_ref, geometry):
    found = []
    for axis in range(2):
        found.append(
            8.0
            + 4.0
            * (
                camera_at(small_ref, axis, 0) * geometry[0:1]
                + camera_at(small_ref, axis, 1) * geometry[1:2]
                + camera_at(small_ref, axis, 2) * geometry[2:3]
                + camera_at(small_ref, axis, 3)
            )
        )
    return found


def offsets(small_ref, geometry, pixels):
    center_col, center_row = centers(small_ref, geometry)
    pixel = iota((pixels, geometry.shape[1]), 0)
    across = (pixel & (WIDTH - 1)).astype(F32) + 0.5
    downward = lax.shift_right_logical(pixel, WIDTH.bit_length() - 1).astype(F32) + 0.5
    return across - center_col, downward - center_row


def render_kernel(
    rows,
    groups,
    paired,
    length_ref,
    small_ref,
    pos_row_ref,
    pos_col_ref,
    target_ref,
    *refs,
):
    received = refs[:-7][::-1]
    tile_ref, send_near_ref, send_far_ref, weight_ref, ratio_ref, geometry_ref, feature_ref = refs[-7:]
    count = pos_row_ref.shape[1]
    places = groups * rows
    pixels, channels = tile_ref.shape
    pick = onehot(pos_col_ref[...] == iota((count, places), 1))
    pick_t = onehot(pos_row_ref[...] == iota((places, count), 0))
    if paired:
        sent = jnp.concatenate([ref[0 : 2 * rows] for ref in received], axis=0)
        lines = jnp.concatenate([ref[2 * rows :] for ref in received], axis=1)
    else:
        sent = jnp.concatenate([received[0][group, 0:rows] for group in range(groups)], axis=0)
        lines = jnp.concatenate(
            [received[0][group, rows:][:, :rows] for group in range(groups)], axis=1
        )
    feature = dot(pick, jnp.concatenate(split2(sent), axis=1)).astype(BF16)
    feature_ref[...] = feature
    geometry = dot(jnp.concatenate(split3(lines), axis=0), pick_t)
    geometry = geometry[0:8] + geometry[8:16] + geometry[16:24]
    geometry_ref[...] = geometry
    du, dv = offsets(small_ref, geometry, pixels)
    a = geometry[3:4] * du
    b = geometry[4:5] * dv
    exponent = -0.5 * (a * a + 2.0 * geometry[5:6] * a * b + b * b)
    alive = iota((1, count), 1) < length_ref[0, 0]
    sigmoid = 1.0 / (1.0 + jnp.exp(-geometry[6:7]))
    raw = sigmoid * jnp.exp(exponent)
    alpha = jnp.where(alive, jnp.minimum(raw, 0.99), 0.0)
    keep = 1.0 - alpha
    log_keep = jnp.log(keep)
    before = onehot(iota((count, count), 0) < iota((count, count), 1))
    high, low = split2(log_keep)
    weight = alpha * jnp.exp(dot(high, before) + dot(low, before))
    weight_ref[...] = weight
    ratio_ref[...] = jnp.where(raw < 0.99, alpha, 0.0) / keep
    high, low = split2(weight)
    tile = dot(high, feature)
    tile = tile[:, :channels] + tile[:, channels:] + dot(low, feature[:, :channels])
    tile_ref[...] = tile
    top = jnp.concatenate([tile[0 : 2 * WIDTH], target_ref[0:WIDTH]], axis=0)
    bottom = jnp.concatenate([tile[pixels - 2 * WIDTH :], target_ref[pixels - WIDTH : pixels]], axis=0)
    even = lax.axis_index("strip") % 2 == 0
    send_near_ref[...] = jnp.where(even, bottom, top)
    send_far_ref[...] = jnp.where(even, top, bottom)


def spread_kernel(pos_row_ref, weight_ref, spread_ref):
    places = spread_ref.shape[0]
    pixels, count = weight_ref.shape
    pick_t = onehot(pos_row_ref[...] == iota((places, count), 0))
    high, low = split2(weight_ref[...])
    spread_ref[:, :pixels] = dot_nt(pick_t, high).astype(BF16)
    spread_ref[:, pixels:] = dot_nt(pick_t, low).astype(BF16)


def shifted(value, scratch_ref):
    count = value.shape[0]
    scratch_ref[8 : 8 + count] = value
    column = iota((count, 1), 0) & (WIDTH - 1)
    left = jnp.where(column == 0, 0.0, scratch_ref[7 : 7 + count])
    right = jnp.where(column == WIDTH - 1, 0.0, scratch_ref[9 : 9 + count])
    return jnp.concatenate([left, value, right], axis=1)


def taps(wide, kernel_ref, count, channels):
    high, low = split2(wide)
    total = jnp.zeros((count, channels), F32)
    for i in range(3):
        part = dot(high[WIDTH * i : WIDTH * i + count], kernel_ref[i])
        total = total + part[:, :channels] + part[:, channels:]
        total = total + dot(low[WIDTH * i : WIDTH * i + count], kernel_ref[i][:, :channels])
    return total


def decode(tile_ref, near_ref, far_ref, target_ref, kernel_ref, small_ref, scratch_ref, sum_ref):
    pixels, channels = tile_ref.shape
    edge = 2 * WIDTH
    strip = lax.axis_index("strip")
    even = strip % 2 == 0
    near, far = near_ref[...], far_ref[...]
    above, below = jnp.where(even, far, near), jnp.where(even, near, far)
    scratch_ref[0:8] = jnp.zeros((8, channels), F32)
    padded = jnp.concatenate([above[0:edge], tile_ref[...], below[0:edge]], axis=0)
    count = pixels + 2 * WIDTH
    scratch_ref[8 + count + 2 * WIDTH : 16 + count + 2 * WIDTH] = jnp.zeros((8, channels), F32)
    wide = shifted(padded, scratch_ref)
    goal = jnp.concatenate([above[edge:], target_ref[...], below[edge:]], axis=0)
    residual = taps(wide, kernel_ref, count, channels) + small_ref[1:2] - goal
    pixel = iota((count, 1), 0)
    outside = ((pixel < WIDTH) & (strip == 0)) | (
        (pixel >= count - WIDTH) & (strip == lax.axis_size("strip") - 1)
    )
    residual = jnp.where(outside, 0.0, residual)

    own = residual[WIDTH : WIDTH + pixels]
    turned_high, turned_low = split2(own.T)
    high, low = split2(wide)
    for i in range(3):
        first = WIDTH * (1 + i)
        part = (
            dot(turned_high, high[first : first + pixels])
            + dot(turned_high, low[first : first + pixels])
            + dot(turned_low, high[first : first + pixels])
        )
        for j in range(3):
            block = (3 * i + j) * channels
            sum_ref[block : block + channels] = part[:, j * channels : (j + 1) * channels].T
    return residual, jnp.sum(own, axis=0, keepdims=True)


def back_kernel(
    rows,
    groups,
    paired,
    small_ref,
    tile_ref,
    far_ref,
    near_ref,
    target_ref,
    straight_ref,
    turned_ref,
    weight_ref,
    ratio_ref,
    geometry_ref,
    feature_ref,
    spread_ref,
    pos_col_ref,
    slot_ref,
    same_ref,
    cross_ref,
    keep_ref,
    own_bias_ref,
    scratch_ref,
    sum_ref,
):
    pixels, count = weight_ref.shape
    channels = tile_ref.shape[1]
    places = groups * rows
    lead = rows + 8
    half = keep_ref.shape[0]
    residual, bias_grad = decode(
        tile_ref, near_ref, far_ref, target_ref, straight_ref, small_ref, scratch_ref, sum_ref
    )
    start = cross_ref.shape[0] - half - 8
    bias_rows = jnp.where(iota((8, channels), 0) == 0, bias_grad, 0.0)
    own_bias_ref[...] = bias_rows
    cross_ref[start + half :] = bias_rows
    even = lax.axis_index("strip") % 2 == 0
    keep_ref[...] = jnp.where(even, sum_ref[0:half], sum_ref[half:])
    cross_ref[start : start + half] = jnp.where(even, sum_ref[half:], sum_ref[0:half])

    def put(group, first, value):
        amount = value.shape[0]
        if not paired:
            same_ref[group, first : first + amount] = value
        elif group % 2 == 0:
            same_ref[group // 2, first : first + amount] = value
        else:
            first = group // 2 * lead + first
            cross_ref[first : first + amount] = value

    extent = residual.shape[0]
    scratch_ref[8 + extent : 16 + extent] = jnp.zeros((8, channels), F32)
    wide = shifted(residual, scratch_ref)
    grad = taps(wide, turned_ref, pixels, channels)
    high, low = split2(grad)
    both = jnp.concatenate([high, low], axis=1)
    part = dot(spread_ref[:, :pixels], both)
    part = part[:, :channels] + part[:, channels:] + dot(spread_ref[:, pixels:], high)
    for group in range(groups):
        put(group, 0, part[group * rows : (group + 1) * rows])

    near, far = feature_ref[:, :channels], feature_ref[:, channels:]
    weight_grad = dot_nt(high, near) + dot_nt(high, far) + dot_nt(low, near)
    pull = weight_grad * weight_ref[...]
    behind = onehot(iota((count, count), 0) > iota((count, count), 1))
    high, low = split2(pull)
    suffix = dot(high, behind) + dot(low, behind)
    ratio = ratio_ref[...]
    change = jnp.where(ratio > 0.0, pull - ratio * suffix, 0.0)

    geometry = geometry_ref[...]
    du, dv = offsets(small_ref, geometry, pixels)

    def total(x):
        return jnp.sum(x, axis=0, keepdims=True)

    change_u, change_v = change * du, change * dv
    m, mu, mv = total(change), total(change_u), total(change_v)
    muu, muv, mvv = total(change_u * du), total(change_u * dv), total(change_v * dv)
    g3, g4, g5, g6 = (geometry[i : i + 1] for i in range(3, 7))
    center_col = g3 * (g3 * mu + g5 * g4 * mv)
    center_row = g4 * (g5 * g3 * mu + g4 * mv)
    lines = [
        4.0 * (camera_at(small_ref, 0, i) * center_col + camera_at(small_ref, 1, i) * center_row)
        for i in range(3)
    ]
    lines.append(-(g3 * muu + g5 * g4 * muv))
    lines.append(-(g4 * mvv + g5 * g3 * muv))
    lines.append(-(g3 * g4 * muv))
    lines.append(m / (1.0 + jnp.exp(g6)))
    lines.append(slot_ref[...].astype(F32))
    pick = onehot(pos_col_ref[...] == iota((count, places), 1))
    moved = dot(jnp.concatenate(split3(jnp.concatenate(lines, axis=0)), axis=0), pick)
    moved = moved[0:8] + moved[8:16] + moved[16:24]
    for group in range(groups):
        piece = moved[:, group * rows : (group + 1) * rows]
        if rows < LANES:
            piece = jnp.concatenate([piece, jnp.zeros((8, LANES - rows), F32)], axis=1)
        put(group, rows, piece)


def pack_kernel(places, amount, paired, *refs):
    inputs = [refs[place] for place in places]
    values, parts = inputs[:amount], inputs[amount:]
    packed_ref, sum_ref = refs[-2:]
    rows = values[0].shape[0] - (8 if paired else 0)
    for place, value in enumerate(values):
        packed_ref[place * rows : (place + 1) * rows] = value[0:rows]
    if paired:
        bias_rows = values[0][rows:]
        for value in values[1:]:
            bias_rows = bias_rows + value[rows:]
        packed_ref[amount * rows :] = bias_rows
    sum_kernel(*parts, sum_ref)


def gather_rows(slot_row, half_ref, start, count):
    channels = half_ref.shape[1] // 2
    pick_t = onehot(slot_row == iota((count, half_ref.shape[0]), 0) + start)
    part = dot(pick_t, half_ref[...])
    return part[:, :channels] + part[:, channels:]


def gather_first_kernel(rows, groups, views, paired, token_ref, *refs):
    arrived = refs[:views]
    feature_ref, half_ref, lines_ref, bias_ref, geometry_ref = refs[views:]
    blocks = geometry_ref.shape[1] // LANES
    channels = feature_ref.shape[1]
    step = 2 * rows if paired else rows
    pieces = groups * rows // step
    amount = views * groups * rows
    lines = []
    for view in range(views):
        for group in range(pieces):
            first = group * (step + 8)
            piece = view * pieces + group
            high, low = split2(arrived[view][first : first + step])
            half_ref[piece * step : (piece + 1) * step, :channels] = high
            half_ref[piece * step : (piece + 1) * step, channels:] = low
            lines.append(arrived[view][first + step : first + step + 8][:, :step])
    lines = jnp.concatenate(lines, axis=1)
    lines_ref[...] = lines
    if paired:
        last = arrived[0].shape[0] - 8
        bias = arrived[0][last : last + 1]
        for value in arrived[1:]:
            bias = bias + value[last : last + 1]
        bias_ref[...] = bias
    else:
        bias_ref[...] = jnp.zeros(bias_ref.shape, F32)
    slot_row = lines[7:8].astype(jnp.int32)
    minor = onehot((slot_row & (LANES - 1)) == iota((LANES, amount), 0))
    major = lax.shift_right_logical(slot_row, 7)
    stacked = jnp.concatenate([jnp.where(major == a, lines, 0.0) for a in range(blocks)], axis=0)
    high, low = split2(stacked)
    product = dot_nt(high, minor) + dot_nt(low, minor)
    for a in range(blocks):
        geometry_ref[:, a * LANES : (a + 1) * LANES] = product[a * 8 : a * 8 + 7]
    tile = 256
    for start in range(0, feature_ref.shape[0], tile):
        feature_ref[start : start + tile] = gather_rows(slot_row, half_ref, start, tile)


def gather_second_kernel(
    token_ref,
    half_ref,
    lines_ref,
    begun_ref,
    bias_in_ref,
    geometry_ref,
    feature_hbm,
    geometry_hbm,
    bias_hbm,
    end_ref,
    out_ref,
    sems,
):
    owned = feature_hbm.shape[0]
    begun = begun_ref.shape[0]
    lines = lines_ref[...]
    copies = [
        pltpu.make_async_copy(geometry_ref, geometry_hbm, sems.at[2]),
        pltpu.make_async_copy(begun_ref, feature_hbm.at[0:begun], sems.at[0]),
        pltpu.make_async_copy(bias_in_ref, bias_hbm, sems.at[1]),
    ]
    for copy in copies:
        copy.start()
    slot_row = lines[7:8].astype(jnp.int32)
    tile = out_ref.shape[1]
    for step, start in enumerate(range(begun, owned, tile)):
        out_ref[step] = gather_rows(slot_row, half_ref, start, tile)
        copies.append(
            pltpu.make_async_copy(
                out_ref.at[step], feature_hbm.at[start : start + tile], sems.at[3 + step]
            )
        )
        copies[-1].start()
    end_ref[...] = jnp.zeros(end_ref.shape, F32)
    for copy in copies:
        copy.wait()


def mix_kernel(pieces, same_ref, keep_ref, own_bias_ref, other_ref, *out_refs):
    parts = len(out_refs) - pieces
    rows = keep_ref.shape[0] // parts
    start = other_ref.shape[0] - keep_ref.shape[0] - 8
    bias_rows = own_bias_ref[...] + other_ref[start + keep_ref.shape[0] :]
    for m in range(pieces):
        lead = same_ref.shape[1]
        join_pair(same_ref[m], other_ref[m * lead : (m + 1) * lead], out_refs[m])
        out_refs[m][2 * lead - 8 :] = bias_rows
    view = lax.axis_index("view")
    for m in range(parts):
        first = pl.multiple_of((view ^ m) * rows, 8)
        second = pl.multiple_of(start + (view ^ m) * rows, 8)
        out_refs[pieces + m][...] = keep_ref[pl.ds(first, rows)] + other_ref[pl.ds(second, rows)]


def sum_kernel(*refs):
    total = refs[0][...]
    for ref in refs[1:-1]:
        total = total + ref[...]
    refs[-1][...] = total


def join_kernel(token_ref, *refs):
    parts = len(refs) - 1
    rows = refs[0].shape[0]
    view = lax.axis_index("view")
    for m in range(parts):
        start = pl.multiple_of((view ^ m) * rows, 8)
        refs[-1][pl.ds(start, rows)] = refs[m][...]


def finish_kernel(token_ref, mine_ref, other_ref, kernel_hbm, sems):
    half = mine_ref.shape[0]

    def move(first, second):
        copies = [
            pltpu.make_async_copy(first, kernel_hbm.at[0:half], sems.at[0]),
            pltpu.make_async_copy(second, kernel_hbm.at[half:], sems.at[1]),
        ]
        for copy in copies:
            copy.start()
        for copy in copies:
            copy.wait()

    even = lax.axis_index("strip") % 2 == 0

    @pl.when(even)
    def _():
        move(mine_ref, other_ref)

    @pl.when(jnp.logical_not(even))
    def _():
        move(other_ref, mine_ref)


def swap(value, axis, mask):
    count = lax.axis_size(axis)
    return lax.ppermute(value, axis, [(i, i ^ mask) for i in range(count)])


def near_sum(value, axis, unit, amount):
    step = unit
    while amount > 1:
        near = 4 if amount % 4 == 0 else 2
        parts = [value] + [swap(value, axis, step * m) for m in ((2, 3, 1) if near == 4 else (1,))]
        value = call(sum_kernel, jax.ShapeDtypeStruct(value.shape, F32), [VMEM] * near)(*parts)
        step, amount = step * near, amount // near
    return value


def per_device(
    means,
    inv_scales,
    correlation,
    opacity,
    features,
    cameras,
    owners,
    slots,
    lengths,
    target,
    weights,
    bias,
):
    shape = jax.ShapeDtypeStruct
    strips = lax.axis_size("strip")
    views = lax.axis_size("view")
    count = slots.shape[1] * slots.shape[2]
    owned, channels = features.shape
    height, breadth = target.shape[1], target.shape[2]
    pixels = height * breadth
    assert slots.shape[1] == 1 and breadth == WIDTH and channels == LANES
    bucket = max(4, 2 * count // strips)
    places = strips * bucket
    rows = bucket if bucket % 8 == 0 else 64
    groups = places // rows
    direct = rows == bucket
    paired = direct and strips <= 8 and 2 * rows == LANES
    lead = rows + 8
    wire_lead = bucket + 8

    def to_wire(value):
        if direct:
            return value
        top = value[:, :rows].reshape(strips, bucket, LANES)
        low = value[:, rows:, :rows].transpose(1, 0, 2).reshape(8, strips, bucket)
        low = jnp.pad(low.transpose(1, 0, 2), ((0, 0), (0, 0), (0, LANES - bucket)))
        return jnp.concatenate([top, low], axis=1)

    def from_wire(value):
        if direct:
            return value
        top = value[:, :bucket].reshape(groups, rows, LANES)
        low = value[:, bucket:, :bucket].transpose(1, 0, 2).reshape(8, groups, rows)
        low = jnp.pad(low.transpose(1, 0, 2), ((0, 0), (0, 0), (0, LANES - rows)))
        return jnp.concatenate([top, low], axis=1)

    def exchange(value):
        return lax.all_to_all(value, "strip", split_axis=0, concat_axis=0, tiled=True)

    goal = target.reshape(pixels, channels)

    pieces = strips // 2 if paired else 0
    asks = shape((max(8, pieces), LANES), F32)
    pos_row, pos_col, slot_row, *request = call(
        functools.partial(route_kernel, bucket, rows, paired, groups),
        [
            shape((1, count), jnp.int32),
            shape((count, 1), jnp.int32),
            shape((1, count), jnp.int32),
        ]
        + ([asks] * 2 if paired else [shape((groups, 1, LANES), F32)]),
        [VMEM],
    )(jnp.concatenate([owners.reshape(1, count), slots.reshape(1, count)], axis=0))
    if paired:
        chips = call(ask_kernel, [shape((8, LANES), F32)] * pieces, [VMEM] * 2)(
            request[0], swap(request[1], "strip", 1)
        )
        asked = [swap(chips[m], "strip", 2 * m) for m in range(pieces - 1, 0, -1)] + [chips[0]]
    elif direct:
        asked = [exchange(request[0])]
    else:
        request = request[0][:, 0, :rows].reshape(strips, 1, bucket)
        asked = exchange(jnp.pad(request, ((0, 0), (0, 0), (0, LANES - bucket))))
        asked = asked[:, 0, :bucket].reshape(groups, 1, rows)
        asked = [jnp.pad(asked, ((0, 0), (0, 0), (0, LANES - rows)))]

    table = jnp.concatenate(
        [
            means,
            inv_scales,
            correlation[None, :],
            opacity[None, :],
        ],
        axis=0,
    )
    small = jnp.concatenate(
        [jnp.pad(cameras.reshape(1, 8), ((0, 0), (0, LANES - 8))), bias[None, :]], axis=0
    )
    half, parts = call(
        prepare_kernel,
        [
            shape((owned, 2 * channels), BF16),
            shape((3 * 8 * (owned // LANES), LANES), BF16),
        ],
        [ANY, VMEM, VMEM],
        flops=2**33,
        moved=2**24,
    )(pos_row, table, features)
    replies = call(
        functools.partial(reply_kernel, rows, paired, groups),
        [shape((pieces, lead, LANES), F32), shape((pieces * lead, LANES), F32)]
        if paired
        else [shape((groups, lead, LANES), F32)],
        [VMEM] * (2 + len(asked)),
        [pltpu.VMEM((places, owned), BF16)],
    )(half, parts, *asked)
    straight, turned = call(
        weights_kernel,
        [shape((3, 3 * channels, 2 * channels), BF16)] * 2,
        [ANY, VMEM],
        flops=2**32,
        moved=2**23,
    )(replies[0], weights)
    if paired:
        same, cross = replies
        chips = call(
            relay_kernel, [shape((2 * lead - 8, LANES), F32)] * pieces, [VMEM] * 2
        )(same, swap(cross, "strip", 1))
        far = {m: swap(chips[m], "strip", 2 * m) for m in range(pieces - 1, 0, -1)}
        fetched = [far[m] for m in range(pieces - 1, 0, -1)] + [chips[0]]
    else:
        fetched = [from_wire(exchange(to_wire(replies[0])))]

    tile, send_near, send_far, weight, ratio, geometry, feature = call(
        functools.partial(render_kernel, rows, groups, paired),
        [
            shape((pixels, channels), F32),
            shape((3 * WIDTH, channels), F32),
            shape((3 * WIDTH, channels), F32),
            shape((pixels, count), F32),
            shape((pixels, count), F32),
            shape((8, count), F32),
            shape((count, 2 * channels), BF16),
        ],
        [SMEM] + [VMEM] * (4 + len(fetched)),
    )(lengths, small, pos_row, pos_col, goal, *fetched)
    between = [(i, i + 1) for i in range(1, strips - 1, 2)]
    far = lax.ppermute(send_far, "strip", between + [(b, a) for a, b in between])
    near = swap(send_near, "strip", 1)
    spread = call(
        spread_kernel, shape((places, 2 * pixels), BF16), [VMEM] * 2, moved=2**21
    )(pos_row, weight)

    half = 9 * channels // 2
    assert half % (8 * views) == 0
    same, cross, keep, own_bias = call(
        functools.partial(back_kernel, rows, groups, paired),
        [
            shape((pieces if paired else groups, lead, LANES), F32),
            shape((pieces * lead + half + 8, LANES), F32),
            shape((half, channels), F32),
            shape((8, channels), F32),
        ],
        [VMEM] * 14,
        [
            pltpu.VMEM((pixels + 4 * WIDTH + 16, channels), F32),
            pltpu.VMEM((9 * channels, channels), F32),
        ],
        flops=2**30,
        moved=2**22,
    )(
        small,
        tile,
        far,
        near,
        goal,
        straight,
        turned,
        weight,
        ratio,
        geometry,
        feature,
        spread,
        pos_col,
        slot_row,
    )
    other = swap(cross, "strip", 1)
    part = shape((half // views, channels), F32)
    mixed = call(
        functools.partial(mix_kernel, pieces),
        [shape((2 * lead, LANES), F32)] * pieces + [part] * views,
        [VMEM] * 4,
    )(same, keep, own_bias, other)
    if paired:
        order = range(pieces - 1, 0, -1)
        moved = {m: swap(mixed[m], "strip", 2 * m) for m in order}
        returned = [moved[m] for m in order] + [mixed[0]]
    else:
        returned = [from_wire(exchange(to_wire(same))).reshape(groups * lead, LANES)]
    parts = [mixed[pieces]] + [swap(mixed[pieces + m], "view", m) for m in range(1, views)]
    length = pieces * (2 * lead - 8) + 8 if paired else groups * lead
    inputs = returned + parts
    issue = list(range(len(inputs)))
    if paired and pieces == 4 and views == 4:
        issue = [5, 0, 1, 7, 2, 6, 3, 4]
    packed, total = call(
        functools.partial(pack_kernel, [issue.index(i) for i in range(len(issue))], len(returned), paired),
        [shape((length, LANES), F32), part],
        [VMEM] * len(inputs),
    )(*[inputs[i] for i in issue])
    far = {m: swap(packed, "view", m) for m in range(views - 1, 0, -1)}
    arrived = [packed] + [far[m] for m in range(1, views)]

    total = near_sum(total, "strip", 2, strips // 2)
    parts = [total] + [swap(total, "view", m) for m in range(1, views)]
    first = owned * 3 // 4
    feature_first, rowed, lines, bias_sum, geometry_sum = call(
        functools.partial(gather_first_kernel, rows, groups, views, paired),
        [
            shape((first, channels), F32),
            shape((views * places, 2 * channels), BF16),
            shape((8, views * places), F32),
            shape((1, channels), F32),
            shape((7, owned), F32),
        ],
        [ANY] + [VMEM] * views,
        flops=2**31,
        moved=2**22,
    )(total, *arrived)
    if not paired:
        bias_sum = lax.psum(own_bias[0:1], ("view", "strip"))
    joined = call(join_kernel, shape((half, channels), F32), [ANY] + [VMEM] * views)(lines, *parts)
    other = swap(joined, "strip", 1)
    tile = 256
    feature_grad, geometry_grad, bias_grad, end = call(
        gather_second_kernel,
        [
            shape((owned, channels), F32),
            shape((7, owned), F32),
            shape((1, channels), F32),
            shape((8, LANES), F32),
        ],
        [ANY] + [VMEM] * 5,
        [
            pltpu.VMEM(((owned - first) // tile, tile, channels), F32),
            pltpu.SemaphoreType.DMA((3 + (owned - first) // tile,)),
        ],
        out=[HBM, HBM, HBM, VMEM],
        flops=2**31,
        moved=2**22,
    )(joined, rowed, lines, feature_first, bias_sum, geometry_sum)
    kernel_grad = call(
        finish_kernel,
        shape((9 * channels, channels), F32),
        [ANY, ANY, ANY],
        [pltpu.SemaphoreType.DMA((2,))],
        out=HBM,
    )(end, joined, other)
    return (
        geometry_grad,
        feature_grad,
        kernel_grad.reshape(weights.shape),
        bias_grad.reshape(bias.shape),
    )


def solution(mesh):
    return jax.shard_map(
        per_device,
        mesh=mesh,
        in_specs=(
            P(None, "strip"),
            P(None, "strip"),
            P("strip"),
            P("strip"),
            P("strip", None),
            P("view", None, None),
            P("view", "strip", None, None),
            P("view", "strip", None),
            P("view", "strip"),
            P("view", "strip", None, None),
            P(),
            P(),
        ),
        out_specs=(P(None, "strip"), P("strip", None), P(), P()),
        check_vma=False,
    )
```

```python
import functools

import jax
import jax.numpy as jnp
from jax import lax
from jax.experimental import pallas as pl
from jax.experimental.pallas import tpu as pltpu
from jax.sharding import PartitionSpec as P

HIGHEST = lax.Precision.HIGHEST
F32 = jnp.float32
BF16 = jnp.bfloat16
LANES = 128
WIDTH = 16
VMEM = pl.BlockSpec(memory_space=pltpu.VMEM)
SMEM = pl.BlockSpec(memory_space=pltpu.SMEM)
ANY = pl.BlockSpec(memory_space=pl.ANY)
HBM = pl.BlockSpec(memory_space=pltpu.HBM)


def iota(shape, dim):
    return lax.broadcasted_iota(jnp.int32, shape, dim)


def onehot(mask):
    return jnp.where(mask, 1.0, 0.0).astype(BF16)


def split2(x):
    high = x.astype(BF16)
    return high, (x - high.astype(F32)).astype(BF16)


def split3(x):
    high = x.astype(BF16)
    rest = x - high.astype(F32)
    middle = rest.astype(BF16)
    return high, middle, (rest - middle.astype(F32)).astype(BF16)


def dot(a, b):
    return jnp.dot(a, b, preferred_element_type=F32)


def dot_nt(a, b):
    return lax.dot_general(a, b, (((1,), (1,)), ((), ())), preferred_element_type=F32)


def call(kernel, out_shape, in_specs, scratch=(), flops=0, moved=0, out=VMEM, alias=None):
    return pl.pallas_call(
        kernel,
        out_shape=out_shape,
        in_specs=in_specs,
        out_specs=out if isinstance(out, list) else jax.tree.map(lambda _: out, out_shape),
        input_output_aliases=alias or {},
        scratch_shapes=list(scratch),
        compiler_params=pltpu.CompilerParams(vmem_limit_bytes=48 * 2**20),
        cost_estimate=pl.CostEstimate(flops=flops, bytes_accessed=moved, transcendentals=0),
    )


def route_kernel(
    bucket,
    rows,
    paired,
    groups,
    entry_ref,
    pos_row_ref,
    pos_col_ref,
    slot_copy_ref,
    *refs,
):
    owner_ref, slot_ref = entry_ref.at[0:1], entry_ref.at[1:2]
    slot_copy_ref[...] = slot_ref[...]
    count = owner_ref.shape[1]
    owner_row = owner_ref[...].astype(F32)
    down, across = iota((count, count), 0), iota((count, count), 1)
    owner_col = jnp.sum(jnp.where(down == across, owner_row, 0.0), axis=1, keepdims=True)
    same = owner_col == owner_row
    rank_row = jnp.sum(jnp.where(same & (down < across), 1.0, 0.0), axis=0, keepdims=True)
    rank_col = jnp.sum(jnp.where(same & (across < down), 1.0, 0.0), axis=1, keepdims=True)
    pos_row = (owner_row * bucket + rank_row).astype(jnp.int32)
    pos_col = (owner_col * bucket + rank_col).astype(jnp.int32)
    mask = lax.axis_index("strip") * bucket if paired else 0
    pos_row, pos_col = pos_row ^ mask, pos_col ^ mask
    pos_row_ref[...] = pos_row
    pos_col_ref[...] = pos_col
    shift = rows.bit_length() - 1
    left = jnp.where(
        iota((groups, count), 0) == lax.shift_right_logical(pos_row, shift),
        slot_ref[...].astype(F32),
        0.0,
    )
    right = jnp.where(iota((count, LANES), 1) == (pos_col & (rows - 1)), 1.0, 0.0)
    wanted = jnp.dot(left, right, precision=HIGHEST, preferred_element_type=F32)
    for group in range(groups):
        if paired:
            refs[group % 2][group // 2 : group // 2 + 1] = wanted[group : group + 1]
        else:
            refs[0][group] = wanted[group : group + 1]


def ask_kernel(same_ref, other_ref, *out_refs):
    for m, out_ref in enumerate(out_refs):
        out_ref[0:1] = same_ref[m : m + 1]
        out_ref[1:2] = other_ref[m : m + 1]


def prepare_kernel(token_ref, table_ref, feature_ref, half_ref, parts_ref):
    owned, channels = feature_ref.shape
    blocks = owned // LANES
    high, low = split2(feature_ref[...])
    half_ref[:, :channels] = high
    half_ref[:, channels:] = low
    table = jnp.concatenate([table_ref[...], jnp.zeros((1, owned), F32)], axis=0)
    stacked = jnp.concatenate(
        [table[:, a * LANES : (a + 1) * LANES] for a in range(blocks)], axis=0
    )
    parts_ref[...] = jnp.concatenate(split3(stacked), axis=0)


def join_pair(same, other, out_ref):
    rows = same.shape[0] - 8
    out_ref[0:rows] = same[0:rows]
    out_ref[rows : 2 * rows] = other[0:rows]
    out_ref[2 * rows : 2 * rows + 8] = jnp.concatenate(
        [same[rows:][:, :rows], other[rows:][:, :rows]], axis=1
    )


def relay_kernel(same_ref, other_ref, *out_refs):
    lead = same_ref.shape[1]
    for m, out_ref in enumerate(out_refs):
        join_pair(same_ref[m], other_ref[m * lead : (m + 1) * lead], out_ref)


def weights_kernel(token_ref, weights_ref, straight_ref, turned_ref):
    size = weights_ref.shape[2]
    for i in range(3):
        for j in range(3):
            block = weights_ref[i, j]
            high, low = split2(block)
            straight_ref[i, j * size : (j + 1) * size, :size] = high
            straight_ref[i, j * size : (j + 1) * size, size:] = low
            high, low = split2(block.T)
            a, b = 2 - i, 2 - j
            turned_ref[a, b * size : (b + 1) * size, :size] = high
            turned_ref[a, b * size : (b + 1) * size, size:] = low


def reply_kernel(rows, paired, groups, half_ref, parts_ref, *refs):
    pick_ref = refs[-1]
    if paired:
        asked = jnp.concatenate([ref[0:2] for ref in refs[: groups // 2][::-1]], axis=0)
        refs = refs[groups // 2 :]
    else:
        asked = jnp.concatenate([refs[0][group] for group in range(groups)], axis=0)
        refs = refs[1:]
    replies = [refs[0].at[group] for group in range(refs[0].shape[0])]
    if paired:
        others = [refs[1].at[m * (rows + 8) : (m + 1) * (rows + 8)] for m in range(len(replies))]
        replies = [ref for pair in zip(replies, others) for ref in pair]
    owned = half_ref.shape[0]
    channels = half_ref.shape[1] // 2
    blocks = owned // LANES
    padded = jnp.concatenate([asked, jnp.zeros((LANES - groups, LANES), F32)], axis=0)
    columns = padded.T.astype(jnp.int32)
    place = iota((rows, owned), 1)
    for group in range(groups):
        pick_ref[group * rows : (group + 1) * rows] = onehot(
            columns[:rows, group : group + 1] == place
        )
    found = dot(pick_ref[...], half_ref[...])
    found = found[:, :channels] + found[:, channels:]
    slots = asked.astype(jnp.int32)
    slots_row = jnp.concatenate([slots[group : group + 1] for group in range(groups)], axis=1)
    wide = slots_row.shape[1]
    minor = onehot((slots_row & (LANES - 1)) == iota((LANES, wide), 0))
    product = dot(parts_ref[...], minor)
    deep = blocks * 8
    product = product[:deep] + product[deep : 2 * deep] + product[2 * deep :]
    major = lax.shift_right_logical(slots_row, 7)
    geometry = jnp.zeros((8, wide), F32)
    for a in range(blocks):
        geometry = geometry + jnp.where(major == a, product[a * 8 : (a + 1) * 8], 0.0)
    for group in range(groups):
        replies[group][0:rows] = found[group * rows : (group + 1) * rows]
        replies[group][rows : rows + 8] = geometry[:, group * LANES : (group + 1) * LANES]


def camera_at(small_ref, axis, i):
    return small_ref[0:1, 4 * axis + i : 4 * axis + i + 1]


def centers(small_ref, geometry):
    found = []
    for axis in range(2):
        found.append(
            8.0
            + 4.0
            * (
                camera_at(small_ref, axis, 0) * geometry[0:1]
                + camera_at(small_ref, axis, 1) * geometry[1:2]
                + camera_at(small_ref, axis, 2) * geometry[2:3]
                + camera_at(small_ref, axis, 3)
            )
        )
    return found


def offsets(small_ref, geometry, pixels):
    center_col, center_row = centers(small_ref, geometry)
    pixel = iota((pixels, geometry.shape[1]), 0)
    across = (pixel & (WIDTH - 1)).astype(F32) + 0.5
    downward = lax.shift_right_logical(pixel, WIDTH.bit_length() - 1).astype(F32) + 0.5
    return across - center_col, downward - center_row


def render_kernel(
    rows,
    groups,
    paired,
    length_ref,
    small_ref,
    pos_row_ref,
    pos_col_ref,
    target_ref,
    *refs,
):
    received = refs[:-7][::-1]
    tile_ref, send_near_ref, send_far_ref, weight_ref, ratio_ref, geometry_ref, feature_ref = refs[-7:]
    count = pos_row_ref.shape[1]
    places = groups * rows
    pixels, channels = tile_ref.shape
    pick = onehot(pos_col_ref[...] == iota((count, places), 1))
    pick_t = onehot(pos_row_ref[...] == iota((places, count), 0))
    if paired:
        sent = jnp.concatenate([ref[0 : 2 * rows] for ref in received], axis=0)
        lines = jnp.concatenate([ref[2 * rows :] for ref in received], axis=1)
    else:
        sent = jnp.concatenate([received[0][group, 0:rows] for group in range(groups)], axis=0)
        lines = jnp.concatenate(
            [received[0][group, rows:][:, :rows] for group in range(groups)], axis=1
        )
    feature = dot(pick, jnp.concatenate(split2(sent), axis=1)).astype(BF16)
    feature_ref[...] = feature
    geometry = dot(jnp.concatenate(split3(lines), axis=0), pick_t)
    geometry = geometry[0:8] + geometry[8:16] + geometry[16:24]
    geometry_ref[...] = geometry
    du, dv = offsets(small_ref, geometry, pixels)
    a = geometry[3:4] * du
    b = geometry[4:5] * dv
    exponent = -0.5 * (a * a + 2.0 * geometry[5:6] * a * b + b * b)
    alive = iota((1, count), 1) < length_ref[0, 0]
    sigmoid = 1.0 / (1.0 + jnp.exp(-geometry[6:7]))
    raw = sigmoid * jnp.exp(exponent)
    alpha = jnp.where(alive, jnp.minimum(raw, 0.99), 0.0)
    keep = 1.0 - alpha
    log_keep = jnp.log(keep)
    before = onehot(iota((count, count), 0) < iota((count, count), 1))
    high, low = split2(log_keep)
    weight = alpha * jnp.exp(dot(high, before) + dot(low, before))
    weight_ref[...] = weight
    ratio_ref[...] = jnp.where(raw < 0.99, alpha, 0.0) / keep
    high, low = split2(weight)
    tile = dot(high, feature)
    tile = tile[:, :channels] + tile[:, channels:] + dot(low, feature[:, :channels])
    tile_ref[...] = tile
    top = jnp.concatenate([tile[0 : 2 * WIDTH], target_ref[0:WIDTH]], axis=0)
    bottom = jnp.concatenate([tile[pixels - 2 * WIDTH :], target_ref[pixels - WIDTH : pixels]], axis=0)
    even = lax.axis_index("strip") % 2 == 0
    send_near_ref[...] = jnp.where(even, bottom, top)
    send_far_ref[...] = jnp.where(even, top, bottom)


def spread_kernel(
    pos_row_ref,
    weight_ref,
    tile_ref,
    target_ref,
    straight_ref,
    small_ref,
    spread_ref,
    partial_ref,
    high_ref,
    low_ref,
    scratch_ref,
):
    places = spread_ref.shape[0]
    pixels, count = weight_ref.shape
    channels = tile_ref.shape[1]
    pick_t = onehot(pos_row_ref[...] == iota((places, count), 0))
    high, low = split2(weight_ref[...])
    spread_ref[:, :pixels] = dot_nt(pick_t, high).astype(BF16)
    spread_ref[:, pixels:] = dot_nt(pick_t, low).astype(BF16)
    wide = shifted(tile_ref[...], scratch_ref)
    high, low = split2(wide)
    high_ref[...] = high
    low_ref[...] = low
    empty = jnp.zeros((2 * WIDTH, 3 * channels), F32)
    wide = jnp.concatenate([empty, wide, empty], axis=0)
    edge = jnp.zeros((WIDTH, channels), F32)
    goal = jnp.concatenate([edge, target_ref[...], edge], axis=0)
    partial = taps(wide, straight_ref, pixels + 2 * WIDTH, channels)
    partial_ref[...] = partial + small_ref[1:2] - goal


def shifted(value, scratch_ref):
    count = value.shape[0]
    scratch_ref[8 : 8 + count] = value
    column = iota((count, 1), 0) & (WIDTH - 1)
    left = jnp.where(column == 0, 0.0, scratch_ref[7 : 7 + count])
    right = jnp.where(column == WIDTH - 1, 0.0, scratch_ref[9 : 9 + count])
    return jnp.concatenate([left, value, right], axis=1)


def taps(wide, kernel_ref, count, channels):
    high, low = split2(wide)
    total = jnp.zeros((count, channels), F32)
    for i in range(3):
        part = dot(high[WIDTH * i : WIDTH * i + count], kernel_ref[i])
        total = total + part[:, :channels] + part[:, channels:]
        total = total + dot(low[WIDTH * i : WIDTH * i + count], kernel_ref[i][:, :channels])
    return total


def decode(partial_ref, high_ref, low_ref, far_ref, near_ref, kernel_ref, scratch_ref, sum_ref):
    count, channels = partial_ref.shape
    pixels = count - 2 * WIDTH
    edge = 2 * WIDTH
    strip = lax.axis_index("strip")
    even = strip % 2 == 0
    near, far = near_ref[...], far_ref[...]
    above, below = jnp.where(even, far, near), jnp.where(even, near, far)
    gap = jnp.zeros((edge, channels), F32)
    beside = shifted(jnp.concatenate([above[0:edge], gap, below[0:edge]], axis=0), scratch_ref)
    more = taps(beside, kernel_ref, 2 * edge, channels)
    partial = partial_ref[...]
    residual = jnp.concatenate(
        [
            partial[0:WIDTH] + more[0:WIDTH] - above[edge:],
            partial[WIDTH:edge] + more[WIDTH:edge],
            partial[edge : count - edge],
            partial[count - edge : count - WIDTH] + more[edge : edge + WIDTH],
            partial[count - WIDTH :] + more[edge + WIDTH :] - below[edge:],
        ],
        axis=0,
    )
    pixel = iota((count, 1), 0)
    outside = ((pixel < WIDTH) & (strip == 0)) | (
        (pixel >= count - WIDTH) & (strip == lax.axis_size("strip") - 1)
    )
    residual = jnp.where(outside, 0.0, residual)

    own = residual[WIDTH : WIDTH + pixels]
    turned_high, turned_low = split2(own.T)
    beside_high, beside_low = split2(beside)
    high, low = (
        jnp.concatenate([ends[WIDTH:edge], mine[...], ends[2 * edge : 2 * edge + WIDTH]], axis=0)
        for ends, mine in ((beside_high, high_ref), (beside_low, low_ref))
    )
    for i in range(3):
        first = WIDTH * i
        part = (
            dot(turned_high, high[first : first + pixels])
            + dot(turned_high, low[first : first + pixels])
            + dot(turned_low, high[first : first + pixels])
        )
        for j in range(3):
            block = (3 * i + j) * channels
            sum_ref[block : block + channels] = part[:, j * channels : (j + 1) * channels].T
    return residual, jnp.sum(own, axis=0, keepdims=True)


def back_kernel(
    rows,
    groups,
    paired,
    small_ref,
    partial_ref,
    high_ref,
    low_ref,
    far_ref,
    near_ref,
    straight_ref,
    turned_ref,
    weight_ref,
    ratio_ref,
    geometry_ref,
    feature_ref,
    spread_ref,
    pos_col_ref,
    slot_ref,
    same_ref,
    cross_ref,
    keep_ref,
    own_bias_ref,
    scratch_ref,
    sum_ref,
):
    pixels, count = weight_ref.shape
    channels = partial_ref.shape[1]
    places = groups * rows
    lead = rows + 8
    half = keep_ref.shape[0]
    residual, bias_grad = decode(
        partial_ref, high_ref, low_ref, far_ref, near_ref, straight_ref, scratch_ref, sum_ref
    )
    start = cross_ref.shape[0] - half - 8
    bias_rows = jnp.where(iota((8, channels), 0) == 0, bias_grad, 0.0)
    own_bias_ref[...] = bias_rows
    cross_ref[start + half :] = bias_rows
    even = lax.axis_index("strip") % 2 == 0
    keep_ref[...] = jnp.where(even, sum_ref[0:half], sum_ref[half:])
    cross_ref[start : start + half] = jnp.where(even, sum_ref[half:], sum_ref[0:half])

    def put(group, first, value):
        amount = value.shape[0]
        if not paired:
            same_ref[group, first : first + amount] = value
        elif group % 2 == 0:
            same_ref[group // 2, first : first + amount] = value
        else:
            first = group // 2 * lead + first
            cross_ref[first : first + amount] = value

    extent = residual.shape[0]
    scratch_ref[8 + extent : 16 + extent] = jnp.zeros((8, channels), F32)
    wide = shifted(residual, scratch_ref)
    grad = taps(wide, turned_ref, pixels, channels)
    high, low = split2(grad)
    both = jnp.concatenate([high, low], axis=1)
    part = dot(spread_ref[:, :pixels], both)
    part = part[:, :channels] + part[:, channels:] + dot(spread_ref[:, pixels:], high)
    for group in range(groups):
        put(group, 0, part[group * rows : (group + 1) * rows])

    near, far = feature_ref[:, :channels], feature_ref[:, channels:]
    weight_grad = dot_nt(high, near) + dot_nt(high, far) + dot_nt(low, near)
    pull = weight_grad * weight_ref[...]
    behind = onehot(iota((count, count), 0) > iota((count, count), 1))
    high, low = split2(pull)
    suffix = dot(high, behind) + dot(low, behind)
    ratio = ratio_ref[...]
    change = jnp.where(ratio > 0.0, pull - ratio * suffix, 0.0)

    geometry = geometry_ref[...]
    du, dv = offsets(small_ref, geometry, pixels)

    def total(x):
        return jnp.sum(x, axis=0, keepdims=True)

    change_u, change_v = change * du, change * dv
    m, mu, mv = total(change), total(change_u), total(change_v)
    muu, muv, mvv = total(change_u * du), total(change_u * dv), total(change_v * dv)
    g3, g4, g5, g6 = (geometry[i : i + 1] for i in range(3, 7))
    center_col = g3 * (g3 * mu + g5 * g4 * mv)
    center_row = g4 * (g5 * g3 * mu + g4 * mv)
    lines = [
        4.0 * (camera_at(small_ref, 0, i) * center_col + camera_at(small_ref, 1, i) * center_row)
        for i in range(3)
    ]
    lines.append(-(g3 * muu + g5 * g4 * muv))
    lines.append(-(g4 * mvv + g5 * g3 * muv))
    lines.append(-(g3 * g4 * muv))
    lines.append(m / (1.0 + jnp.exp(g6)))
    lines.append(slot_ref[...].astype(F32))
    pick = onehot(pos_col_ref[...] == iota((count, places), 1))
    moved = dot(jnp.concatenate(split3(jnp.concatenate(lines, axis=0)), axis=0), pick)
    moved = moved[0:8] + moved[8:16] + moved[16:24]
    for group in range(groups):
        piece = moved[:, group * rows : (group + 1) * rows]
        if rows < LANES:
            piece = jnp.concatenate([piece, jnp.zeros((8, LANES - rows), F32)], axis=1)
        put(group, rows, piece)


def pack_kernel(places, amount, paired, *refs):
    inputs = [refs[place] for place in places]
    values, parts = inputs[:amount], inputs[amount:]
    packed_ref, sum_ref = refs[-2:]
    rows = values[0].shape[0] - (8 if paired else 0)
    for place, value in enumerate(values):
        packed_ref[place * rows : (place + 1) * rows] = value[0:rows]
    if paired:
        bias_rows = values[0][rows:]
        for value in values[1:]:
            bias_rows = bias_rows + value[rows:]
        packed_ref[amount * rows :] = bias_rows
    sum_kernel(*parts, sum_ref)


def gather_rows(slot_row, half_ref, start, count):
    channels = half_ref.shape[1] // 2
    pick_t = onehot(slot_row == iota((count, half_ref.shape[0]), 0) + start)
    part = dot(pick_t, half_ref[...])
    return part[:, :channels] + part[:, channels:]


def gather_first_kernel(rows, groups, views, paired, token_ref, *refs):
    arrived = refs[:views]
    feature_ref, half_ref, lines_ref, bias_ref, geometry_ref = refs[views:]
    blocks = geometry_ref.shape[1] // LANES
    channels = feature_ref.shape[1]
    step = 2 * rows if paired else rows
    pieces = groups * rows // step
    amount = views * groups * rows
    lines = []
    for view in range(views):
        for group in range(pieces):
            first = group * (step + 8)
            piece = view * pieces + group
            high, low = split2(arrived[view][first : first + step])
            half_ref[piece * step : (piece + 1) * step, :channels] = high
            half_ref[piece * step : (piece + 1) * step, channels:] = low
            lines.append(arrived[view][first + step : first + step + 8][:, :step])
    lines = jnp.concatenate(lines, axis=1)
    lines_ref[...] = lines
    if paired:
        last = arrived[0].shape[0] - 8
        bias = arrived[0][last : last + 1]
        for value in arrived[1:]:
            bias = bias + value[last : last + 1]
        bias_ref[...] = bias
    else:
        bias_ref[...] = jnp.zeros(bias_ref.shape, F32)
    slot_row = lines[7:8].astype(jnp.int32)
    minor = onehot((slot_row & (LANES - 1)) == iota((LANES, amount), 0))
    major = lax.shift_right_logical(slot_row, 7)
    stacked = jnp.concatenate([jnp.where(major == a, lines, 0.0) for a in range(blocks)], axis=0)
    high, low = split2(stacked)
    product = dot_nt(high, minor) + dot_nt(low, minor)
    for a in range(blocks):
        geometry_ref[:, a * LANES : (a + 1) * LANES] = product[a * 8 : a * 8 + 7]
    tile = 256
    for start in range(0, feature_ref.shape[0], tile):
        feature_ref[start : start + tile] = gather_rows(slot_row, half_ref, start, tile)


def gather_second_kernel(
    token_ref,
    half_ref,
    lines_ref,
    begun_ref,
    bias_in_ref,
    geometry_ref,
    feature_hbm,
    geometry_hbm,
    bias_hbm,
    end_ref,
    out_ref,
    sems,
):
    owned = feature_hbm.shape[0]
    begun = begun_ref.shape[0]
    lines = lines_ref[...]
    copies = [
        pltpu.make_async_copy(geometry_ref, geometry_hbm, sems.at[2]),
        pltpu.make_async_copy(begun_ref, feature_hbm.at[0:begun], sems.at[0]),
        pltpu.make_async_copy(bias_in_ref, bias_hbm, sems.at[1]),
    ]
    for copy in copies:
        copy.start()
    slot_row = lines[7:8].astype(jnp.int32)
    tile = out_ref.shape[1]
    for step, start in enumerate(range(begun, owned, tile)):
        out_ref[step] = gather_rows(slot_row, half_ref, start, tile)
        copies.append(
            pltpu.make_async_copy(
                out_ref.at[step], feature_hbm.at[start : start + tile], sems.at[3 + step]
            )
        )
        copies[-1].start()
    end_ref[...] = jnp.zeros(end_ref.shape, F32)
    for copy in copies:
        copy.wait()


def mix_kernel(pieces, same_ref, keep_ref, own_bias_ref, other_ref, *out_refs):
    parts = len(out_refs) - pieces
    rows = keep_ref.shape[0] // parts
    start = other_ref.shape[0] - keep_ref.shape[0] - 8
    bias_rows = own_bias_ref[...] + other_ref[start + keep_ref.shape[0] :]
    for m in range(pieces):
        lead = same_ref.shape[1]
        join_pair(same_ref[m], other_ref[m * lead : (m + 1) * lead], out_refs[m])
        out_refs[m][2 * lead - 8 :] = bias_rows
    view = lax.axis_index("view")
    for m in range(parts):
        first = pl.multiple_of((view ^ m) * rows, 8)
        second = pl.multiple_of(start + (view ^ m) * rows, 8)
        out_refs[pieces + m][...] = keep_ref[pl.ds(first, rows)] + other_ref[pl.ds(second, rows)]


def sum_kernel(*refs):
    total = refs[0][...]
    for ref in refs[1:-1]:
        total = total + ref[...]
    refs[-1][...] = total


def join_kernel(token_ref, *refs):
    parts = len(refs) - 1
    rows = refs[0].shape[0]
    view = lax.axis_index("view")
    for m in range(parts):
        start = pl.multiple_of((view ^ m) * rows, 8)
        refs[-1][pl.ds(start, rows)] = refs[m][...]


def finish_kernel(token_ref, mine_ref, other_ref, kernel_hbm, sems):
    half = mine_ref.shape[0]

    def move(first, second):
        copies = [
            pltpu.make_async_copy(first, kernel_hbm.at[0:half], sems.at[0]),
            pltpu.make_async_copy(second, kernel_hbm.at[half:], sems.at[1]),
        ]
        for copy in copies:
            copy.start()
        for copy in copies:
            copy.wait()

    even = lax.axis_index("strip") % 2 == 0

    @pl.when(even)
    def _():
        move(mine_ref, other_ref)

    @pl.when(jnp.logical_not(even))
    def _():
        move(other_ref, mine_ref)


def swap(value, axis, mask):
    count = lax.axis_size(axis)
    return lax.ppermute(value, axis, [(i, i ^ mask) for i in range(count)])


def near_sum(value, axis, unit, amount):
    step = unit
    while amount > 1:
        near = 4 if amount % 4 == 0 else 2
        parts = [value] + [swap(value, axis, step * m) for m in ((2, 3, 1) if near == 4 else (1,))]
        value = call(sum_kernel, jax.ShapeDtypeStruct(value.shape, F32), [VMEM] * near)(*parts)
        step, amount = step * near, amount // near
    return value


def per_device(
    means,
    inv_scales,
    correlation,
    opacity,
    features,
    cameras,
    owners,
    slots,
    lengths,
    target,
    weights,
    bias,
):
    shape = jax.ShapeDtypeStruct
    strips = lax.axis_size("strip")
    views = lax.axis_size("view")
    count = slots.shape[1] * slots.shape[2]
    owned, channels = features.shape
    height, breadth = target.shape[1], target.shape[2]
    pixels = height * breadth
    assert slots.shape[1] == 1 and breadth == WIDTH and channels == LANES
    bucket = max(4, 2 * count // strips)
    places = strips * bucket
    rows = bucket if bucket % 8 == 0 else 64
    groups = places // rows
    direct = rows == bucket
    paired = direct and strips <= 8 and 2 * rows == LANES
    lead = rows + 8
    wire_lead = bucket + 8

    def to_wire(value):
        if direct:
            return value
        top = value[:, :rows].reshape(strips, bucket, LANES)
        low = value[:, rows:, :rows].transpose(1, 0, 2).reshape(8, strips, bucket)
        low = jnp.pad(low.transpose(1, 0, 2), ((0, 0), (0, 0), (0, LANES - bucket)))
        return jnp.concatenate([top, low], axis=1)

    def from_wire(value):
        if direct:
            return value
        top = value[:, :bucket].reshape(groups, rows, LANES)
        low = value[:, bucket:, :bucket].transpose(1, 0, 2).reshape(8, groups, rows)
        low = jnp.pad(low.transpose(1, 0, 2), ((0, 0), (0, 0), (0, LANES - rows)))
        return jnp.concatenate([top, low], axis=1)

    def exchange(value):
        return lax.all_to_all(value, "strip", split_axis=0, concat_axis=0, tiled=True)

    goal = target.reshape(pixels, channels)

    pieces = strips // 2 if paired else 0
    asks = shape((max(8, pieces), LANES), F32)
    pos_row, pos_col, slot_row, *request = call(
        functools.partial(route_kernel, bucket, rows, paired, groups),
        [
            shape((1, count), jnp.int32),
            shape((count, 1), jnp.int32),
            shape((1, count), jnp.int32),
        ]
        + ([asks] * 2 if paired else [shape((groups, 1, LANES), F32)]),
        [VMEM],
    )(jnp.concatenate([owners.reshape(1, count), slots.reshape(1, count)], axis=0))
    if paired:
        chips = call(ask_kernel, [shape((8, LANES), F32)] * pieces, [VMEM] * 2)(
            request[0], swap(request[1], "strip", 1)
        )
        asked = [swap(chips[m], "strip", 2 * m) for m in range(pieces - 1, 0, -1)] + [chips[0]]
    elif direct:
        asked = [exchange(request[0])]
    else:
        request = request[0][:, 0, :rows].reshape(strips, 1, bucket)
        asked = exchange(jnp.pad(request, ((0, 0), (0, 0), (0, LANES - bucket))))
        asked = asked[:, 0, :bucket].reshape(groups, 1, rows)
        asked = [jnp.pad(asked, ((0, 0), (0, 0), (0, LANES - rows)))]

    table = jnp.concatenate(
        [
            means,
            inv_scales,
            correlation[None, :],
            opacity[None, :],
        ],
        axis=0,
    )
    small = jnp.concatenate(
        [jnp.pad(cameras.reshape(1, 8), ((0, 0), (0, LANES - 8))), bias[None, :]], axis=0
    )
    half, parts = call(
        prepare_kernel,
        [
            shape((owned, 2 * channels), BF16),
            shape((3 * 8 * (owned // LANES), LANES), BF16),
        ],
        [ANY, VMEM, VMEM],
        flops=2**33,
        moved=2**24,
    )(pos_row, table, features)
    replies = call(
        functools.partial(reply_kernel, rows, paired, groups),
        [shape((pieces, lead, LANES), F32), shape((pieces * lead, LANES), F32)]
        if paired
        else [shape((groups, lead, LANES), F32)],
        [VMEM] * (2 + len(asked)),
        [pltpu.VMEM((places, owned), BF16)],
    )(half, parts, *asked)
    straight, turned = call(
        weights_kernel,
        [shape((3, 3 * channels, 2 * channels), BF16)] * 2,
        [ANY, VMEM],
        flops=2**32,
        moved=2**23,
    )(replies[0], weights)
    if paired:
        same, cross = replies
        chips = call(
            relay_kernel, [shape((2 * lead - 8, LANES), F32)] * pieces, [VMEM] * 2
        )(same, swap(cross, "strip", 1))
        far = {m: swap(chips[m], "strip", 2 * m) for m in range(pieces - 1, 0, -1)}
        fetched = [far[m] for m in range(pieces - 1, 0, -1)] + [chips[0]]
    else:
        fetched = [from_wire(exchange(to_wire(replies[0])))]

    tile, send_near, send_far, weight, ratio, geometry, feature = call(
        functools.partial(render_kernel, rows, groups, paired),
        [
            shape((pixels, channels), F32),
            shape((3 * WIDTH, channels), F32),
            shape((3 * WIDTH, channels), F32),
            shape((pixels, count), F32),
            shape((pixels, count), F32),
            shape((8, count), F32),
            shape((count, 2 * channels), BF16),
        ],
        [SMEM] + [VMEM] * (4 + len(fetched)),
    )(lengths, small, pos_row, pos_col, goal, *fetched)
    between = [(i, i + 1) for i in range(1, strips - 1, 2)]
    far = lax.ppermute(send_far, "strip", between + [(b, a) for a, b in between])
    near = swap(send_near, "strip", 1)
    spread, partial, wide_high, wide_low = call(
        spread_kernel,
        [
            shape((places, 2 * pixels), BF16),
            shape((pixels + 2 * WIDTH, channels), F32),
            shape((pixels, 3 * channels), BF16),
            shape((pixels, 3 * channels), BF16),
        ],
        [VMEM] * 6,
        [pltpu.VMEM((pixels + 16, channels), F32)],
        moved=2**21,
    )(pos_row, weight, tile, goal, straight, small)

    half = 9 * channels // 2
    assert half % (8 * views) == 0
    same, cross, keep, own_bias = call(
        functools.partial(back_kernel, rows, groups, paired),
        [
            shape((pieces if paired else groups, lead, LANES), F32),
            shape((pieces * lead + half + 8, LANES), F32),
            shape((half, channels), F32),
            shape((8, channels), F32),
        ],
        [VMEM] * 15,
        [
            pltpu.VMEM((pixels + 4 * WIDTH + 16, channels), F32),
            pltpu.VMEM((9 * channels, channels), F32),
        ],
        flops=2**30,
        moved=2**22,
    )(
        small,
        partial,
        wide_high,
        wide_low,
        far,
        near,
        straight,
        turned,
        weight,
        ratio,
        geometry,
        feature,
        spread,
        pos_col,
        slot_row,
    )
    other = swap(cross, "strip", 1)
    part = shape((half // views, channels), F32)
    mixed = call(
        functools.partial(mix_kernel, pieces),
        [shape((2 * lead, LANES), F32)] * pieces + [part] * views,
        [VMEM] * 4,
    )(same, keep, own_bias, other)
    if paired:
        order = range(pieces - 1, 0, -1)
        moved = {m: swap(mixed[m], "strip", 2 * m) for m in order}
        returned = [moved[m] for m in order] + [mixed[0]]
    else:
        returned = [from_wire(exchange(to_wire(same))).reshape(groups * lead, LANES)]
    parts = [mixed[pieces]] + [swap(mixed[pieces + m], "view", m) for m in range(1, views)]
    length = pieces * (2 * lead - 8) + 8 if paired else groups * lead
    inputs = returned + parts
    issue = list(range(len(inputs)))
    if paired and pieces == 4 and views == 4:
        issue = [5, 0, 1, 7, 2, 6, 3, 4]
    packed, total = call(
        functools.partial(pack_kernel, [issue.index(i) for i in range(len(issue))], len(returned), paired),
        [shape((length, LANES), F32), part],
        [VMEM] * len(inputs),
    )(*[inputs[i] for i in issue])
    far = {m: swap(packed, "view", m) for m in range(views - 1, 0, -1)}
    arrived = [packed] + [far[m] for m in range(1, views)]

    total = near_sum(total, "strip", 2, strips // 2)
    parts = [total] + [swap(total, "view", m) for m in range(1, views)]
    first = owned * 3 // 4
    feature_first, rowed, lines, bias_sum, geometry_sum = call(
        functools.partial(gather_first_kernel, rows, groups, views, paired),
        [
            shape((first, channels), F32),
            shape((views * places, 2 * channels), BF16),
            shape((8, views * places), F32),
            shape((1, channels), F32),
            shape((7, owned), F32),
        ],
        [ANY] + [VMEM] * views,
        flops=2**31,
        moved=2**22,
    )(total, *arrived)
    if not paired:
        bias_sum = lax.psum(own_bias[0:1], ("view", "strip"))
    joined = call(join_kernel, shape((half, channels), F32), [ANY] + [VMEM] * views)(lines, *parts)
    other = swap(joined, "strip", 1)
    tile = 256
    feature_grad, geometry_grad, bias_grad, end = call(
        gather_second_kernel,
        [
            shape((owned, channels), F32),
            shape((7, owned), F32),
            shape((1, channels), F32),
            shape((8, LANES), F32),
        ],
        [ANY] + [VMEM] * 5,
        [
            pltpu.VMEM(((owned - first) // tile, tile, channels), F32),
            pltpu.SemaphoreType.DMA((3 + (owned - first) // tile,)),
        ],
        out=[HBM, HBM, HBM, VMEM],
        flops=2**31,
        moved=2**22,
    )(joined, rowed, lines, feature_first, bias_sum, geometry_sum)
    kernel_grad = call(
        finish_kernel,
        shape((9 * channels, channels), F32),
        [ANY, ANY, ANY],
        [pltpu.SemaphoreType.DMA((2,))],
        out=HBM,
    )(end, joined, other)
    return (
        geometry_grad,
        feature_grad,
        kernel_grad.reshape(weights.shape),
        bias_grad.reshape(bias.shape),
    )


def solution(mesh):
    return jax.shard_map(
        per_device,
        mesh=mesh,
        in_specs=(
            P(None, "strip"),
            P(None, "strip"),
            P("strip"),
            P("strip"),
            P("strip", None),
            P("view", None, None),
            P("view", "strip", None, None),
            P("view", "strip", None),
            P("view", "strip"),
            P("view", "strip", None, None),
            P(),
            P(),
        ),
        out_specs=(P(None, "strip"), P("strip", None), P(), P()),
        check_vma=False,
    )
```

```python
import functools

import jax
import jax.numpy as jnp
from jax import lax
from jax.experimental import pallas as pl
from jax.experimental.pallas import tpu as pltpu
from jax.sharding import PartitionSpec as P

HIGHEST = lax.Precision.HIGHEST
F32 = jnp.float32
BF16 = jnp.bfloat16
LANES = 128
WIDTH = 16
VMEM = pl.BlockSpec(memory_space=pltpu.VMEM)
SMEM = pl.BlockSpec(memory_space=pltpu.SMEM)
ANY = pl.BlockSpec(memory_space=pl.ANY)
HBM = pl.BlockSpec(memory_space=pltpu.HBM)


def iota(shape, dim):
    return lax.broadcasted_iota(jnp.int32, shape, dim)


def onehot(mask):
    return jnp.where(mask, 1.0, 0.0).astype(BF16)


def split2(x):
    high = x.astype(BF16)
    return high, (x - high.astype(F32)).astype(BF16)


def split3(x):
    high = x.astype(BF16)
    rest = x - high.astype(F32)
    middle = rest.astype(BF16)
    return high, middle, (rest - middle.astype(F32)).astype(BF16)


def dot(a, b):
    return jnp.dot(a, b, preferred_element_type=F32)


def dot_nt(a, b):
    return lax.dot_general(a, b, (((1,), (1,)), ((), ())), preferred_element_type=F32)


def call(kernel, out_shape, in_specs, scratch=(), flops=0, moved=0, out=VMEM, alias=None):
    return pl.pallas_call(
        kernel,
        out_shape=out_shape,
        in_specs=in_specs,
        out_specs=out if isinstance(out, list) else jax.tree.map(lambda _: out, out_shape),
        input_output_aliases=alias or {},
        scratch_shapes=list(scratch),
        compiler_params=pltpu.CompilerParams(vmem_limit_bytes=48 * 2**20),
        cost_estimate=pl.CostEstimate(flops=flops, bytes_accessed=moved, transcendentals=0),
    )


def route_kernel(
    bucket,
    rows,
    paired,
    groups,
    entry_ref,
    pos_row_ref,
    pos_col_ref,
    slot_copy_ref,
    *refs,
):
    owner_ref, slot_ref = entry_ref.at[0:1], entry_ref.at[1:2]
    slot_copy_ref[...] = slot_ref[...]
    count = owner_ref.shape[1]
    owner_row = owner_ref[...].astype(F32)
    down, across = iota((count, count), 0), iota((count, count), 1)
    owner_col = jnp.sum(jnp.where(down == across, owner_row, 0.0), axis=1, keepdims=True)
    same = owner_col == owner_row
    rank_row = jnp.sum(jnp.where(same & (down < across), 1.0, 0.0), axis=0, keepdims=True)
    rank_col = jnp.sum(jnp.where(same & (across < down), 1.0, 0.0), axis=1, keepdims=True)
    pos_row = (owner_row * bucket + rank_row).astype(jnp.int32)
    pos_col = (owner_col * bucket + rank_col).astype(jnp.int32)
    mask = lax.axis_index("strip") * bucket if paired else 0
    pos_row, pos_col = pos_row ^ mask, pos_col ^ mask
    pos_row_ref[...] = pos_row
    pos_col_ref[...] = pos_col
    shift = rows.bit_length() - 1
    left = jnp.where(
        iota((groups, count), 0) == lax.shift_right_logical(pos_row, shift),
        slot_ref[...].astype(F32),
        0.0,
    )
    right = jnp.where(iota((count, LANES), 1) == (pos_col & (rows - 1)), 1.0, 0.0)
    wanted = jnp.dot(left, right, precision=HIGHEST, preferred_element_type=F32)
    for group in range(groups):
        if paired:
            refs[group % 2][group // 2 : group // 2 + 1] = wanted[group : group + 1]
        else:
            refs[0][group] = wanted[group : group + 1]


def ask_kernel(same_ref, other_ref, *out_refs):
    for m, out_ref in enumerate(out_refs):
        out_ref[0:1] = same_ref[m : m + 1]
        out_ref[1:2] = other_ref[m : m + 1]


def prepare_kernel(token_ref, table_ref, feature_ref, half_ref, parts_ref):
    owned, channels = feature_ref.shape
    blocks = owned // LANES
    high, low = split2(feature_ref[...])
    half_ref[:, :channels] = high
    half_ref[:, channels:] = low
    table = jnp.concatenate([table_ref[...], jnp.zeros((1, owned), F32)], axis=0)
    stacked = jnp.concatenate(
        [table[:, a * LANES : (a + 1) * LANES] for a in range(blocks)], axis=0
    )
    parts_ref[...] = jnp.concatenate(split3(stacked), axis=0)


def join_pair(same, other, out_ref):
    rows = same.shape[0] - 8
    out_ref[0:rows] = same[0:rows]
    out_ref[rows : 2 * rows] = other[0:rows]
    out_ref[2 * rows : 2 * rows + 8] = jnp.concatenate(
        [same[rows:][:, :rows], other[rows:][:, :rows]], axis=1
    )


def relay_kernel(same_ref, other_ref, *out_refs):
    lead = same_ref.shape[1]
    for m, out_ref in enumerate(out_refs):
        join_pair(same_ref[m], other_ref[m * lead : (m + 1) * lead], out_ref)


def weights_kernel(token_ref, weights_ref, straight_ref, turned_ref):
    size = weights_ref.shape[2]
    for i in range(3):
        for j in range(3):
            block = weights_ref[i, j]
            high, low = split2(block)
            straight_ref[i, j * size : (j + 1) * size, :size] = high
            straight_ref[i, j * size : (j + 1) * size, size:] = low
            high, low = split2(block.T)
            a, b = 2 - i, 2 - j
            turned_ref[a, b * size : (b + 1) * size, :size] = high
            turned_ref[a, b * size : (b + 1) * size, size:] = low


def reply_kernel(rows, paired, groups, half_ref, parts_ref, *refs):
    pick_ref = refs[-1]
    if paired:
        asked = jnp.concatenate([ref[0:2] for ref in refs[: groups // 2][::-1]], axis=0)
        refs = refs[groups // 2 :]
    else:
        asked = jnp.concatenate([refs[0][group] for group in range(groups)], axis=0)
        refs = refs[1:]
    replies = [refs[0].at[group] for group in range(refs[0].shape[0])]
    if paired:
        others = [refs[1].at[m * (rows + 8) : (m + 1) * (rows + 8)] for m in range(len(replies))]
        replies = [ref for pair in zip(replies, others) for ref in pair]
    owned = half_ref.shape[0]
    channels = half_ref.shape[1] // 2
    blocks = owned // LANES
    padded = jnp.concatenate([asked, jnp.zeros((LANES - groups, LANES), F32)], axis=0)
    columns = padded.T.astype(jnp.int32)
    place = iota((rows, owned), 1)
    for group in range(groups):
        pick_ref[group * rows : (group + 1) * rows] = onehot(
            columns[:rows, group : group + 1] == place
        )
    found = dot(pick_ref[...], half_ref[...])
    found = found[:, :channels] + found[:, channels:]
    slots = asked.astype(jnp.int32)
    slots_row = jnp.concatenate([slots[group : group + 1] for group in range(groups)], axis=1)
    wide = slots_row.shape[1]
    minor = onehot((slots_row & (LANES - 1)) == iota((LANES, wide), 0))
    product = dot(parts_ref[...], minor)
    deep = blocks * 8
    product = product[:deep] + product[deep : 2 * deep] + product[2 * deep :]
    major = lax.shift_right_logical(slots_row, 7)
    geometry = jnp.zeros((8, wide), F32)
    for a in range(blocks):
        geometry = geometry + jnp.where(major == a, product[a * 8 : (a + 1) * 8], 0.0)
    for group in range(groups):
        replies[group][0:rows] = found[group * rows : (group + 1) * rows]
        replies[group][rows : rows + 8] = geometry[:, group * LANES : (group + 1) * LANES]


def camera_at(small_ref, axis, i):
    return small_ref[0:1, 4 * axis + i : 4 * axis + i + 1]


def centers(small_ref, geometry):
    found = []
    for axis in range(2):
        found.append(
            8.0
            + 4.0
            * (
                camera_at(small_ref, axis, 0) * geometry[0:1]
                + camera_at(small_ref, axis, 1) * geometry[1:2]
                + camera_at(small_ref, axis, 2) * geometry[2:3]
                + camera_at(small_ref, axis, 3)
            )
        )
    return found


def offsets(small_ref, geometry, pixels):
    center_col, center_row = centers(small_ref, geometry)
    pixel = iota((pixels, geometry.shape[1]), 0)
    across = (pixel & (WIDTH - 1)).astype(F32) + 0.5
    downward = lax.shift_right_logical(pixel, WIDTH.bit_length() - 1).astype(F32) + 0.5
    return across - center_col, downward - center_row


def render_kernel(
    rows,
    groups,
    paired,
    length_ref,
    small_ref,
    pos_row_ref,
    pos_col_ref,
    target_ref,
    *refs,
):
    received = refs[:-7][::-1]
    tile_ref, send_near_ref, send_far_ref, weight_ref, ratio_ref, geometry_ref, feature_ref = refs[-7:]
    count = pos_row_ref.shape[1]
    places = groups * rows
    pixels, channels = tile_ref.shape
    pick = onehot(pos_col_ref[...] == iota((count, places), 1))
    pick_t = onehot(pos_row_ref[...] == iota((places, count), 0))
    if paired:
        sent = jnp.concatenate([ref[0 : 2 * rows] for ref in received], axis=0)
        lines = jnp.concatenate([ref[2 * rows :] for ref in received], axis=1)
    else:
        sent = jnp.concatenate([received[0][group, 0:rows] for group in range(groups)], axis=0)
        lines = jnp.concatenate(
            [received[0][group, rows:][:, :rows] for group in range(groups)], axis=1
        )
    feature = dot(pick, jnp.concatenate(split2(sent), axis=1)).astype(BF16)
    feature_ref[...] = feature
    geometry = dot(jnp.concatenate(split3(lines), axis=0), pick_t)
    geometry = geometry[0:8] + geometry[8:16] + geometry[16:24]
    geometry_ref[...] = geometry
    du, dv = offsets(small_ref, geometry, pixels)
    a = geometry[3:4] * du
    b = geometry[4:5] * dv
    exponent = -0.5 * (a * a + 2.0 * geometry[5:6] * a * b + b * b)
    alive = iota((1, count), 1) < length_ref[0, 0]
    sigmoid = 1.0 / (1.0 + jnp.exp(-geometry[6:7]))
    raw = sigmoid * jnp.exp(exponent)
    alpha = jnp.where(alive, jnp.minimum(raw, 0.99), 0.0)
    keep = 1.0 - alpha
    log_keep = jnp.log(keep)
    before = onehot(iota((count, count), 0) < iota((count, count), 1))
    high, low = split2(log_keep)
    weight = alpha * jnp.exp(dot(high, before) + dot(low, before))
    weight_ref[...] = weight
    ratio_ref[...] = jnp.where(raw < 0.99, alpha, 0.0) / keep
    high, low = split2(weight)
    tile = dot(high, feature)
    tile = tile[:, :channels] + tile[:, channels:] + dot(low, feature[:, :channels])
    tile_ref[...] = tile
    top = jnp.concatenate([tile[0 : 2 * WIDTH], target_ref[0:WIDTH]], axis=0)
    bottom = jnp.concatenate([tile[pixels - 2 * WIDTH :], target_ref[pixels - WIDTH : pixels]], axis=0)
    even = lax.axis_index("strip") % 2 == 0
    send_near_ref[...] = jnp.where(even, bottom, top)
    send_far_ref[...] = jnp.where(even, top, bottom)


def spread_kernel(
    pos_row_ref,
    weight_ref,
    tile_ref,
    target_ref,
    straight_ref,
    small_ref,
    spread_ref,
    partial_ref,
    high_ref,
    low_ref,
    scratch_ref,
):
    places = spread_ref.shape[0]
    pixels, count = weight_ref.shape
    channels = tile_ref.shape[1]
    pick_t = onehot(pos_row_ref[...] == iota((places, count), 0))
    high, low = split2(weight_ref[...])
    spread_ref[:, :pixels] = dot_nt(pick_t, high).astype(BF16)
    spread_ref[:, pixels:] = dot_nt(pick_t, low).astype(BF16)
    wide = shifted(tile_ref[...], scratch_ref)
    high, low = split2(wide)
    high_ref[...] = high
    low_ref[...] = low
    empty = jnp.zeros((2 * WIDTH, 3 * channels), F32)
    wide = jnp.concatenate([empty, wide, empty], axis=0)
    edge = jnp.zeros((WIDTH, channels), F32)
    goal = jnp.concatenate([edge, target_ref[...], edge], axis=0)
    partial = taps(wide, straight_ref, pixels + 2 * WIDTH, channels)
    partial_ref[...] = partial + small_ref[1:2] - goal


def shifted(value, scratch_ref):
    count = value.shape[0]
    scratch_ref[8 : 8 + count] = value
    column = iota((count, 1), 0) & (WIDTH - 1)
    left = jnp.where(column == 0, 0.0, scratch_ref[7 : 7 + count])
    right = jnp.where(column == WIDTH - 1, 0.0, scratch_ref[9 : 9 + count])
    return jnp.concatenate([left, value, right], axis=1)


def taps(wide, kernel_ref, count, channels):
    high, low = split2(wide)
    total = jnp.zeros((count, channels), F32)
    for i in range(3):
        part = dot(high[WIDTH * i : WIDTH * i + count], kernel_ref[i])
        total = total + part[:, :channels] + part[:, channels:]
        total = total + dot(low[WIDTH * i : WIDTH * i + count], kernel_ref[i][:, :channels])
    return total


def decode(partial_ref, high_ref, low_ref, far_ref, near_ref, kernel_ref, scratch_ref, sum_ref):
    count, channels = partial_ref.shape
    pixels = count - 2 * WIDTH
    edge = 2 * WIDTH
    strip = lax.axis_index("strip")
    even = strip % 2 == 0
    near, far = near_ref[...], far_ref[...]
    above, below = jnp.where(even, far, near), jnp.where(even, near, far)
    gap = jnp.zeros((edge, channels), F32)
    beside = shifted(jnp.concatenate([above[0:edge], gap, below[0:edge]], axis=0), scratch_ref)
    more = taps(beside, kernel_ref, 2 * edge, channels)
    partial = partial_ref[...]
    residual = jnp.concatenate(
        [
            partial[0:WIDTH] + more[0:WIDTH] - above[edge:],
            partial[WIDTH:edge] + more[WIDTH:edge],
            partial[edge : count - edge],
            partial[count - edge : count - WIDTH] + more[edge : edge + WIDTH],
            partial[count - WIDTH :] + more[edge + WIDTH :] - below[edge:],
        ],
        axis=0,
    )
    pixel = iota((count, 1), 0)
    outside = ((pixel < WIDTH) & (strip == 0)) | (
        (pixel >= count - WIDTH) & (strip == lax.axis_size("strip") - 1)
    )
    residual = jnp.where(outside, 0.0, residual)

    own = residual[WIDTH : WIDTH + pixels]
    turned_high, turned_low = split2(own.T)
    beside_high, beside_low = split2(beside)
    high, low = (
        jnp.concatenate([ends[WIDTH:edge], mine[...], ends[2 * edge : 2 * edge + WIDTH]], axis=0)
        for ends, mine in ((beside_high, high_ref), (beside_low, low_ref))
    )
    for i in range(3):
        first = WIDTH * i
        part = (
            dot(turned_high, high[first : first + pixels])
            + dot(turned_high, low[first : first + pixels])
            + dot(turned_low, high[first : first + pixels])
        )
        for j in range(3):
            block = (3 * i + j) * channels
            sum_ref[block : block + channels] = part[:, j * channels : (j + 1) * channels].T
    return residual, jnp.sum(own, axis=0, keepdims=True)


def back_kernel(
    rows,
    groups,
    paired,
    small_ref,
    partial_ref,
    high_ref,
    low_ref,
    far_ref,
    near_ref,
    straight_ref,
    turned_ref,
    weight_ref,
    ratio_ref,
    geometry_ref,
    feature_ref,
    spread_ref,
    pos_col_ref,
    slot_ref,
    same_ref,
    cross_ref,
    keep_ref,
    own_bias_ref,
    scratch_ref,
    sum_ref,
):
    pixels, count = weight_ref.shape
    channels = partial_ref.shape[1]
    places = groups * rows
    lead = rows + 8
    half = keep_ref.shape[0]
    residual, bias_grad = decode(
        partial_ref, high_ref, low_ref, far_ref, near_ref, straight_ref, scratch_ref, sum_ref
    )
    start = cross_ref.shape[0] - half - 8
    bias_rows = jnp.where(iota((8, channels), 0) == 0, bias_grad, 0.0)
    own_bias_ref[...] = bias_rows
    cross_ref[start + half :] = bias_rows
    even = lax.axis_index("strip") % 2 == 0
    keep_ref[...] = jnp.where(even, sum_ref[0:half], sum_ref[half:])
    cross_ref[start : start + half] = jnp.where(even, sum_ref[half:], sum_ref[0:half])

    def put(group, first, value):
        amount = value.shape[0]
        if not paired:
            same_ref[group, first : first + amount] = value
        elif group % 2 == 0:
            same_ref[group // 2, first : first + amount] = value
        else:
            first = group // 2 * lead + first
            cross_ref[first : first + amount] = value

    extent = residual.shape[0]
    scratch_ref[8 + extent : 16 + extent] = jnp.zeros((8, channels), F32)
    wide = shifted(residual, scratch_ref)
    grad = taps(wide, turned_ref, pixels, channels)
    high, low = split2(grad)
    both = jnp.concatenate([high, low], axis=1)
    part = dot(spread_ref[:, :pixels], both)
    part = part[:, :channels] + part[:, channels:] + dot(spread_ref[:, pixels:], high)
    for group in range(groups):
        put(group, 0, part[group * rows : (group + 1) * rows])

    near, far = feature_ref[:, :channels], feature_ref[:, channels:]
    weight_grad = dot_nt(high, near) + dot_nt(high, far) + dot_nt(low, near)
    pull = weight_grad * weight_ref[...]
    behind = onehot(iota((count, count), 0) > iota((count, count), 1))
    high, low = split2(pull)
    suffix = dot(high, behind) + dot(low, behind)
    ratio = ratio_ref[...]
    change = jnp.where(ratio > 0.0, pull - ratio * suffix, 0.0)

    geometry = geometry_ref[...]
    du, dv = offsets(small_ref, geometry, pixels)

    def total(x):
        return jnp.sum(x, axis=0, keepdims=True)

    change_u, change_v = change * du, change * dv
    m, mu, mv = total(change), total(change_u), total(change_v)
    muu, muv, mvv = total(change_u * du), total(change_u * dv), total(change_v * dv)
    g3, g4, g5, g6 = (geometry[i : i + 1] for i in range(3, 7))
    center_col = g3 * (g3 * mu + g5 * g4 * mv)
    center_row = g4 * (g5 * g3 * mu + g4 * mv)
    lines = [
        4.0 * (camera_at(small_ref, 0, i) * center_col + camera_at(small_ref, 1, i) * center_row)
        for i in range(3)
    ]
    lines.append(-(g3 * muu + g5 * g4 * muv))
    lines.append(-(g4 * mvv + g5 * g3 * muv))
    lines.append(-(g3 * g4 * muv))
    lines.append(m / (1.0 + jnp.exp(g6)))
    lines.append(slot_ref[...].astype(F32))
    pick = onehot(pos_col_ref[...] == iota((count, places), 1))
    moved = dot(jnp.concatenate(split3(jnp.concatenate(lines, axis=0)), axis=0), pick)
    moved = moved[0:8] + moved[8:16] + moved[16:24]
    for group in range(groups):
        piece = moved[:, group * rows : (group + 1) * rows]
        if rows < LANES:
            piece = jnp.concatenate([piece, jnp.zeros((8, LANES - rows), F32)], axis=1)
        put(group, rows, piece)


def pack_kernel(places, amount, paired, *refs):
    inputs = [refs[place] for place in places]
    values, parts = inputs[:amount], inputs[amount:]
    packed_ref, sum_ref = refs[-2:]
    rows = values[0].shape[0] - (8 if paired else 0)
    for place, value in enumerate(values):
        packed_ref[place * rows : (place + 1) * rows] = value[0:rows]
    if paired:
        bias_rows = values[0][rows:]
        for value in values[1:]:
            bias_rows = bias_rows + value[rows:]
        packed_ref[amount * rows :] = bias_rows
    sum_kernel(*parts, sum_ref)


def gather_rows(slot_row, half_ref, start, count):
    channels = half_ref.shape[1] // 2
    pick_t = onehot(slot_row == iota((count, half_ref.shape[0]), 0) + start)
    part = dot(pick_t, half_ref[...])
    return part[:, :channels] + part[:, channels:]


def gather_first_kernel(rows, groups, views, paired, token_ref, *refs):
    arrived = refs[:views]
    feature_ref, half_ref, lines_ref, bias_ref, geometry_ref = refs[views:]
    blocks = geometry_ref.shape[1] // LANES
    channels = feature_ref.shape[1]
    step = 2 * rows if paired else rows
    pieces = groups * rows // step
    amount = views * groups * rows
    lines = []
    for view in range(views):
        for group in range(pieces):
            first = group * (step + 8)
            piece = view * pieces + group
            high, low = split2(arrived[view][first : first + step])
            half_ref[piece * step : (piece + 1) * step, :channels] = high
            half_ref[piece * step : (piece + 1) * step, channels:] = low
            lines.append(arrived[view][first + step : first + step + 8][:, :step])
    lines = jnp.concatenate(lines, axis=1)
    lines_ref[...] = lines
    if paired:
        last = arrived[0].shape[0] - 8
        bias = arrived[0][last : last + 1]
        for value in arrived[1:]:
            bias = bias + value[last : last + 1]
        bias_ref[...] = bias
    else:
        bias_ref[...] = jnp.zeros(bias_ref.shape, F32)
    slot_row = lines[7:8].astype(jnp.int32)
    minor = onehot((slot_row & (LANES - 1)) == iota((LANES, amount), 0))
    major = lax.shift_right_logical(slot_row, 7)
    stacked = jnp.concatenate([jnp.where(major == a, lines, 0.0) for a in range(blocks)], axis=0)
    high, low = split2(stacked)
    product = dot_nt(high, minor) + dot_nt(low, minor)
    for a in range(blocks):
        geometry_ref[:, a * LANES : (a + 1) * LANES] = product[a * 8 : a * 8 + 7]
    tile = 256
    for start in range(0, feature_ref.shape[0], tile):
        feature_ref[start : start + tile] = gather_rows(slot_row, half_ref, start, tile)


def gather_second_kernel(
    token_ref,
    half_ref,
    lines_ref,
    begun_ref,
    bias_in_ref,
    geometry_ref,
    feature_hbm,
    geometry_hbm,
    bias_hbm,
    end_ref,
    out_ref,
    sems,
):
    owned = feature_hbm.shape[0]
    begun = begun_ref.shape[0]
    lines = lines_ref[...]
    copies = [
        pltpu.make_async_copy(geometry_ref, geometry_hbm, sems.at[2]),
        pltpu.make_async_copy(begun_ref, feature_hbm.at[0:begun], sems.at[0]),
        pltpu.make_async_copy(bias_in_ref, bias_hbm, sems.at[1]),
    ]
    for copy in copies:
        copy.start()
    slot_row = lines[7:8].astype(jnp.int32)
    tile = out_ref.shape[1]
    for step, start in enumerate(range(begun, owned, tile)):
        out_ref[step] = gather_rows(slot_row, half_ref, start, tile)
        copies.append(
            pltpu.make_async_copy(
                out_ref.at[step], feature_hbm.at[start : start + tile], sems.at[3 + step]
            )
        )
        copies[-1].start()
    end_ref[...] = jnp.zeros(end_ref.shape, F32)
    for copy in copies:
        copy.wait()


def mix_kernel(pieces, same_ref, keep_ref, own_bias_ref, other_ref, *out_refs):
    parts = len(out_refs) - pieces
    rows = keep_ref.shape[0] // parts
    start = other_ref.shape[0] - keep_ref.shape[0] - 8
    bias_rows = own_bias_ref[...] + other_ref[start + keep_ref.shape[0] :]
    for m in range(pieces):
        lead = same_ref.shape[1]
        join_pair(same_ref[m], other_ref[m * lead : (m + 1) * lead], out_refs[m])
        out_refs[m][2 * lead - 8 :] = bias_rows
    view = lax.axis_index("view")
    for m in range(parts):
        first = pl.multiple_of((view ^ m) * rows, 8)
        second = pl.multiple_of(start + (view ^ m) * rows, 8)
        out_refs[pieces + m][...] = keep_ref[pl.ds(first, rows)] + other_ref[pl.ds(second, rows)]


def sum_kernel(*refs):
    total = refs[0][...]
    for ref in refs[1:-1]:
        total = total + ref[...]
    refs[-1][...] = total


def join_kernel(token_ref, *refs):
    parts = len(refs) - 1
    rows = refs[0].shape[0]
    view = lax.axis_index("view")
    for m in range(parts):
        start = pl.multiple_of((view ^ m) * rows, 8)
        refs[-1][pl.ds(start, rows)] = refs[m][...]


def finish_kernel(token_ref, mine_ref, other_ref, kernel_hbm, sems):
    half = mine_ref.shape[0]

    def move(first, second):
        copies = [
            pltpu.make_async_copy(first, kernel_hbm.at[0:half], sems.at[0]),
            pltpu.make_async_copy(second, kernel_hbm.at[half:], sems.at[1]),
        ]
        for copy in copies:
            copy.start()
        for copy in copies:
            copy.wait()

    even = lax.axis_index("strip") % 2 == 0

    @pl.when(even)
    def _():
        move(mine_ref, other_ref)

    @pl.when(jnp.logical_not(even))
    def _():
        move(other_ref, mine_ref)


def swap(value, axis, mask):
    count = lax.axis_size(axis)
    return lax.ppermute(value, axis, [(i, i ^ mask) for i in range(count)])


def near_sum(value, axis, unit, amount):
    step = unit
    while amount > 1:
        near = 4 if amount % 4 == 0 else 2
        parts = [value] + [swap(value, axis, step * m) for m in ((2, 3, 1) if near == 4 else (1,))]
        value = call(sum_kernel, jax.ShapeDtypeStruct(value.shape, F32), [VMEM] * near)(*parts)
        step, amount = step * near, amount // near
    return value


def per_device(
    means,
    inv_scales,
    correlation,
    opacity,
    features,
    cameras,
    owners,
    slots,
    lengths,
    target,
    weights,
    bias,
):
    shape = jax.ShapeDtypeStruct
    strips = lax.axis_size("strip")
    views = lax.axis_size("view")
    count = slots.shape[1] * slots.shape[2]
    owned, channels = features.shape
    height, breadth = target.shape[1], target.shape[2]
    pixels = height * breadth
    assert slots.shape[1] == 1 and breadth == WIDTH and channels == LANES
    bucket = max(4, 2 * count // strips)
    places = strips * bucket
    rows = bucket if bucket % 8 == 0 else 64
    groups = places // rows
    direct = rows == bucket
    paired = direct and strips <= 8 and 2 * rows == LANES
    lead = rows + 8
    wire_lead = bucket + 8

    def to_wire(value):
        if direct:
            return value
        top = value[:, :rows].reshape(strips, bucket, LANES)
        low = value[:, rows:, :rows].transpose(1, 0, 2).reshape(8, strips, bucket)
        low = jnp.pad(low.transpose(1, 0, 2), ((0, 0), (0, 0), (0, LANES - bucket)))
        return jnp.concatenate([top, low], axis=1)

    def from_wire(value):
        if direct:
            return value
        top = value[:, :bucket].reshape(groups, rows, LANES)
        low = value[:, bucket:, :bucket].transpose(1, 0, 2).reshape(8, groups, rows)
        low = jnp.pad(low.transpose(1, 0, 2), ((0, 0), (0, 0), (0, LANES - rows)))
        return jnp.concatenate([top, low], axis=1)

    def exchange(value):
        return lax.all_to_all(value, "strip", split_axis=0, concat_axis=0, tiled=True)

    goal = target.reshape(pixels, channels)

    pieces = strips // 2 if paired else 0
    asks = shape((max(8, pieces), LANES), F32)
    pos_row, pos_col, slot_row, *request = call(
        functools.partial(route_kernel, bucket, rows, paired, groups),
        [
            shape((1, count), jnp.int32),
            shape((count, 1), jnp.int32),
            shape((1, count), jnp.int32),
        ]
        + ([asks] * 2 if paired else [shape((groups, 1, LANES), F32)]),
        [VMEM],
    )(jnp.concatenate([owners.reshape(1, count), slots.reshape(1, count)], axis=0))
    if paired:
        chips = call(ask_kernel, [shape((8, LANES), F32)] * pieces, [VMEM] * 2)(
            request[0], swap(request[1], "strip", 1)
        )
        asked = [swap(chips[m], "strip", 2 * m) for m in range(pieces - 1, 0, -1)] + [chips[0]]
    elif direct:
        asked = [exchange(request[0])]
    else:
        request = request[0][:, 0, :rows].reshape(strips, 1, bucket)
        asked = exchange(jnp.pad(request, ((0, 0), (0, 0), (0, LANES - bucket))))
        asked = asked[:, 0, :bucket].reshape(groups, 1, rows)
        asked = [jnp.pad(asked, ((0, 0), (0, 0), (0, LANES - rows)))]

    table = jnp.concatenate(
        [
            means,
            inv_scales,
            correlation[None, :],
            opacity[None, :],
        ],
        axis=0,
    )
    small = jnp.concatenate(
        [jnp.pad(cameras.reshape(1, 8), ((0, 0), (0, LANES - 8))), bias[None, :]], axis=0
    )
    half, parts = call(
        prepare_kernel,
        [
            shape((owned, 2 * channels), BF16),
            shape((3 * 8 * (owned // LANES), LANES), BF16),
        ],
        [ANY, VMEM, VMEM],
        flops=2**33,
        moved=2**24,
    )(pos_row, table, features)
    replies = call(
        functools.partial(reply_kernel, rows, paired, groups),
        [shape((pieces, lead, LANES), F32), shape((pieces * lead, LANES), F32)]
        if paired
        else [shape((groups, lead, LANES), F32)],
        [VMEM] * (2 + len(asked)),
        [pltpu.VMEM((places, owned), BF16)],
    )(half, parts, *asked)
    straight, turned = call(
        weights_kernel,
        [shape((3, 3 * channels, 2 * channels), BF16)] * 2,
        [ANY, VMEM],
        flops=2**32,
        moved=2**23,
    )(replies[0], weights)
    if paired:
        same, cross = replies
        chips = call(
            relay_kernel, [shape((2 * lead - 8, LANES), F32)] * pieces, [VMEM] * 2
        )(same, swap(cross, "strip", 1))
        far = {m: swap(chips[m], "strip", 2 * m) for m in range(pieces - 1, 0, -1)}
        fetched = [far[m] for m in range(pieces - 1, 0, -1)] + [chips[0]]
    else:
        fetched = [from_wire(exchange(to_wire(replies[0])))]

    tile, send_near, send_far, weight, ratio, geometry, feature = call(
        functools.partial(render_kernel, rows, groups, paired),
        [
            shape((pixels, channels), F32),
            shape((3 * WIDTH, channels), F32),
            shape((3 * WIDTH, channels), F32),
            shape((pixels, count), F32),
            shape((pixels, count), F32),
            shape((8, count), F32),
            shape((count, 2 * channels), BF16),
        ],
        [SMEM] + [VMEM] * (4 + len(fetched)),
    )(lengths, small, pos_row, pos_col, goal, *fetched)
    between = [(i, i + 1) for i in range(1, strips - 1, 2)]
    far = lax.ppermute(send_far, "strip", between + [(b, a) for a, b in between])
    near = swap(send_near, "strip", 1)
    spread, partial, wide_high, wide_low = call(
        spread_kernel,
        [
            shape((places, 2 * pixels), BF16),
            shape((pixels + 2 * WIDTH, channels), F32),
            shape((pixels, 3 * channels), BF16),
            shape((pixels, 3 * channels), BF16),
        ],
        [VMEM] * 6,
        [pltpu.VMEM((pixels + 16, channels), F32)],
        moved=2**21,
    )(pos_row, weight, tile, goal, straight, small)

    half = 9 * channels // 2
    assert half % (8 * views) == 0
    same, cross, keep, own_bias = call(
        functools.partial(back_kernel, rows, groups, paired),
        [
            shape((pieces if paired else groups, lead, LANES), F32),
            shape((pieces * lead + half + 8, LANES), F32),
            shape((half, channels), F32),
            shape((8, channels), F32),
        ],
        [VMEM] * 15,
        [
            pltpu.VMEM((pixels + 4 * WIDTH + 16, channels), F32),
            pltpu.VMEM((9 * channels, channels), F32),
        ],
        flops=2**30,
        moved=2**22,
    )(
        small,
        partial,
        wide_high,
        wide_low,
        far,
        near,
        straight,
        turned,
        weight,
        ratio,
        geometry,
        feature,
        spread,
        pos_col,
        slot_row,
    )
    other = swap(cross, "strip", 1)
    part = shape((half // views, channels), F32)
    mixed = call(
        functools.partial(mix_kernel, pieces),
        [shape((2 * lead, LANES), F32)] * pieces + [part] * views,
        [VMEM] * 4,
    )(same, keep, own_bias, other)
    if paired:
        order = range(pieces - 1, 0, -1)
        moved = {m: swap(mixed[m], "strip", 2 * m) for m in order}
        returned = [moved[m] for m in order] + [mixed[0]]
    else:
        returned = [from_wire(exchange(to_wire(same))).reshape(groups * lead, LANES)]
    parts = [mixed[pieces]] + [swap(mixed[pieces + m], "view", m) for m in range(1, views)]
    length = pieces * (2 * lead - 8) + 8 if paired else groups * lead
    inputs = returned + parts
    issue = list(range(len(inputs)))
    if paired and pieces == 4 and views == 4:
        issue = [2, 0, 1, 7, 5, 6, 3, 4]
    packed, total = call(
        functools.partial(pack_kernel, [issue.index(i) for i in range(len(issue))], len(returned), paired),
        [shape((length, LANES), F32), part],
        [VMEM] * len(inputs),
    )(*[inputs[i] for i in issue])
    far = {m: swap(packed, "view", m) for m in range(views - 1, 0, -1)}
    arrived = [packed] + [far[m] for m in range(1, views)]

    total = near_sum(total, "strip", 2, strips // 2)
    parts = [total] + [swap(total, "view", m) for m in range(1, views)]
    first = owned * 7 // 8
    feature_first, rowed, lines, bias_sum, geometry_sum = call(
        functools.partial(gather_first_kernel, rows, groups, views, paired),
        [
            shape((first, channels), F32),
            shape((views * places, 2 * channels), BF16),
            shape((8, views * places), F32),
            shape((1, channels), F32),
            shape((7, owned), F32),
        ],
        [ANY] + [VMEM] * views,
        flops=2**31,
        moved=2**22,
    )(total, *arrived)
    if not paired:
        bias_sum = lax.psum(own_bias[0:1], ("view", "strip"))
    joined = call(join_kernel, shape((half, channels), F32), [ANY] + [VMEM] * views)(lines, *parts)
    other = swap(joined, "strip", 1)
    tile = 256
    feature_grad, geometry_grad, bias_grad, end = call(
        gather_second_kernel,
        [
            shape((owned, channels), F32),
            shape((7, owned), F32),
            shape((1, channels), F32),
            shape((8, LANES), F32),
        ],
        [ANY] + [VMEM] * 5,
        [
            pltpu.VMEM(((owned - first) // tile, tile, channels), F32),
            pltpu.SemaphoreType.DMA((3 + (owned - first) // tile,)),
        ],
        out=[HBM, HBM, HBM, VMEM],
        flops=2**31,
        moved=2**22,
    )(joined, rowed, lines, feature_first, bias_sum, geometry_sum)
    kernel_grad = call(
        finish_kernel,
        shape((9 * channels, channels), F32),
        [ANY, ANY, ANY],
        [pltpu.SemaphoreType.DMA((2,))],
        out=HBM,
    )(end, joined, other)
    return (
        geometry_grad,
        feature_grad,
        kernel_grad.reshape(weights.shape),
        bias_grad.reshape(bias.shape),
    )


def solution(mesh):
    return jax.shard_map(
        per_device,
        mesh=mesh,
        in_specs=(
            P(None, "strip"),
            P(None, "strip"),
            P("strip"),
            P("strip"),
            P("strip", None),
            P("view", None, None),
            P("view", "strip", None, None),
            P("view", "strip", None),
            P("view", "strip"),
            P("view", "strip", None, None),
            P(),
            P(),
        ),
        out_specs=(P(None, "strip"), P("strip", None), P(), P()),
        check_vma=False,
    )
```

```python
import functools

import jax
import jax.numpy as jnp
from jax import lax
from jax.experimental import pallas as pl
from jax.experimental.pallas import tpu as pltpu
from jax.sharding import PartitionSpec as P

HIGHEST = lax.Precision.HIGHEST
F32 = jnp.float32
BF16 = jnp.bfloat16
LANES = 128
WIDTH = 16
VMEM = pl.BlockSpec(memory_space=pltpu.VMEM)
SMEM = pl.BlockSpec(memory_space=pltpu.SMEM)
ANY = pl.BlockSpec(memory_space=pl.ANY)
HBM = pl.BlockSpec(memory_space=pltpu.HBM)


def iota(shape, dim):
    return lax.broadcasted_iota(jnp.int32, shape, dim)


def onehot(mask):
    return jnp.where(mask, 1.0, 0.0).astype(BF16)


def split2(x):
    high = x.astype(BF16)
    return high, (x - high.astype(F32)).astype(BF16)


def split3(x):
    high = x.astype(BF16)
    rest = x - high.astype(F32)
    middle = rest.astype(BF16)
    return high, middle, (rest - middle.astype(F32)).astype(BF16)


def dot(a, b):
    return jnp.dot(a, b, preferred_element_type=F32)


def dot_nt(a, b):
    return lax.dot_general(a, b, (((1,), (1,)), ((), ())), preferred_element_type=F32)


def call(kernel, out_shape, in_specs, scratch=(), flops=0, moved=0, out=VMEM, alias=None):
    return pl.pallas_call(
        kernel,
        out_shape=out_shape,
        in_specs=in_specs,
        out_specs=out if isinstance(out, list) else jax.tree.map(lambda _: out, out_shape),
        input_output_aliases=alias or {},
        scratch_shapes=list(scratch),
        compiler_params=pltpu.CompilerParams(vmem_limit_bytes=48 * 2**20),
        cost_estimate=pl.CostEstimate(flops=flops, bytes_accessed=moved, transcendentals=0),
    )


def route_kernel(
    bucket,
    rows,
    paired,
    groups,
    entry_ref,
    pos_row_ref,
    pos_col_ref,
    slot_copy_ref,
    *refs,
):
    owner_ref, slot_ref = entry_ref.at[0:1], entry_ref.at[1:2]
    slot_copy_ref[...] = slot_ref[...]
    count = owner_ref.shape[1]
    owner_row = owner_ref[...].astype(F32)
    down, across = iota((count, count), 0), iota((count, count), 1)
    owner_col = jnp.sum(jnp.where(down == across, owner_row, 0.0), axis=1, keepdims=True)
    same = owner_col == owner_row
    rank_row = jnp.sum(jnp.where(same & (down < across), 1.0, 0.0), axis=0, keepdims=True)
    rank_col = jnp.sum(jnp.where(same & (across < down), 1.0, 0.0), axis=1, keepdims=True)
    pos_row = (owner_row * bucket + rank_row).astype(jnp.int32)
    pos_col = (owner_col * bucket + rank_col).astype(jnp.int32)
    mask = lax.axis_index("strip") * bucket if paired else 0
    pos_row, pos_col = pos_row ^ mask, pos_col ^ mask
    pos_row_ref[...] = pos_row
    pos_col_ref[...] = pos_col
    shift = rows.bit_length() - 1
    left = jnp.where(
        iota((groups, count), 0) == lax.shift_right_logical(pos_row, shift),
        slot_ref[...].astype(F32),
        0.0,
    )
    right = jnp.where(iota((count, LANES), 1) == (pos_col & (rows - 1)), 1.0, 0.0)
    wanted = jnp.dot(left, right, precision=HIGHEST, preferred_element_type=F32)
    for group in range(groups):
        if paired:
            refs[group % 2][group // 2 : group // 2 + 1] = wanted[group : group + 1]
        else:
            refs[0][group] = wanted[group : group + 1]


def ask_kernel(same_ref, other_ref, *out_refs):
    for m, out_ref in enumerate(out_refs):
        out_ref[0:1] = same_ref[m : m + 1]
        out_ref[1:2] = other_ref[m : m + 1]


def prepare_kernel(token_ref, table_ref, feature_ref, half_ref, parts_ref):
    owned, channels = feature_ref.shape
    blocks = owned // LANES
    high, low = split2(feature_ref[...])
    half_ref[:, :channels] = high
    half_ref[:, channels:] = low
    table = jnp.concatenate([table_ref[...], jnp.zeros((1, owned), F32)], axis=0)
    stacked = jnp.concatenate(
        [table[:, a * LANES : (a + 1) * LANES] for a in range(blocks)], axis=0
    )
    parts_ref[...] = jnp.concatenate(split3(stacked), axis=0)


def join_pair(same, other, out_ref):
    rows = same.shape[0] - 8
    out_ref[0:rows] = same[0:rows]
    out_ref[rows : 2 * rows] = other[0:rows]
    out_ref[2 * rows : 2 * rows + 8] = jnp.concatenate(
        [same[rows:][:, :rows], other[rows:][:, :rows]], axis=1
    )


def relay_kernel(same_ref, other_ref, *out_refs):
    lead = same_ref.shape[1]
    for m, out_ref in enumerate(out_refs):
        join_pair(same_ref[m], other_ref[m * lead : (m + 1) * lead], out_ref)


def weights_kernel(token_ref, weights_ref, straight_ref, turned_ref):
    size = weights_ref.shape[2]
    for i in range(3):
        for j in range(3):
            block = weights_ref[i, j]
            high, low = split2(block)
            straight_ref[i, j * size : (j + 1) * size, :size] = high
            straight_ref[i, j * size : (j + 1) * size, size:] = low
            high, low = split2(block.T)
            a, b = 2 - i, 2 - j
            turned_ref[a, b * size : (b + 1) * size, :size] = high
            turned_ref[a, b * size : (b + 1) * size, size:] = low


def reply_kernel(rows, paired, groups, half_ref, parts_ref, *refs):
    pick_ref = refs[-1]
    if paired:
        asked = jnp.concatenate([ref[0:2] for ref in refs[: groups // 2][::-1]], axis=0)
        refs = refs[groups // 2 :]
    else:
        asked = jnp.concatenate([refs[0][group] for group in range(groups)], axis=0)
        refs = refs[1:]
    replies = [refs[0].at[group] for group in range(refs[0].shape[0])]
    if paired:
        others = [refs[1].at[m * (rows + 8) : (m + 1) * (rows + 8)] for m in range(len(replies))]
        replies = [ref for pair in zip(replies, others) for ref in pair]
    owned = half_ref.shape[0]
    channels = half_ref.shape[1] // 2
    blocks = owned // LANES
    padded = jnp.concatenate([asked, jnp.zeros((LANES - groups, LANES), F32)], axis=0)
    columns = padded.T.astype(jnp.int32)
    place = iota((rows, owned), 1)
    for group in range(groups):
        pick_ref[group * rows : (group + 1) * rows] = onehot(
            columns[:rows, group : group + 1] == place
        )
    found = dot(pick_ref[...], half_ref[...])
    found = found[:, :channels] + found[:, channels:]
    slots = asked.astype(jnp.int32)
    slots_row = jnp.concatenate([slots[group : group + 1] for group in range(groups)], axis=1)
    wide = slots_row.shape[1]
    minor = onehot((slots_row & (LANES - 1)) == iota((LANES, wide), 0))
    product = dot(parts_ref[...], minor)
    deep = blocks * 8
    product = product[:deep] + product[deep : 2 * deep] + product[2 * deep :]
    major = lax.shift_right_logical(slots_row, 7)
    geometry = jnp.zeros((8, wide), F32)
    for a in range(blocks):
        geometry = geometry + jnp.where(major == a, product[a * 8 : (a + 1) * 8], 0.0)
    for group in range(groups):
        replies[group][0:rows] = found[group * rows : (group + 1) * rows]
        replies[group][rows : rows + 8] = geometry[:, group * LANES : (group + 1) * LANES]


def camera_at(small_ref, axis, i):
    return small_ref[0:1, 4 * axis + i : 4 * axis + i + 1]


def centers(small_ref, geometry):
    found = []
    for axis in range(2):
        found.append(
            8.0
            + 4.0
            * (
                camera_at(small_ref, axis, 0) * geometry[0:1]
                + camera_at(small_ref, axis, 1) * geometry[1:2]
                + camera_at(small_ref, axis, 2) * geometry[2:3]
                + camera_at(small_ref, axis, 3)
            )
        )
    return found


def offsets(small_ref, geometry, pixels):
    center_col, center_row = centers(small_ref, geometry)
    pixel = iota((pixels, geometry.shape[1]), 0)
    across = (pixel & (WIDTH - 1)).astype(F32) + 0.5
    downward = lax.shift_right_logical(pixel, WIDTH.bit_length() - 1).astype(F32) + 0.5
    return across - center_col, downward - center_row


def render_kernel(
    rows,
    groups,
    paired,
    length_ref,
    small_ref,
    pos_row_ref,
    pos_col_ref,
    target_ref,
    *refs,
):
    received = refs[:-7][::-1]
    tile_ref, send_near_ref, send_far_ref, weight_ref, ratio_ref, geometry_ref, feature_ref = refs[-7:]
    count = pos_row_ref.shape[1]
    places = groups * rows
    pixels, channels = tile_ref.shape
    pick = onehot(pos_col_ref[...] == iota((count, places), 1))
    pick_t = onehot(pos_row_ref[...] == iota((places, count), 0))
    if paired:
        sent = jnp.concatenate([ref[0 : 2 * rows] for ref in received], axis=0)
        lines = jnp.concatenate([ref[2 * rows :] for ref in received], axis=1)
    else:
        sent = jnp.concatenate([received[0][group, 0:rows] for group in range(groups)], axis=0)
        lines = jnp.concatenate(
            [received[0][group, rows:][:, :rows] for group in range(groups)], axis=1
        )
    feature = dot(pick, jnp.concatenate(split2(sent), axis=1)).astype(BF16)
    feature_ref[...] = feature
    geometry = dot(jnp.concatenate(split3(lines), axis=0), pick_t)
    geometry = geometry[0:8] + geometry[8:16] + geometry[16:24]
    geometry_ref[...] = geometry
    du, dv = offsets(small_ref, geometry, pixels)
    a = geometry[3:4] * du
    b = geometry[4:5] * dv
    exponent = -0.5 * (a * a + 2.0 * geometry[5:6] * a * b + b * b)
    alive = iota((1, count), 1) < length_ref[0, 0]
    sigmoid = 1.0 / (1.0 + jnp.exp(-geometry[6:7]))
    raw = sigmoid * jnp.exp(exponent)
    alpha = jnp.where(alive, jnp.minimum(raw, 0.99), 0.0)
    keep = 1.0 - alpha
    log_keep = jnp.log(keep)
    before = onehot(iota((count, count), 0) < iota((count, count), 1))
    high, low = split2(log_keep)
    weight = alpha * jnp.exp(dot(high, before) + dot(low, before))
    weight_ref[...] = weight
    ratio_ref[...] = jnp.where(raw < 0.99, alpha, 0.0) / keep
    high, low = split2(weight)
    tile = dot(high, feature)
    tile = tile[:, :channels] + tile[:, channels:] + dot(low, feature[:, :channels])
    tile_ref[...] = tile
    top = jnp.concatenate([tile[0 : 2 * WIDTH], target_ref[0:WIDTH]], axis=0)
    bottom = jnp.concatenate([tile[pixels - 2 * WIDTH :], target_ref[pixels - WIDTH : pixels]], axis=0)
    even = lax.axis_index("strip") % 2 == 0
    send_near_ref[...] = jnp.where(even, bottom, top)
    send_far_ref[...] = jnp.where(even, top, bottom)


def spread_kernel(
    pos_row_ref,
    weight_ref,
    tile_ref,
    target_ref,
    straight_ref,
    small_ref,
    spread_ref,
    partial_ref,
    high_ref,
    low_ref,
    scratch_ref,
):
    places = spread_ref.shape[0]
    pixels, count = weight_ref.shape
    channels = tile_ref.shape[1]
    pick_t = onehot(pos_row_ref[...] == iota((places, count), 0))
    high, low = split2(weight_ref[...])
    spread_ref[:, :pixels] = dot_nt(pick_t, high).astype(BF16)
    spread_ref[:, pixels:] = dot_nt(pick_t, low).astype(BF16)
    wide = shifted(tile_ref[...], scratch_ref)
    high, low = split2(wide)
    high_ref[...] = high
    low_ref[...] = low
    empty = jnp.zeros((2 * WIDTH, 3 * channels), F32)
    wide = jnp.concatenate([empty, wide, empty], axis=0)
    edge = jnp.zeros((WIDTH, channels), F32)
    goal = jnp.concatenate([edge, target_ref[...], edge], axis=0)
    partial = taps(wide, straight_ref, pixels + 2 * WIDTH, channels)
    partial_ref[...] = partial + small_ref[1:2] - goal


def shifted(value, scratch_ref):
    count = value.shape[0]
    scratch_ref[8 : 8 + count] = value
    column = iota((count, 1), 0) & (WIDTH - 1)
    left = jnp.where(column == 0, 0.0, scratch_ref[7 : 7 + count])
    right = jnp.where(column == WIDTH - 1, 0.0, scratch_ref[9 : 9 + count])
    return jnp.concatenate([left, value, right], axis=1)


def taps(wide, kernel_ref, count, channels):
    high, low = split2(wide)
    total = jnp.zeros((count, channels), F32)
    for i in range(3):
        part = dot(high[WIDTH * i : WIDTH * i + count], kernel_ref[i])
        total = total + part[:, :channels] + part[:, channels:]
        total = total + dot(low[WIDTH * i : WIDTH * i + count], kernel_ref[i][:, :channels])
    return total


def decode(partial_ref, high_ref, low_ref, far_ref, near_ref, kernel_ref, scratch_ref, sum_ref):
    count, channels = partial_ref.shape
    pixels = count - 2 * WIDTH
    edge = 2 * WIDTH
    strip = lax.axis_index("strip")
    even = strip % 2 == 0
    near, far = near_ref[...], far_ref[...]
    above, below = jnp.where(even, far, near), jnp.where(even, near, far)
    gap = jnp.zeros((edge, channels), F32)
    beside = shifted(jnp.concatenate([above[0:edge], gap, below[0:edge]], axis=0), scratch_ref)
    more = taps(beside, kernel_ref, 2 * edge, channels)
    partial = partial_ref[...]
    residual = jnp.concatenate(
        [
            partial[0:WIDTH] + more[0:WIDTH] - above[edge:],
            partial[WIDTH:edge] + more[WIDTH:edge],
            partial[edge : count - edge],
            partial[count - edge : count - WIDTH] + more[edge : edge + WIDTH],
            partial[count - WIDTH :] + more[edge + WIDTH :] - below[edge:],
        ],
        axis=0,
    )
    pixel = iota((count, 1), 0)
    outside = ((pixel < WIDTH) & (strip == 0)) | (
        (pixel >= count - WIDTH) & (strip == lax.axis_size("strip") - 1)
    )
    residual = jnp.where(outside, 0.0, residual)

    own = residual[WIDTH : WIDTH + pixels]
    turned_high, turned_low = split2(own.T)
    beside_high, beside_low = split2(beside)
    high, low = (
        jnp.concatenate([ends[WIDTH:edge], mine[...], ends[2 * edge : 2 * edge + WIDTH]], axis=0)
        for ends, mine in ((beside_high, high_ref), (beside_low, low_ref))
    )
    for i in range(3):
        first = WIDTH * i
        part = (
            dot(turned_high, high[first : first + pixels])
            + dot(turned_high, low[first : first + pixels])
            + dot(turned_low, high[first : first + pixels])
        )
        for j in range(3):
            block = (3 * i + j) * channels
            sum_ref[block : block + channels] = part[:, j * channels : (j + 1) * channels].T
    return residual, jnp.sum(own, axis=0, keepdims=True)


def back_kernel(
    rows,
    groups,
    paired,
    small_ref,
    partial_ref,
    high_ref,
    low_ref,
    far_ref,
    near_ref,
    straight_ref,
    turned_ref,
    weight_ref,
    ratio_ref,
    geometry_ref,
    feature_ref,
    spread_ref,
    pos_col_ref,
    slot_ref,
    same_ref,
    cross_ref,
    keep_ref,
    own_bias_ref,
    scratch_ref,
    sum_ref,
):
    pixels, count = weight_ref.shape
    channels = partial_ref.shape[1]
    places = groups * rows
    lead = rows + 8
    half = keep_ref.shape[0]
    residual, bias_grad = decode(
        partial_ref, high_ref, low_ref, far_ref, near_ref, straight_ref, scratch_ref, sum_ref
    )
    start = cross_ref.shape[0] - half - 8
    bias_rows = jnp.where(iota((8, channels), 0) == 0, bias_grad, 0.0)
    own_bias_ref[...] = bias_rows
    cross_ref[start + half :] = bias_rows
    even = lax.axis_index("strip") % 2 == 0
    keep_ref[...] = jnp.where(even, sum_ref[0:half], sum_ref[half:])
    cross_ref[start : start + half] = jnp.where(even, sum_ref[half:], sum_ref[0:half])

    def put(group, first, value):
        amount = value.shape[0]
        if not paired:
            same_ref[group, first : first + amount] = value
        elif group % 2 == 0:
            same_ref[group // 2, first : first + amount] = value
        else:
            first = group // 2 * lead + first
            cross_ref[first : first + amount] = value

    extent = residual.shape[0]
    scratch_ref[8 + extent : 16 + extent] = jnp.zeros((8, channels), F32)
    wide = shifted(residual, scratch_ref)
    grad = taps(wide, turned_ref, pixels, channels)
    high, low = split2(grad)
    both = jnp.concatenate([high, low], axis=1)
    part = dot(spread_ref[:, :pixels], both)
    part = part[:, :channels] + part[:, channels:] + dot(spread_ref[:, pixels:], high)
    for group in range(groups):
        put(group, 0, part[group * rows : (group + 1) * rows])

    near, far = feature_ref[:, :channels], feature_ref[:, channels:]
    weight_grad = dot_nt(high, near) + dot_nt(high, far) + dot_nt(low, near)
    pull = weight_grad * weight_ref[...]
    behind = onehot(iota((count, count), 0) > iota((count, count), 1))
    high, low = split2(pull)
    suffix = dot(high, behind) + dot(low, behind)
    ratio = ratio_ref[...]
    change = jnp.where(ratio > 0.0, pull - ratio * suffix, 0.0)

    geometry = geometry_ref[...]
    du, dv = offsets(small_ref, geometry, pixels)

    def total(x):
        return jnp.sum(x, axis=0, keepdims=True)

    change_u, change_v = change * du, change * dv
    m, mu, mv = total(change), total(change_u), total(change_v)
    muu, muv, mvv = total(change_u * du), total(change_u * dv), total(change_v * dv)
    g3, g4, g5, g6 = (geometry[i : i + 1] for i in range(3, 7))
    center_col = g3 * (g3 * mu + g5 * g4 * mv)
    center_row = g4 * (g5 * g3 * mu + g4 * mv)
    lines = [
        4.0 * (camera_at(small_ref, 0, i) * center_col + camera_at(small_ref, 1, i) * center_row)
        for i in range(3)
    ]
    lines.append(-(g3 * muu + g5 * g4 * muv))
    lines.append(-(g4 * mvv + g5 * g3 * muv))
    lines.append(-(g3 * g4 * muv))
    lines.append(m / (1.0 + jnp.exp(g6)))
    lines.append(slot_ref[...].astype(F32))
    pick = onehot(pos_col_ref[...] == iota((count, places), 1))
    moved = dot(jnp.concatenate(split3(jnp.concatenate(lines, axis=0)), axis=0), pick)
    moved = moved[0:8] + moved[8:16] + moved[16:24]
    for group in range(groups):
        piece = moved[:, group * rows : (group + 1) * rows]
        if rows < LANES:
            piece = jnp.concatenate([piece, jnp.zeros((8, LANES - rows), F32)], axis=1)
        put(group, rows, piece)


def pack_kernel(places, amount, paired, *refs):
    inputs = [refs[place] for place in places]
    values, parts = inputs[:amount], inputs[amount:]
    packed_ref, sum_ref = refs[-2:]
    rows = values[0].shape[0] - (8 if paired else 0)
    for place, value in enumerate(values):
        packed_ref[place * rows : (place + 1) * rows] = value[0:rows]
    if paired:
        bias_rows = values[0][rows:]
        for value in values[1:]:
            bias_rows = bias_rows + value[rows:]
        packed_ref[amount * rows :] = bias_rows
    sum_kernel(*parts, sum_ref)


def gather_rows(slot_row, half_ref, start, count):
    channels = half_ref.shape[1] // 2
    pick_t = onehot(slot_row == iota((count, half_ref.shape[0]), 0) + start)
    part = dot(pick_t, half_ref[...])
    return part[:, :channels] + part[:, channels:]


def gather_first_kernel(rows, groups, views, paired, token_ref, *refs):
    arrived = refs[:views]
    feature_ref, half_ref, lines_ref, bias_ref, geometry_ref = refs[views:]
    blocks = geometry_ref.shape[1] // LANES
    channels = feature_ref.shape[1]
    step = 2 * rows if paired else rows
    pieces = groups * rows // step
    amount = views * groups * rows
    lines = []
    for view in range(views):
        for group in range(pieces):
            first = group * (step + 8)
            piece = view * pieces + group
            high, low = split2(arrived[view][first : first + step])
            half_ref[piece * step : (piece + 1) * step, :channels] = high
            half_ref[piece * step : (piece + 1) * step, channels:] = low
            lines.append(arrived[view][first + step : first + step + 8][:, :step])
    lines = jnp.concatenate(lines, axis=1)
    lines_ref[...] = lines
    if paired:
        last = arrived[0].shape[0] - 8
        bias = arrived[0][last : last + 1]
        for value in arrived[1:]:
            bias = bias + value[last : last + 1]
        bias_ref[...] = bias
    else:
        bias_ref[...] = jnp.zeros(bias_ref.shape, F32)
    slot_row = lines[7:8].astype(jnp.int32)
    minor = onehot((slot_row & (LANES - 1)) == iota((LANES, amount), 0))
    major = lax.shift_right_logical(slot_row, 7)
    stacked = jnp.concatenate([jnp.where(major == a, lines, 0.0) for a in range(blocks)], axis=0)
    high, low = split2(stacked)
    product = dot_nt(high, minor) + dot_nt(low, minor)
    for a in range(blocks):
        geometry_ref[:, a * LANES : (a + 1) * LANES] = product[a * 8 : a * 8 + 7]
    tile = 256
    for start in range(0, feature_ref.shape[0], tile):
        feature_ref[start : start + tile] = gather_rows(slot_row, half_ref, start, tile)


def gather_second_kernel(
    token_ref,
    half_ref,
    lines_ref,
    begun_ref,
    bias_in_ref,
    geometry_ref,
    feature_hbm,
    geometry_hbm,
    bias_hbm,
    end_ref,
    out_ref,
    sems,
):
    owned = feature_hbm.shape[0]
    begun = begun_ref.shape[0]
    lines = lines_ref[...]
    copies = [
        pltpu.make_async_copy(geometry_ref, geometry_hbm, sems.at[2]),
        pltpu.make_async_copy(begun_ref, feature_hbm.at[0:begun], sems.at[0]),
        pltpu.make_async_copy(bias_in_ref, bias_hbm, sems.at[1]),
    ]
    for copy in copies:
        copy.start()
    slot_row = lines[7:8].astype(jnp.int32)
    tile = out_ref.shape[1]
    for step, start in enumerate(range(begun, owned, tile)):
        out_ref[step] = gather_rows(slot_row, half_ref, start, tile)
        copies.append(
            pltpu.make_async_copy(
                out_ref.at[step], feature_hbm.at[start : start + tile], sems.at[3 + step]
            )
        )
        copies[-1].start()
    end_ref[...] = jnp.zeros(end_ref.shape, F32)
    for copy in copies:
        copy.wait()


def mix_kernel(pieces, same_ref, keep_ref, own_bias_ref, other_ref, *out_refs):
    parts = len(out_refs) - pieces
    rows = keep_ref.shape[0] // parts
    start = other_ref.shape[0] - keep_ref.shape[0] - 8
    bias_rows = own_bias_ref[...] + other_ref[start + keep_ref.shape[0] :]
    for m in range(pieces):
        lead = same_ref.shape[1]
        join_pair(same_ref[m], other_ref[m * lead : (m + 1) * lead], out_refs[m])
        out_refs[m][2 * lead - 8 :] = bias_rows
    view = lax.axis_index("view")
    for m in range(parts):
        first = pl.multiple_of((view ^ m) * rows, 8)
        second = pl.multiple_of(start + (view ^ m) * rows, 8)
        out_refs[pieces + m][...] = keep_ref[pl.ds(first, rows)] + other_ref[pl.ds(second, rows)]


def sum_kernel(*refs):
    total = refs[0][...]
    for ref in refs[1:-1]:
        total = total + ref[...]
    refs[-1][...] = total


def join_kernel(token_ref, *refs):
    parts = len(refs) - 1
    rows = refs[0].shape[0]
    view = lax.axis_index("view")
    for m in range(parts):
        start = pl.multiple_of((view ^ m) * rows, 8)
        refs[-1][pl.ds(start, rows)] = refs[m][...]


def finish_kernel(token_ref, mine_ref, other_ref, kernel_hbm, sems):
    half = mine_ref.shape[0]

    def move(first, second):
        copies = [
            pltpu.make_async_copy(first, kernel_hbm.at[0:half], sems.at[0]),
            pltpu.make_async_copy(second, kernel_hbm.at[half:], sems.at[1]),
        ]
        for copy in copies:
            copy.start()
        for copy in copies:
            copy.wait()

    even = lax.axis_index("strip") % 2 == 0

    @pl.when(even)
    def _():
        move(mine_ref, other_ref)

    @pl.when(jnp.logical_not(even))
    def _():
        move(other_ref, mine_ref)


def swap(value, axis, mask):
    count = lax.axis_size(axis)
    return lax.ppermute(value, axis, [(i, i ^ mask) for i in range(count)])


def near_sum(value, axis, unit, amount):
    step = unit
    while amount > 1:
        near = 4 if amount % 4 == 0 else 2
        parts = [value] + [swap(value, axis, step * m) for m in ((3, 2, 1) if near == 4 else (1,))]
        value = call(sum_kernel, jax.ShapeDtypeStruct(value.shape, F32), [VMEM] * near)(*parts)
        step, amount = step * near, amount // near
    return value


def per_device(
    means,
    inv_scales,
    correlation,
    opacity,
    features,
    cameras,
    owners,
    slots,
    lengths,
    target,
    weights,
    bias,
):
    shape = jax.ShapeDtypeStruct
    strips = lax.axis_size("strip")
    views = lax.axis_size("view")
    count = slots.shape[1] * slots.shape[2]
    owned, channels = features.shape
    height, breadth = target.shape[1], target.shape[2]
    pixels = height * breadth
    assert slots.shape[1] == 1 and breadth == WIDTH and channels == LANES
    bucket = max(4, 2 * count // strips)
    places = strips * bucket
    rows = bucket if bucket % 8 == 0 else 64
    groups = places // rows
    direct = rows == bucket
    paired = direct and strips <= 8 and 2 * rows == LANES
    lead = rows + 8
    wire_lead = bucket + 8

    def to_wire(value):
        if direct:
            return value
        top = value[:, :rows].reshape(strips, bucket, LANES)
        low = value[:, rows:, :rows].transpose(1, 0, 2).reshape(8, strips, bucket)
        low = jnp.pad(low.transpose(1, 0, 2), ((0, 0), (0, 0), (0, LANES - bucket)))
        return jnp.concatenate([top, low], axis=1)

    def from_wire(value):
        if direct:
            return value
        top = value[:, :bucket].reshape(groups, rows, LANES)
        low = value[:, bucket:, :bucket].transpose(1, 0, 2).reshape(8, groups, rows)
        low = jnp.pad(low.transpose(1, 0, 2), ((0, 0), (0, 0), (0, LANES - rows)))
        return jnp.concatenate([top, low], axis=1)

    def exchange(value):
        return lax.all_to_all(value, "strip", split_axis=0, concat_axis=0, tiled=True)

    goal = target.reshape(pixels, channels)

    pieces = strips // 2 if paired else 0
    asks = shape((max(8, pieces), LANES), F32)
    pos_row, pos_col, slot_row, *request = call(
        functools.partial(route_kernel, bucket, rows, paired, groups),
        [
            shape((1, count), jnp.int32),
            shape((count, 1), jnp.int32),
            shape((1, count), jnp.int32),
        ]
        + ([asks] * 2 if paired else [shape((groups, 1, LANES), F32)]),
        [VMEM],
    )(jnp.concatenate([owners.reshape(1, count), slots.reshape(1, count)], axis=0))
    if paired:
        chips = call(ask_kernel, [shape((8, LANES), F32)] * pieces, [VMEM] * 2)(
            request[0], swap(request[1], "strip", 1)
        )
        asked = [swap(chips[m], "strip", 2 * m) for m in range(pieces - 1, 0, -1)] + [chips[0]]
    elif direct:
        asked = [exchange(request[0])]
    else:
        request = request[0][:, 0, :rows].reshape(strips, 1, bucket)
        asked = exchange(jnp.pad(request, ((0, 0), (0, 0), (0, LANES - bucket))))
        asked = asked[:, 0, :bucket].reshape(groups, 1, rows)
        asked = [jnp.pad(asked, ((0, 0), (0, 0), (0, LANES - rows)))]

    table = jnp.concatenate(
        [
            means,
            inv_scales,
            correlation[None, :],
            opacity[None, :],
        ],
        axis=0,
    )
    small = jnp.concatenate(
        [jnp.pad(cameras.reshape(1, 8), ((0, 0), (0, LANES - 8))), bias[None, :]], axis=0
    )
    half, parts = call(
        prepare_kernel,
        [
            shape((owned, 2 * channels), BF16),
            shape((3 * 8 * (owned // LANES), LANES), BF16),
        ],
        [ANY, VMEM, VMEM],
        flops=2**33,
        moved=2**24,
    )(pos_row, table, features)
    replies = call(
        functools.partial(reply_kernel, rows, paired, groups),
        [shape((pieces, lead, LANES), F32), shape((pieces * lead, LANES), F32)]
        if paired
        else [shape((groups, lead, LANES), F32)],
        [VMEM] * (2 + len(asked)),
        [pltpu.VMEM((places, owned), BF16)],
    )(half, parts, *asked)
    straight, turned = call(
        weights_kernel,
        [shape((3, 3 * channels, 2 * channels), BF16)] * 2,
        [ANY, VMEM],
        flops=2**32,
        moved=2**23,
    )(replies[0], weights)
    if paired:
        same, cross = replies
        chips = call(
            relay_kernel, [shape((2 * lead - 8, LANES), F32)] * pieces, [VMEM] * 2
        )(same, swap(cross, "strip", 1))
        far = {m: swap(chips[m], "strip", 2 * m) for m in range(pieces - 1, 0, -1)}
        fetched = [far[m] for m in range(pieces - 1, 0, -1)] + [chips[0]]
    else:
        fetched = [from_wire(exchange(to_wire(replies[0])))]

    tile, send_near, send_far, weight, ratio, geometry, feature = call(
        functools.partial(render_kernel, rows, groups, paired),
        [
            shape((pixels, channels), F32),
            shape((3 * WIDTH, channels), F32),
            shape((3 * WIDTH, channels), F32),
            shape((pixels, count), F32),
            shape((pixels, count), F32),
            shape((8, count), F32),
            shape((count, 2 * channels), BF16),
        ],
        [SMEM] + [VMEM] * (4 + len(fetched)),
    )(lengths, small, pos_row, pos_col, goal, *fetched)
    between = [(i, i + 1) for i in range(1, strips - 1, 2)]
    far = lax.ppermute(send_far, "strip", between + [(b, a) for a, b in between])
    near = swap(send_near, "strip", 1)
    spread, partial, wide_high, wide_low = call(
        spread_kernel,
        [
            shape((places, 2 * pixels), BF16),
            shape((pixels + 2 * WIDTH, channels), F32),
            shape((pixels, 3 * channels), BF16),
            shape((pixels, 3 * channels), BF16),
        ],
        [VMEM] * 6,
        [pltpu.VMEM((pixels + 16, channels), F32)],
        moved=2**21,
    )(pos_row, weight, tile, goal, straight, small)

    half = 9 * channels // 2
    assert half % (8 * views) == 0
    same, cross, keep, own_bias = call(
        functools.partial(back_kernel, rows, groups, paired),
        [
            shape((pieces if paired else groups, lead, LANES), F32),
            shape((pieces * lead + half + 8, LANES), F32),
            shape((half, channels), F32),
            shape((8, channels), F32),
        ],
        [VMEM] * 15,
        [
            pltpu.VMEM((pixels + 4 * WIDTH + 16, channels), F32),
            pltpu.VMEM((9 * channels, channels), F32),
        ],
        flops=2**30,
        moved=2**22,
    )(
        small,
        partial,
        wide_high,
        wide_low,
        far,
        near,
        straight,
        turned,
        weight,
        ratio,
        geometry,
        feature,
        spread,
        pos_col,
        slot_row,
    )
    other = swap(cross, "strip", 1)
    part = shape((half // views, channels), F32)
    mixed = call(
        functools.partial(mix_kernel, pieces),
        [shape((2 * lead, LANES), F32)] * pieces + [part] * views,
        [VMEM] * 4,
    )(same, keep, own_bias, other)
    if paired:
        order = range(pieces - 1, 0, -1)
        moved = {m: swap(mixed[m], "strip", 2 * m) for m in order}
        returned = [moved[m] for m in order] + [mixed[0]]
    else:
        returned = [from_wire(exchange(to_wire(same))).reshape(groups * lead, LANES)]
    parts = [mixed[pieces]] + [swap(mixed[pieces + m], "view", m) for m in range(1, views)]
    length = pieces * (2 * lead - 8) + 8 if paired else groups * lead
    inputs = returned + parts
    issue = list(range(len(inputs)))
    if paired and pieces == 4 and views == 4:
        issue = [2, 0, 1, 7, 5, 6, 3, 4]
    packed, total = call(
        functools.partial(pack_kernel, [issue.index(i) for i in range(len(issue))], len(returned), paired),
        [shape((length, LANES), F32), part],
        [VMEM] * len(inputs),
    )(*[inputs[i] for i in issue])
    far = {m: swap(packed, "view", m) for m in range(views - 1, 0, -1)}
    arrived = [packed] + [far[m] for m in range(1, views)]

    total = near_sum(total, "strip", 2, strips // 2)
    parts = [total] + [swap(total, "view", m) for m in range(1, views)]
    first = owned * 7 // 8
    feature_first, rowed, lines, bias_sum, geometry_sum = call(
        functools.partial(gather_first_kernel, rows, groups, views, paired),
        [
            shape((first, channels), F32),
            shape((views * places, 2 * channels), BF16),
            shape((8, views * places), F32),
            shape((1, channels), F32),
            shape((7, owned), F32),
        ],
        [ANY] + [VMEM] * views,
        flops=2**31,
        moved=2**22,
    )(total, *arrived)
    if not paired:
        bias_sum = lax.psum(own_bias[0:1], ("view", "strip"))
    joined = call(join_kernel, shape((half, channels), F32), [ANY] + [VMEM] * views)(lines, *parts)
    other = swap(joined, "strip", 1)
    tile = 256
    feature_grad, geometry_grad, bias_grad, end = call(
        gather_second_kernel,
        [
            shape((owned, channels), F32),
            shape((7, owned), F32),
            shape((1, channels), F32),
            shape((8, LANES), F32),
        ],
        [ANY] + [VMEM] * 5,
        [
            pltpu.VMEM(((owned - first) // tile, tile, channels), F32),
            pltpu.SemaphoreType.DMA((3 + (owned - first) // tile,)),
        ],
        out=[HBM, HBM, HBM, VMEM],
        flops=2**31,
        moved=2**22,
    )(joined, rowed, lines, feature_first, bias_sum, geometry_sum)
    kernel_grad = call(
        finish_kernel,
        shape((9 * channels, channels), F32),
        [ANY, ANY, ANY],
        [pltpu.SemaphoreType.DMA((2,))],
        out=HBM,
    )(end, joined, other)
    return (
        geometry_grad,
        feature_grad,
        kernel_grad.reshape(weights.shape),
        bias_grad.reshape(bias.shape),
    )


def solution(mesh):
    return jax.shard_map(
        per_device,
        mesh=mesh,
        in_specs=(
            P(None, "strip"),
            P(None, "strip"),
            P("strip"),
            P("strip"),
            P("strip", None),
            P("view", None, None),
            P("view", "strip", None, None),
            P("view", "strip", None),
            P("view", "strip"),
            P("view", "strip", None, None),
            P(),
            P(),
        ),
        out_specs=(P(None, "strip"), P("strip", None), P(), P()),
        check_vma=False,
    )
```
